32 devices in a mesh: ctx: 16 (over z, y, x), mix: 2 (over core).
Axes of the slice: x: 2, y: 2, z: 4, core: 2. Of those that a mesh axis runs over, the one named last changes fastest.
Arguments:
- sources: float32 [8, 131072], P('mix', 'ctx'), may hold values from -6 to 6
- source_ids: int32 [4, 3], replicated, may hold values from 0 to 7
- mix_weights: float32 [4, 3], replicated, may hold values from 0.1 to 0.8, as said below
- source_lengths: int32 [4, 3], replicated, may hold values from 512 to 4096, as said below
- w_embed: bfloat16 [512, 32], replicated, may hold values from -1 to 1
- w_qkv: bfloat16 [512, 1536], replicated, may hold values from -0.25 to 0.25
- w_out: bfloat16 [512, 512], replicated, may hold values from -0.25 to 0.25
- forget: float32 [4, 4, 4096], P('mix', None, 'ctx'), may hold values from 0.5 to 1, as said below
- cotangent: bfloat16 [4, 4096, 512], P('mix', 'ctx'), may hold values from -0.125 to 0.125
Outputs:
- output: bfloat16 [4, 4096, 512], P('mix', 'ctx')
- grad_qkv: float32 [512, 1536], P('ctx')
- grad_out: float32 [512, 512], P('ctx')
- grad_embed: float32 [512, 32], P('ctx')
The draws below stay inside these ranges and needn't reach their ends.
Inputs may be any that keep to these rules, and one draw needn't show every extreme that they name: `mix_weights`: each row sums to one. `source_lengths`: in every row one entry equals 4096. `forget`: below one.
All inputs are finite; a program needn't handle non-finite values.
Results may differ from the reference program's by a relative error of at most 0.015.
Values sent between devices are 32-bit elements; how exact they have to be, the bound alone decides.
No kernel may reach another device: no remote copies, remote signals or barrier semaphores. Data moves between devices by JAX's collectives and lax.ppermute only.
A program may use at most 128 MiB of HBM per device.

```python
import math
import jax
import jax.numpy as jnp
from jax import lax

D = 512
H = 4
PATCH = 32
SPAN = 256
TERMS = 3
HEAD = 128
LENGTH = 4096
MIXTURES = 4
NSRC = 8
ROWS = 16384


def draw_mix_weights(key, part):
    draws = jax.random.uniform(jax.random.fold_in(key, 31), (MIXTURES, TERMS), minval=1e-06, maxval=1.0)
    spread = -jnp.log(draws)
    return (0.1 + 0.7 * spread / jnp.sum(spread, axis=1, keepdims=True)).astype(jnp.float32)


def draw_source_lengths(key, part):
    first_key, second_key = jax.random.split(jax.random.fold_in(key, 47))
    others = jax.random.randint(first_key, (MIXTURES, TERMS), LENGTH // 8, LENGTH + 1)
    whole = jax.random.randint(second_key, (MIXTURES,), 0, TERMS)
    slots = jnp.arange(TERMS, dtype=jnp.int32)
    return jnp.where(slots[None, :] == whole[:, None], LENGTH, others).astype(jnp.int32)


def draw_forget(key, part):
    kind_key, slow_key, fast_key, jitter_key, where_key, depth_key = jax.random.split(jax.random.fold_in(key, 59), 6)
    fast_share = 0.5
    slow_lo = 0.05
    slow_hi = 0.6
    fast = jax.random.uniform(kind_key, (MIXTURES, H, 1)) < fast_share
    slow_rate = jnp.exp(jax.random.uniform(slow_key, (MIXTURES, H, 1), minval=math.log(slow_lo / LENGTH), maxval=math.log(slow_hi / LENGTH)))
    fast_rate = jnp.exp(jax.random.uniform(fast_key, (MIXTURES, H, 1), minval=math.log(1.0 / 50.0), maxval=math.log(1.0 / 30.0)))
    rate = jnp.where(fast, fast_rate, slow_rate)
    jitter = jax.random.uniform(jitter_key, (MIXTURES, H, LENGTH), minval=0.5, maxval=1.5)
    gate_signal = jnp.minimum(1.0 - rate * jitter, 1.0 - 1.2e-07)
    spots = jax.random.randint(where_key, (MIXTURES, H, 3), 0, LENGTH)
    recursion_level = jax.random.uniform(depth_key, (MIXTURES, H, 3), minval=0.5, maxval=0.8)
    positions = jnp.arange(LENGTH, dtype=jnp.int32)
    match_flag = positions[None, None, :, None] == spots[:, :, None, :]
    spike_event = jnp.min(jnp.where(match_flag, recursion_level[:, :, None, :], 1.0), axis=-1)
    return jnp.minimum(gate_signal, spike_event).astype(jnp.float32)


def place_ends(result, own_key, smallest, top_value):
    spot = [jax.random.randint(jax.random.fold_in(own_key, axis), (), 0, length) for axis, length in enumerate(result.shape)]
    widest = result.shape.index(max(result.shape))
    neighbour = spot[:widest] + [(spot[widest] + 1) % result.shape[widest]] + spot[widest + 1:]
    return result.at[tuple(spot)].set(smallest).at[tuple(neighbour)].set(top_value)


def steps_of(stream_key, dims, cuts, least, high):
    def one(axis_at, blocks):
        heights = jax.random.uniform(jax.random.fold_in(jax.random.fold_in(stream_key, 6), axis_at), (blocks,), jnp.float32, least / len(cuts), high / len(cuts))
        return jnp.repeat(jnp.exp(heights), dims[axis_at] // blocks).reshape((-1,) + (1,) * (len(dims) - axis_at - 1))

    gain = one(*cuts[0])
    for cut in cuts[1:]:
        gain = gain * one(*cut)
    return gain


def centred(own_key, dims, scale, limit, shards=(), kind=jnp.bfloat16):
    values = jax.random.normal(own_key, dims, jnp.float32) * scale
    if len(shards) > 0:
        values = steps_of(own_key, dims, shards, -0.22, 0.18) * values
    return jnp.clip(values, min=-limit, max=limit).astype(kind)


def setup_inputs(seed: int = 0) -> dict:
    arg_keys = jax.random.split(jax.random.key(seed), 10)
    return {
        "sources": centred(arg_keys[0], (NSRC, LENGTH * PATCH), 1.0, 6.0, ((0, 2), (1, 16)), jnp.float32),
        "source_ids": place_ends(jax.random.randint(arg_keys[1], (MIXTURES, TERMS), 0, NSRC), jax.random.fold_in(arg_keys[1], 1), 0, NSRC - 1).astype(jnp.int32),
        "mix_weights": draw_mix_weights(jax.random.fold_in(arg_keys[9], 71), 0),
        "source_lengths": draw_source_lengths(jax.random.fold_in(arg_keys[9], 71), 0),
        "w_embed": centred(arg_keys[4], (D, PATCH), PATCH ** -0.5, 1.0),
        "w_qkv": centred(arg_keys[5], (D, 3 * D), D ** -0.5, 0.25),
        "w_out": centred(arg_keys[6], (D, D), D ** -0.5, 0.25),
        "forget": draw_forget(jax.random.fold_in(arg_keys[9], 71), 0),
        "cotangent": centred(arg_keys[8], (MIXTURES, LENGTH, D), (ROWS ** -0.5), 0.125, ((0, 2), (1, 16))),
    }


EPS = 1e-06

def product(spec, left, right):
    return jnp.einsum(spec, left.astype(jnp.float32), right.astype(jnp.float32))

def scaled(array, factor):
    return (array.astype(jnp.float32) * factor[..., None]).astype(jnp.bfloat16)

def causal_decay(cumulative):
    length = cumulative.shape[-1]
    causal = jnp.arange(length)[:, None] >= jnp.arange(length)[None, :]
    return jnp.where(causal, jnp.exp(cumulative[..., :, None] - cumulative[..., None, :]), 0.0)

def block_forward(queries, key_rows, value_rows, log_gate, memory):
    cumulative = jnp.cumsum(log_gate, axis=-1)
    final = cumulative[..., -1:]
    decay_mask = causal_decay(cumulative)
    from_memory = product('bhcd,bhde->bhce', scaled(queries, jnp.exp(cumulative)), memory.astype(jnp.bfloat16))
    weights = (product('bhcd,bhsd->bhcs', queries, key_rows) * decay_mask).astype(jnp.bfloat16)
    inside = product('bhcs,bhse->bhce', weights, value_rows)
    written = product('bhcd,bhce->bhde', scaled(key_rows, jnp.exp(final - cumulative)), value_rows)
    updated = jnp.exp(final)[..., None] * memory + written
    return (from_memory + inside, updated)

def block_backward(queries, key_rows, value_rows, grad_read, log_gate, memory, later):
    cumulative = jnp.cumsum(log_gate, axis=-1)
    final = cumulative[..., -1:]
    decay_mask = causal_decay(cumulative)
    growth = jnp.exp(cumulative)
    decay_factor = jnp.exp(final - cumulative)
    left = (product('bhce,bhse->bhcs', grad_read, value_rows) * decay_mask).astype(jnp.bfloat16)
    right = (product('bhcd,bhsd->bhcs', queries, key_rows) * decay_mask).astype(jnp.bfloat16)
    later_half = later.astype(jnp.bfloat16)
    grad_query = product('bhce,bhde->bhcd', scaled(grad_read, growth), memory.astype(jnp.bfloat16)) + product('bhcs,bhsd->bhcd', left, key_rows)
    grad_key = product('bhcs,bhcd->bhsd', left, queries) + product('bhse,bhde->bhsd', scaled(value_rows, decay_factor), later_half)
    grad_value = product('bhcs,bhce->bhse', right, grad_read) + product('bhsd,bhde->bhse', scaled(key_rows, decay_factor), later_half)
    earlier = jnp.exp(final)[..., None] * later + product('bhcd,bhce->bhde', scaled(queries, growth), grad_read)
    return (grad_query, grad_key, grad_value, earlier)

def to_blocks(array):
    shaped = array.reshape(array.shape[:2] + (array.shape[2] // SPAN, SPAN) + array.shape[3:])
    return jnp.moveaxis(shaped, 2, 0)

def from_blocks(blocked):
    moved = jnp.moveaxis(blocked, 0, 2)
    return moved.reshape(moved.shape[:2] + (moved.shape[2] * moved.shape[3],) + moved.shape[4:])

def reference(sources, source_ids, mix_weights, source_lengths, w_embed, w_qkv, w_out, forget, cotangent):
    positions = jnp.arange(LENGTH, dtype=jnp.int32)
    mixture = jnp.zeros((MIXTURES, LENGTH, PATCH), jnp.float32)
    for term in range(TERMS):
        chosen = sources[source_ids[:, term]].reshape(MIXTURES, LENGTH, PATCH)
        cover = jnp.where(positions[None, :] < source_lengths[:, term:term + 1], mix_weights[:, term:term + 1], 0.0)
        mixture = mixture + cover[:, :, None] * chosen

    def one_mixture(inputs):
        mixture_one, forget_one, cotangent_one = inputs
        mixture_half = mixture_one.astype(jnp.bfloat16)
        embedded = jnp.dot(mixture_half, w_embed.T, preferred_element_type=jnp.float32).astype(jnp.bfloat16)
        projected = jnp.dot(embedded, w_qkv, preferred_element_type=jnp.float32).astype(jnp.bfloat16)
        parts = projected.reshape(LENGTH, 3, H, HEAD).transpose(1, 2, 0, 3)
        queries = parts[0][None]
        key_rows = parts[1][None]
        value_rows = parts[2][None]
        log_gate = jnp.log1p(forget_one - 1.0)[None]
        query_blocks = to_blocks(queries)
        key_blocks = to_blocks(key_rows)
        value_blocks = to_blocks(value_rows)
        gate_blocks = to_blocks(log_gate)

        def forward_step(memory, inputs_block):
            read_block, updated = block_forward(inputs_block[0], inputs_block[1], inputs_block[2], inputs_block[3], memory)
            return (updated, (read_block, memory))
        start = jnp.zeros((1, H, HEAD, HEAD), jnp.float32)
        last_state, (read_blocks, block_states) = lax.scan(forward_step, start, (query_blocks, key_blocks, value_blocks, gate_blocks))
        read = from_blocks(read_blocks)
        inverse_rms = lax.rsqrt(lax.optimization_barrier(jnp.mean(read * read, axis=-1, keepdims=True)) + EPS)
        normed = read * inverse_rms
        normed_half = normed[0].transpose(1, 0, 2).reshape(LENGTH, D).astype(jnp.bfloat16)
        output_one = jnp.dot(normed_half, w_out, preferred_element_type=jnp.float32).astype(jnp.bfloat16)
        grad_out_one = jnp.dot(normed_half.T, cotangent_one, preferred_element_type=jnp.float32)
        grad_normed = jnp.dot(cotangent_one, w_out.T, preferred_element_type=jnp.float32)
        grad_normed = grad_normed.reshape(LENGTH, H, HEAD).transpose(1, 0, 2)[None]
        grad_read = (inverse_rms * (grad_normed - normed * lax.optimization_barrier(jnp.mean(grad_normed * normed, axis=-1, keepdims=True)))).astype(jnp.bfloat16)

        def backward_step(later, inputs_block):
            grad_query, grad_key, grad_value, earlier = block_backward(inputs_block[0], inputs_block[1], inputs_block[2], inputs_block[3], inputs_block[4], inputs_block[5], later)
            return (earlier, (grad_query, grad_key, grad_value))
        first_back, (query_grads, key_grads, value_grads) = lax.scan(backward_step, start, (query_blocks, key_blocks, value_blocks, to_blocks(grad_read), gate_blocks, block_states), reverse=True)
        stacked = jnp.stack([from_blocks(query_grads)[0], from_blocks(key_grads)[0], from_blocks(value_grads)[0]])
        grad_proj = stacked.transpose(2, 0, 1, 3).reshape(LENGTH, 3 * D).astype(jnp.bfloat16)
        grad_qkv_one = jnp.dot(embedded.T, grad_proj, preferred_element_type=jnp.float32)
        grad_embedded = jnp.dot(grad_proj, w_qkv.T, preferred_element_type=jnp.float32).astype(jnp.bfloat16)
        grad_embed_one = jnp.dot(grad_embedded.T, mixture_half, preferred_element_type=jnp.float32)
        return (output_one, grad_qkv_one, grad_out_one, grad_embed_one)
    outputs, grad_qkv_all, grad_out_all, grad_embed_all = lax.map(one_mixture, (mixture, forget, cotangent))
    return (outputs, lax.optimization_barrier(jnp.sum(grad_qkv_all, axis=0)), lax.optimization_barrier(jnp.sum(grad_out_all, axis=0)), lax.optimization_barrier(jnp.sum(grad_embed_all, axis=0)))
```

```python
import functools

import jax
import jax.numpy as jnp
from jax import lax
from jax.experimental import pallas as pl
from jax.experimental.pallas import tpu as pltpu
from jax.sharding import PartitionSpec as P

EPS = 1e-06
F32 = jnp.float32
BF16 = jnp.bfloat16
VMEM_LIMIT = 24 * 2**20


def exact(left, right, dims=((1,), (0,))):
    return lax.dot_general(
        left, right, (dims, ((), ())), precision=lax.Precision.HIGHEST, preferred_element_type=F32
    )


def quick(left, right, dims=((1,), (0,))):
    return lax.dot_general(
        left.astype(BF16), right.astype(BF16), (dims, ((), ())), preferred_element_type=F32
    )


def halves(array):
    high = array.astype(BF16)
    return high, (array - high.astype(F32)).astype(BF16)


def split_right(left, right, dims=((1,), (0,))):
    high, low = halves(right)
    return quick(left, high, dims) + quick(left, low, dims)


def rows_cols(shape):
    return lax.broadcasted_iota(jnp.int32, shape, 0), lax.broadcasted_iota(jnp.int32, shape, 1)


def block_mask(heads, high, wide):
    row, col = rows_cols((heads * high, heads * wide))
    return (row // high) == (col // wide)


def stacked(array, heads):
    return jnp.concatenate([array] * heads, axis=0)


def radices(count):
    found = []
    while count > 1:
        radix = 4 if count % 4 == 0 else 2 if count % 2 == 0 else count
        found.append(radix)
        count //= radix
    return found


def other(place, radix, slot):
    if radix & (radix - 1) == 0:
        return place ^ slot
    return (place + slot) % radix


def swap(array, axis, stride, radix, slot):
    pairs = []
    for source in range(lax.axis_size(axis)):
        place = (source // stride) % radix
        for target in range(radix):
            if other(target, radix, slot) == place:
                pairs.append((source, source + (target - place) * stride))
    return lax.ppermute(array, axis, pairs)


def call(kernel, outs, ins, smem=(), flops=0, scratch=()):
    specs = [
        pl.BlockSpec(memory_space=pltpu.SMEM if i in smem else pltpu.VMEM) for i in range(len(ins))
    ]
    return pl.pallas_call(
        kernel,
        out_shape=[jax.ShapeDtypeStruct(s, d) for s, d in outs],
        in_specs=specs,
        out_specs=[pl.BlockSpec(memory_space=pltpu.VMEM) for _ in outs],
        scratch_shapes=list(scratch),
        compiler_params=pltpu.CompilerParams(vmem_limit_bytes=VMEM_LIMIT),
        cost_estimate=pl.CostEstimate(flops=flops, bytes_accessed=1 << 20, transcendentals=0),
    )(*ins)


def mix_kernel(local, patch, mixes, ids, weights, lengths, src, *outs):
    me = lax.axis_index("mix")
    first = lax.axis_index("ctx") * (src.shape[1] * src.shape[2] // patch)
    held = src.shape[0]
    row, col = rows_cols(src.shape[1:])
    position = first + row * (src.shape[2] // patch) + col // patch
    for slot in range(mixes):
        target = other(me, mixes, slot)
        for b in range(local):
            total = jnp.zeros(src.shape[1:], F32)
            for term in range(ids.shape[1]):
                mixture = target * local + b
                at = ids[mixture, term] - me * held
                here = jnp.logical_and(at >= 0, at < held)
                factor = jnp.where(here, weights[mixture, term], 0.0)
                rows = src[jnp.where(here, at, 0)]
                total += jnp.where(position < lengths[mixture, term], factor, 0.0) * rows
            outs[slot][b] = total


def gram_kernel(heads, patch, count, *refs):
    parts, forget = refs[:count], refs[count]
    mt_ref, gx_ref, row_ref, pack_ref = refs[count + 1 :]
    local, _, steps = forget.shape
    lanes = heads * patch
    per = lanes // patch
    t, r = rows_cols((steps, steps // per))
    spread = (t // per == r).astype(BF16)
    t, lane = rows_cols((steps, lanes))
    chosen = t % per == lane // patch
    a, b_ = rows_cols((lanes, lanes))
    fold = (a % patch == b_ % patch).astype(BF16)
    s, t2 = rows_cols((steps, steps))
    upto = (s <= t2).astype(F32)
    pack_ref[...] = jnp.zeros_like(pack_ref)
    for b in range(local):
        total = parts[0][b]
        for part in parts[1:]:
            total = total + part[b]
        wide = quick(spread, total)
        mt = quick(jnp.where(chosen, wide, 0.0), fold)
        log_gate = jnp.log1p(forget[b] - 1.0)
        row_ref[b * heads : (b + 1) * heads] = exact(log_gate, upto)
        repeated = jnp.broadcast_to(log_gate[:, None, :], (heads, patch, steps)).reshape(lanes, steps)
        gx = exact(upto, repeated, ((0,), (1,)))
        last = gx[steps - 1 : steps]
        gram = quick(mt, mt * jnp.exp(last - gx), ((0,), (0,)))
        mt_ref[b] = mt.astype(BF16)
        gx_ref[b] = gx
        pack_ref[b * patch : (b + 1) * patch] = gram[:patch]
        pack_ref[local * patch + b : local * patch + b + 1] = last


def weight_kernel(heads, w_embed, w_qkv, w_out, cot, a_ref, m_ref, c_ref, b_ref, bb_ref):
    patch = w_embed.shape[1]
    width = w_out.shape[0]
    a = quick(w_embed[...], w_qkv[...], ((0,), (0,)))
    a_ref[...] = a
    mask = block_mask(heads, patch, width // heads)
    blocks = [
        jnp.where(mask, stacked(a[:, j * width : (j + 1) * width], heads), 0.0) for j in range(3)
    ]
    m_ref[...] = exact(blocks[0], blocks[1], ((1,), (1,)))
    c_ref[...] = exact(blocks[2], blocks[2], ((1,), (1,)))
    high, low = halves(blocks[2])
    product = quick(high, w_out[...]) + quick(low, w_out[...])
    b_ref[...] = product.astype(BF16)
    for b in range(cot.shape[0]):
        bb_ref[b] = quick(cot[b], product, ((1,), (1,)))


def weighted(left, mt, gx, grow, heads):
    steps, lanes = mt.shape
    patch = lanes // heads
    t, s = rows_cols((steps, steps))
    causal = t >= s
    _, lane = rows_cols((steps, lanes))
    result = jnp.zeros((steps, lanes), F32)
    for h in range(heads):
        own = lane // patch == h
        scores = quick(jnp.where(own, left, 0.0), mt, ((1,), (1,)))
        decay = jnp.exp(gx[:, h * patch : h * patch + 1] - grow[h : h + 1])
        scores = jnp.where(causal, scores * decay, 0.0)
        result = jnp.where(own, quick(scores, mt), result)
    return result


def intra_kernel(heads, mt, gx, grow, m, z_ref):
    for b in range(mt.shape[0]):
        left = split_right(mt[b], m[...])
        z_ref[b] = weighted(left, mt[b], gx[b], grow[b * heads : (b + 1) * heads], heads)


def level(packs, place, local, patch, wanted):
    radix = len(packs)
    at = [other(place, radix, slot) for slot in range(radix)]
    totals = [pack[local * patch :] for pack in packs]
    zero = jnp.zeros_like(totals[0])
    grams = None
    total = zero
    for m in range(radix):
        if wanted == "before" and m == 0:
            continue
        power = zero
        for k in range(radix):
            if k == m or (wanted == "before" and k == 0):
                continue
            after = at[k] > at[m]
            if wanted == "before":
                after = jnp.logical_and(after, at[k] < place)
            power = power + jnp.where(after, totals[k], 0.0)
        factor = jnp.exp(power)
        if wanted == "before":
            factor = jnp.where(at[m] < place, factor, 0.0)
            total = total + jnp.where(at[m] < place, totals[m], 0.0)
        else:
            total = total + totals[m]
        terms = [factor[b : b + 1] * packs[m][b * patch : (b + 1) * patch] for b in range(local)]
        grams = terms if grams is None else [g + x for g, x in zip(grams, terms)]
    return jnp.concatenate(grams + [total], axis=0)


def joined(near, far, local, patch):
    totals = near[local * patch :]
    factor = jnp.exp(totals)
    grams = [
        near[b * patch : (b + 1) * patch] + factor[b : b + 1] * far[b * patch : (b + 1) * patch]
        for b in range(local)
    ]
    return jnp.concatenate(grams + [totals + far[local * patch :]], axis=0)


def level_kernel(local, patch, stride, radix, first, *refs):
    place = (lax.axis_index("ctx") // stride) % radix
    packs = [ref[...] for ref in refs[:radix]]
    before = level(packs, place, local, patch, "before")
    if not first:
        before = joined(refs[radix][...], before, local, patch)
    refs[-2][...] = level(packs, place, local, patch, "whole")
    refs[-1][...] = before


def main_kernel(
    heads, stride, radix, near_given, mixes, *refs
):
    count = radix + int(near_given)
    packs = [ref[...] for ref in refs[:radix]]
    mt, gx, grow, intra, bb, m, c, big_b, a, w_out, cot = refs[count : count + 11]
    out_ref, *part_refs = refs[count + 11 : -1]
    z_scr = refs[-1]
    local, steps, lanes = mt.shape
    patch = lanes // heads
    width = w_out.shape[0]
    size = width // heads
    place = (lax.axis_index("ctx") // stride) % radix
    state = level(packs, place, local, patch, "before")
    if near_given:
        state = joined(refs[radix][...], state, local, patch)
    square = block_mask(heads, patch, patch)
    ones = square.astype(F32)
    x_total = jnp.zeros((patch, lanes), F32)
    big_z = jnp.zeros((lanes, width), F32)
    w_total = jnp.zeros((lanes, lanes), F32)
    for b in range(local):
        before = jnp.where(square, stacked(state[b * patch : (b + 1) * patch], heads), 0.0)
        grown = jnp.exp(gx[b])
        decays = grow[b * heads : (b + 1) * heads]
        z = intra[b] + grown * split_right(mt[b], exact(m[...], before))
        zc = exact(z, c[...])
        irms = lax.rsqrt(exact(z * zc, ones) / size + EPS)
        zn = z * irms
        znb = zn.astype(BF16)
        out_ref[b] = quick(znb, big_b[...]).astype(BF16)
        aligned = exact(zn * bb[b], ones) / size
        u = irms * (bb[b] - aligned * (irms * zc))
        y = weighted(u, mt[b], gx[b], decays, heads) + grown * split_right(u, before)
        x_total += quick(mt[b], y, ((0,), (0,)))[:patch]
        big_z += quick(znb, cot[b], ((0,), (0,)))
        w_total += quick(zn, aligned * zn, ((0,), (0,)))
    v = stacked_heads(a[:, 2 * width :], heads)
    y_total = -exact(jnp.where(square, w_total, 0.0), v)
    y_rows = []
    for h in range(heads):
        rows = slice(h * patch, (h + 1) * patch)
        high, low = halves(big_z[rows])
        kernel_rows = w_out[h * size : (h + 1) * size]
        y_rows.append(
            y_total[rows]
            + quick(high, kernel_rows, ((1,), (1,)))
            + quick(low, kernel_rows, ((1,), (1,)))
        )
    y_total = jnp.concatenate(y_rows, axis=0)
    per = lax.axis_size("ctx") // heads
    head = lax.axis_index("ctx") // per
    me = lax.axis_index("mix")
    panels = width // 128
    share = panels // mixes
    for k in range(panels):
        z_scr[k] = big_z[:, k * 128 : (k + 1) * 128]
    y_high = lanes // mixes
    x_high = patch // mixes
    z_scr[panels] = y_total
    z_scr[panels + 1, :patch] = x_total
    for slot in range(mixes):
        part = other(me, mixes, slot)
        out = part_refs[slot]
        at = 0
        for q in range(heads):
            for k in range(share):
                rows = pl.ds(other(head, heads, q) * patch, patch)
                out[at : at + patch] = z_scr[part * share + k, rows, :]
                at += patch
        out[at : at + y_high] = z_scr[panels, pl.ds(part * y_high, y_high), :]
        at += y_high
        out[at : at + x_high] = z_scr[panels + 1, pl.ds(part * x_high, x_high), :]


def stacked_heads(array, heads):
    size = array.shape[1] // heads
    return jnp.concatenate([array[:, h * size : (h + 1) * size] for h in range(heads)], axis=0)


def final_kernel(heads, mixes, rows_out, *refs):
    parts = refs[:mixes]
    a, w_embed, w_qkv = refs[mixes : mixes + 3]
    gq_ref, go_ref, ge_ref, scr, wide = refs[mixes + 3 :]
    patch = w_embed.shape[1]
    width = w_embed.shape[0]
    size = width // heads
    lanes = heads * patch
    panels = width // 128
    share = panels // mixes
    y_high = lanes // mixes
    x_high = patch // mixes
    me = lax.axis_index("mix")
    ctx = lax.axis_index("ctx")
    per = lax.axis_size("ctx") // heads
    head = ctx // per
    for slot in range(mixes):
        part = other(me, mixes, slot)
        at = 0
        for k in range(share):
            scr[part * share + k, :patch] = parts[slot][at : at + patch]
            at += patch
        scr[panels, pl.ds(part * y_high, y_high), :] = parts[slot][at : at + y_high]
        at += y_high
        scr[panels + 1, pl.ds(part * x_high, x_high), :] = parts[slot][at : at + x_high]
    y = scr[panels]
    x = scr[panels + 1, :patch]
    mask = block_mask(heads, patch, size)
    query, key, value = [a[:, j * width : (j + 1) * width] for j in range(3)]
    t_query = exact(x, jnp.where(mask, stacked(key, heads), 0.0))
    crossed = exact(x, query, ((0,), (0,)))
    t_key = [crossed[h * patch : (h + 1) * patch, h * size : (h + 1) * size] for h in range(heads)]
    t_value = [y[h * patch : (h + 1) * patch] for h in range(heads)]
    t = jnp.concatenate([t_query] + t_key + t_value, axis=1)
    high, low = halves(t)
    mine = pl.ds(pl.multiple_of(ctx * rows_out, rows_out), rows_out)
    embed_rows = w_embed[mine, :]
    qkv_rows = w_qkv[mine, :]
    gq_ref[...] = quick(embed_rows, high) + quick(embed_rows, low)
    ge_ref[...] = quick(qkv_rows, high, ((1,), (1,))) + quick(qkv_rows, low, ((1,), (1,)))
    big_z = jnp.concatenate([scr[k, :patch] for k in range(panels)], axis=1)
    for h in range(heads):
        wide[h, :patch] = value[:, h * size : (h + 1) * size]
    own = wide[head, :patch]
    wide[heads + 1 :, :, :] = jnp.stack(
        [
            panel
            for panel in jnp.split(exact(own, big_z, ((0,), (0,))), panels, axis=1)
        ]
    )
    first = pl.ds(pl.multiple_of((ctx % per) * rows_out, rows_out), rows_out)
    for k in range(panels):
        go_ref[:, k * 128 : (k + 1) * 128] = wide[heads + 1 + k, first, :]


def shards(
    sources, source_ids, mix_weights, source_lengths, w_embed, w_qkv, w_out, forget, cotangent
):
    mixes = lax.axis_size("mix")
    count = lax.axis_size("ctx")
    patch = w_embed.shape[1]
    local, heads, steps = forget.shape
    width = w_out.shape[0]
    size = width // heads
    lanes = heads * patch
    held = sources.shape[0]
    packed = sources.reshape(held, steps * patch // lanes, lanes)
    partial_shape = ((local, steps * patch // lanes, lanes), F32)
    partials = call(
        functools.partial(mix_kernel, local, patch, mixes),
        [partial_shape] * mixes,
        [source_ids, mix_weights, source_lengths, packed],
        smem=(0, 1, 2),
    )
    got = [partials[0]] + [swap(partials[s], "mix", 1, mixes, s) for s in range(1, mixes)]
    high = -(-local // 8) * 8
    pack_shape = ((local * patch + high, lanes), F32)
    mt, gx, grow, pack = call(
        functools.partial(gram_kernel, heads, patch, mixes),
        [
            ((local, steps, lanes), BF16),
            ((local, steps, lanes), F32),
            ((local * heads, steps), F32),
            pack_shape,
        ],
        got + [forget],
    )
    a, m, c, big_b, bb = call(
        functools.partial(weight_kernel, heads),
        [
            ((patch, 3 * width), F32),
            ((lanes, lanes), F32),
            ((lanes, lanes), F32),
            ((lanes, width), BF16),
            ((local, steps, lanes), F32),
        ],
        [w_embed, w_qkv, w_out, cotangent],
        flops=10**9,
    )
    (intra,) = call(
        functools.partial(intra_kernel, heads),
        [((local, steps, lanes), F32)],
        [mt, gx, grow, m],
        flops=10**9,
    )
    steps_up = radices(count)
    stride = 1
    near = []
    for i, radix in enumerate(steps_up):
        packs = [pack] + [swap(pack, "ctx", stride, radix, s) for s in range(1, radix)]
        if i == len(steps_up) - 1:
            break
        pack, before = call(
            functools.partial(level_kernel, local, patch, stride, radix, i == 0),
            [pack_shape] * 2,
            packs + near,
        )
        near = [before]
        stride *= radix
    per = count // heads
    part_rows = heads * (width // 128 // mixes) * patch + lanes // mixes + patch // mixes
    output, *parts = call(
        functools.partial(main_kernel, heads, stride, radix, bool(near), mixes),
        [((local, steps, width), BF16)] + [((part_rows, 128), F32)] * mixes,
        packs + near + [mt, gx, grow, intra, bb, m, c, big_b, a, w_out, cotangent],
        flops=10**9,
        scratch=[pltpu.VMEM((width // 128 + 2, lanes, 128), F32)],
    )
    total = parts[0]
    for s in range(1, mixes):
        total = total + swap(parts[s], "mix", 1, mixes, s)
    z_high = (width // 128 // mixes) * patch
    z_slots = [total[q * z_high : (q + 1) * z_high] for q in range(heads)]
    xy = total[heads * z_high :]
    inner = []
    stride = 1
    for radix in radices(per):
        inner.append((stride, radix))
        stride *= radix
    across = (per, heads)

    def z_across(z):
        return z[0] + sum(swap(z[s], "ctx", per, heads, s) for s in range(1, heads))

    def everywhere(array, where):
        return array + sum(swap(array, "ctx", where[0], where[1], s) for s in range(1, where[1]))

    z = z_slots
    stages = len(inner) + 1
    for stage in range(stages):
        z = z_across(z) if stage == 0 else everywhere(z, inner[stage - 1])
        xy = everywhere(xy, inner[stage] if stage < len(inner) else across)
    both = jnp.concatenate([z, xy], axis=0)
    pieces = [both] + [swap(both, "mix", 1, mixes, s) for s in range(1, mixes)]
    rows_out = width // count
    grads = call(
        functools.partial(final_kernel, heads, mixes, rows_out),
        [((rows_out, 3 * width), F32), ((rows_out, width), F32), ((rows_out, patch), F32)],
        pieces + [a, w_embed, w_qkv],
        scratch=[
            pltpu.VMEM((width // 128 + 2, lanes, 128), F32),
            pltpu.VMEM((heads + 1 + width // 128, size, 128), F32),
        ],
    )
    return output, grads[0], grads[1], grads[2]


def solution(mesh):
    placed = (
        P("mix", "ctx"),
        P(),
        P(),
        P(),
        P(),
        P(),
        P(),
        P("mix", None, "ctx"),
        P("mix", "ctx", None),
    )
    return jax.shard_map(
        shards,
        mesh=mesh,
        in_specs=placed,
        out_specs=(P("mix", "ctx", None), P("ctx", None), P("ctx", None), P("ctx", None)),
        check_vma=False,
    )
```

```python
import functools

import jax
import jax.numpy as jnp
from jax import lax
from jax.experimental import pallas as pl
from jax.experimental.pallas import tpu as pltpu
from jax.sharding import PartitionSpec as P

EPS = 1e-06
F32 = jnp.float32
BF16 = jnp.bfloat16
ORDERS = {4: (1, 2, 3)}
VMEM_LIMIT = 24 * 2**20


def exact(left, right, dims=((1,), (0,))):
    return lax.dot_general(
        left, right, (dims, ((), ())), precision=lax.Precision.HIGHEST, preferred_element_type=F32
    )


def quick(left, right, dims=((1,), (0,))):
    return lax.dot_general(
        left.astype(BF16), right.astype(BF16), (dims, ((), ())), preferred_element_type=F32
    )


def halves(array):
    high = array.astype(BF16)
    return high, (array - high.astype(F32)).astype(BF16)


def split_right(left, right, dims=((1,), (0,))):
    high, low = halves(right)
    return quick(left, high, dims) + quick(left, low, dims)


def rows_cols(shape):
    return lax.broadcasted_iota(jnp.int32, shape, 0), lax.broadcasted_iota(jnp.int32, shape, 1)


def block_mask(heads, high, wide):
    row, col = rows_cols((heads * high, heads * wide))
    return (row // high) == (col // wide)


def stacked(array, heads):
    return jnp.concatenate([array] * heads, axis=0)


def radices(count):
    found = []
    while count > 1:
        radix = 4 if count % 4 == 0 else 2 if count % 2 == 0 else count
        found.append(radix)
        count //= radix
    return found


def other(place, radix, slot):
    if radix & (radix - 1) == 0:
        return place ^ slot
    return (place + slot) % radix


def swap(array, axis, stride, radix, slot):
    pairs = []
    for source in range(lax.axis_size(axis)):
        place = (source // stride) % radix
        for target in range(radix):
            if other(target, radix, slot) == place:
                pairs.append((source, source + (target - place) * stride))
    return lax.ppermute(array, axis, pairs)


def call(kernel, outs, ins, hbm=(), flops=0, scratch=()):
    specs = [
        pl.BlockSpec(memory_space=pltpu.HBM if i in hbm else pltpu.VMEM) for i in range(len(ins))
    ]
    ins = [
        pltpu.with_memory_space_constraint(x, pltpu.HBM) if i in hbm else x
        for i, x in enumerate(ins)
    ]
    return pl.pallas_call(
        kernel,
        out_shape=[jax.ShapeDtypeStruct(s, d) for s, d in outs],
        in_specs=specs,
        out_specs=[pl.BlockSpec(memory_space=pltpu.VMEM) for _ in outs],
        scratch_shapes=list(scratch),
        compiler_params=pltpu.CompilerParams(vmem_limit_bytes=VMEM_LIMIT),
        cost_estimate=pl.CostEstimate(flops=flops, bytes_accessed=1 << 20, transcendentals=0),
    )(*ins)


def rebuilt(high, low):
    top = jnp.concatenate([high, low], axis=1)
    bottom = jnp.concatenate([high, jnp.zeros_like(low)], axis=1)
    return jnp.concatenate([top, bottom], axis=0)


def pair(array):
    return jnp.concatenate(halves(array), axis=1)


def fine(left, right):
    both = quick(left, right)
    half = both.shape[1] // 2
    return both[:, :half] + both[:, half:]


def summed(array, ones):
    return quick(pair(array), ones)


def fetch(sources, targets, sems):
    copies = [
        pltpu.make_async_copy(source, target, sems.at[i])
        for i, (source, target) in enumerate(zip(sources, targets))
    ]
    for copy in copies:
        copy.start()
    return copies


def mix_kernel(local, patch, mixes, ids_hbm, weights_hbm, lengths_hbm, src_hbm, *rest):
    outs, (ids, weights, lengths, raw, src, sems) = rest[:mixes], rest[mixes:]
    copies = fetch((ids_hbm, weights_hbm, lengths_hbm, src_hbm), (ids, weights, lengths, raw), sems)
    me = lax.axis_index("mix")
    held, high, lanes = src.shape
    first = lax.axis_index("ctx") * (high * lanes // patch)
    row, col = rows_cols((high, lanes))
    position = first + row * (lanes // patch) + col // patch
    for copy in copies:
        copy.wait()
    for r in range(high):
        rows = raw[:, r * lanes : (r + 1) * lanes]
        for s in range(held):
            src[s, r : r + 1] = rows[s : s + 1]
    for slot in range(mixes):
        target = other(me, mixes, slot)
        for b in range(local):
            total = jnp.zeros((high, lanes), F32)
            for term in range(ids.shape[1]):
                mixture = target * local + b
                at = ids[mixture, term] - me * held
                here = jnp.logical_and(at >= 0, at < held)
                factor = jnp.where(here, weights[mixture, term], 0.0)
                rows = src[jnp.where(here, at, 0)]
                total += jnp.where(position < lengths[mixture, term], factor, 0.0) * rows
            outs[slot][b] = total


def gate_kernel(patch, forget_hbm, gx_ref, row_ref, forget, sems):
    copies = fetch((forget_hbm,), (forget,), sems)
    local, heads, steps = forget.shape
    lanes = heads * patch
    s, t = rows_cols((steps, steps))
    upto = (s <= t).astype(BF16)
    for copy in copies:
        copy.wait()
    for b in range(local):
        log_gate = jnp.log1p(forget[b] - 1.0)
        high, low = halves(log_gate)
        lowest = (log_gate - high.astype(F32) - low.astype(F32)).astype(BF16)
        sums = quick(jnp.concatenate([high, low, lowest, jnp.zeros_like(low)], axis=0), upto)
        sums = sums[:heads] + sums[heads : 2 * heads] + sums[2 * heads : 3 * heads]
        row_ref[b * heads : (b + 1) * heads] = sums
        wide = jnp.broadcast_to(sums[:, None, :], (heads, patch, steps)).reshape(lanes, steps)
        gx_ref[b] = wide.T


def gram_kernel(heads, patch, count, *refs):
    parts, gx_ref = refs[:count], refs[count]
    mt_ref, pack_ref = refs[count + 1 :]
    local, steps, lanes = gx_ref.shape
    per = lanes // patch
    t, r = rows_cols((steps, steps // per))
    spread = (t // per == r).astype(BF16)
    t, lane = rows_cols((steps, lanes))
    chosen = t % per == lane // patch
    a, b_ = rows_cols((lanes, lanes))
    fold = (a % patch == b_ % patch).astype(BF16)
    pack_ref[...] = jnp.zeros_like(pack_ref)
    for b in range(local):
        total = parts[0][b]
        for part in parts[1:]:
            total = total + part[b]
        wide = quick(spread, total)
        mt = quick(jnp.where(chosen, wide, 0.0), fold)
        gx = gx_ref[b]
        last = gx[steps - 1 : steps]
        gram = quick(mt[:, :patch], mt * jnp.exp(last - gx), ((0,), (0,)))
        mt_ref[b] = mt.astype(BF16)
        pack_ref[b * patch : (b + 1) * patch] = gram
        pack_ref[local * patch + b : local * patch + b + 1] = last


def weight_kernel(heads, per, *refs):
    embed_hbm, qkv_hbm, out_hbm, cot_hbm, _ = refs[:5]
    a_ref, m_ref, c_ref, b_ref, bb_ref, k_ref, v_ref, own_ref, qkv_ref = refs[5:14]
    embed, qkv, w_out, cot, tall, sems = refs[14:]
    copies = fetch((embed_hbm, qkv_hbm, out_hbm, cot_hbm), (embed, qkv, w_out, cot), sems)
    patch, width = embed.shape
    rows_out = qkv_ref.shape[0]
    ctx = lax.axis_index("ctx")
    mine = pl.ds(pl.multiple_of(ctx * rows_out, rows_out), rows_out)
    copies[0].wait()
    tall[:, :patch] = embed[...].astype(F32).T
    copies[1].wait()
    a = quick(embed[...], qkv[...])
    a_ref[...] = a
    qkv_ref[...] = qkv[mine, :]
    mask = block_mask(heads, patch, width // heads)
    query, key, value = [
        jnp.where(mask, stacked(a[:, j * width : (j + 1) * width], heads), 0.0) for j in range(3)
    ]
    across = ((1,), (1,))
    key_high, key_low = halves(key)
    value_high, value_low = halves(value)
    query_high, query_low = halves(query)
    k_ref[...] = jnp.concatenate([key_high, key_high, key_low], axis=0)
    m = quick(query_high, key_high, across) + quick(query_high, key_low, across)
    m = m + quick(query_low, key_high, across)
    m_ref[...] = rebuilt(*halves(m))
    mixed = quick(value_high, value_low, across)
    c = quick(value_high, value_high, across) + mixed + mixed.T
    c_ref[...] = rebuilt(*halves(c))
    v_ref[...] = stacked_heads(a[:, 2 * width :], heads)
    tall[:, patch : 2 * patch] = a[:, 2 * width :].T
    own_ref[...] = tall[mine, :]
    copies[2].wait()
    product = (quick(value_high, w_out[...]) + quick(value_low, w_out[...])).astype(BF16)
    b_ref[...] = product
    copies[3].wait()
    for b in range(cot.shape[0]):
        bb_ref[b] = quick(cot[b], product, across)


def weighted(left, mt, decay, heads):
    steps, lanes = mt.shape
    patch = lanes // heads
    _, lane = rows_cols((steps, lanes))
    own = [lane // patch == h for h in range(heads)]
    lefts = jnp.concatenate([jnp.where(o, left, 0.0).astype(BF16) for o in own], axis=0)
    scores = quick(lefts, mt, ((1,), (1,))) * decay
    found = quick(scores, mt)
    result = found[:steps]
    for h in range(1, heads):
        result = jnp.where(own[h], found[h * steps : (h + 1) * steps], result)
    return result


def intra_kernel(heads, mt, gx, grow, m, z_ref, q_ref, decay_ref):
    _, steps, lanes = mt.shape
    patch = lanes // heads
    t, s = rows_cols((steps, steps))
    causal = t >= s
    for b in range(mt.shape[0]):
        for h in range(heads):
            at = b * heads + h
            decay = jnp.exp(gx[b, :, h * patch : h * patch + 1] - grow[at : at + 1])
            decay_ref[b, h * steps : (h + 1) * steps] = jnp.where(causal, decay, 0.0)
        query = fine(jnp.concatenate([mt[b], jnp.zeros_like(mt[b])], axis=1), m[...])
        q_ref[b] = pair(query)
        z_ref[b] = weighted(query, mt[b], decay_ref[b], heads)


def level(packs, place, local, patch, wanted):
    radix = len(packs)
    at = [other(place, radix, slot) for slot in range(radix)]
    totals = [pack[local * patch :] for pack in packs]
    zero = jnp.zeros_like(totals[0])
    grams = None
    total = zero
    for m in range(radix):
        if wanted == "before" and m == 0:
            continue
        power = zero
        for k in range(radix):
            if k == m or (wanted == "before" and k == 0):
                continue
            after = at[k] > at[m]
            if wanted == "before":
                after = jnp.logical_and(after, at[k] < place)
            power = power + jnp.where(after, totals[k], 0.0)
        factor = jnp.exp(power)
        if wanted == "before":
            factor = jnp.where(at[m] < place, factor, 0.0)
            total = total + jnp.where(at[m] < place, totals[m], 0.0)
        else:
            total = total + totals[m]
        terms = [factor[b : b + 1] * packs[m][b * patch : (b + 1) * patch] for b in range(local)]
        grams = terms if grams is None else [g + x for g, x in zip(grams, terms)]
    return jnp.concatenate(grams + [total], axis=0)


def joined(near, far, local, patch):
    totals = near[local * patch :]
    factor = jnp.exp(totals)
    grams = [
        near[b * patch : (b + 1) * patch] + factor[b : b + 1] * far[b * patch : (b + 1) * patch]
        for b in range(local)
    ]
    return jnp.concatenate(grams + [totals + far[local * patch :]], axis=0)


def in_slots(packs):
    order = (0,) + ORDERS.get(len(packs), tuple(range(1, len(packs))))
    return [packs[order.index(slot)] for slot in range(len(packs))]


def level_kernel(local, patch, stride, radix, first, *refs):
    place = (lax.axis_index("ctx") // stride) % radix
    packs = in_slots([ref[...] for ref in refs[:radix]])
    before = level(packs, place, local, patch, "before")
    if not first:
        before = joined(refs[radix][...], before, local, patch)
    refs[-2][...] = level(packs, place, local, patch, "whole")
    refs[-1][...] = before


def main_kernel(heads, stride, radix, near_given, mixes, *refs):
    count = radix + int(near_given)
    packs = in_slots([ref[...] for ref in refs[:radix]])
    mt, gx, decay, intra, query, bb, c, big_b, v, w_out, cot = refs[count : count + 11]
    out_ref, *part_refs = refs[count + 11 : -1]
    z_scr = refs[-1]
    local, steps, lanes = mt.shape
    patch = lanes // heads
    width = w_out.shape[0]
    size = width // heads
    place = (lax.axis_index("ctx") // stride) % radix
    state = level(packs, place, local, patch, "before")
    if near_given:
        state = joined(refs[radix][...], state, local, patch)
    square = block_mask(heads, patch, patch)
    ones = jnp.concatenate([square.astype(BF16)] * 2, axis=0)
    x_total = jnp.zeros((patch, lanes), F32)
    zw_total = jnp.zeros((lanes, width + lanes), F32)
    for b in range(local):
        before = jnp.where(square, stacked(state[b * patch : (b + 1) * patch], heads), 0.0)
        before = rebuilt(*halves(before))
        grown = jnp.exp(gx[b])
        z = intra[b] + grown * fine(query[b], before)
        zc = fine(pair(z), c[...])
        irms = lax.rsqrt(summed(z * zc, ones) * (1.0 / size) + EPS)
        zn = z * irms
        znb = zn.astype(BF16)
        out_ref[b] = quick(znb, big_b[...]).astype(BF16)
        aligned = summed(zn * bb[b], ones) * (1.0 / size)
        u = irms * (bb[b] - aligned * (irms * zc))
        y = weighted(u, mt[b], decay[b], heads) + grown * fine(pair(u), before)
        x_total += quick(mt[b, :, :patch], y, ((0,), (0,)))
        right = jnp.concatenate([cot[b], (aligned * zn).astype(BF16)], axis=1)
        zw_total += quick(znb, right, ((0,), (0,)))
    big_z = zw_total[:, :width]
    w_total = jnp.where(square, zw_total[:, width:], 0.0)
    y_total = -fine(pair(w_total), rebuilt(*halves(v[...])))
    y_rows = []
    for h in range(heads):
        rows = slice(h * patch, (h + 1) * patch)
        both = jnp.concatenate(halves(big_z[rows]), axis=0)
        found = quick(both, w_out[h * size : (h + 1) * size], ((1,), (1,)))
        y_rows.append(y_total[rows] + found[:patch] + found[patch:])
    y_total = jnp.concatenate(y_rows, axis=0)
    per = lax.axis_size("ctx") // heads
    head = lax.axis_index("ctx") // per
    me = lax.axis_index("mix")
    panels = width // 128
    share = panels // mixes
    for k in range(panels):
        z_scr[k] = big_z[:, k * 128 : (k + 1) * 128]
    y_high = lanes // mixes
    x_high = patch // mixes
    z_scr[panels] = y_total
    z_scr[panels + 1, :patch] = x_total
    for slot in range(mixes):
        part = other(me, mixes, slot)
        out = part_refs[slot]
        at = 0
        for q in range(heads):
            for k in range(share):
                rows = pl.ds(other(head, heads, q) * patch, patch)
                out[at : at + patch] = z_scr[part * share + k, rows, :]
                at += patch
        out[at : at + y_high] = z_scr[panels, pl.ds(part * y_high, y_high), :]
        at += y_high
        out[at : at + x_high] = z_scr[panels + 1, pl.ds(part * x_high, x_high), :]


def stacked_heads(array, heads):
    size = array.shape[1] // heads
    return jnp.concatenate([array[:, h * size : (h + 1) * size] for h in range(heads)], axis=0)


def final_kernel(heads, mixes, *refs):
    parts = refs[:mixes]
    a, keys, own, qkv_rows = refs[mixes : mixes + 4]
    gq_ref, go_ref, ge_ref, scr = refs[mixes + 4 :]
    patch = ge_ref.shape[1]
    width = go_ref.shape[1]
    size = width // heads
    lanes = heads * patch
    panels = width // 128
    share = panels // mixes
    y_high = lanes // mixes
    x_high = patch // mixes
    me = lax.axis_index("mix")
    for slot in range(mixes):
        part = other(me, mixes, slot)
        at = 0
        for k in range(share):
            scr[part * share + k, :patch] = parts[slot][at : at + patch]
            at += patch
        scr[panels, pl.ds(part * y_high, y_high), :] = parts[slot][at : at + y_high]
        at += y_high
        scr[panels + 1, pl.ds(part * x_high, x_high), :] = parts[slot][at : at + x_high]
    y = scr[panels]
    x_high, x_low = halves(scr[panels + 1, :patch])
    t_query = quick(jnp.concatenate([x_high, x_low, x_high], axis=1), keys[...])
    query_high, query_low = halves(a[:, :width])
    crossed = quick(
        jnp.concatenate([x_high, x_low, x_high], axis=0),
        jnp.concatenate([query_high, query_high, query_low], axis=0),
        ((0,), (0,)),
    )
    t_key = [crossed[h * patch : (h + 1) * patch, h * size : (h + 1) * size] for h in range(heads)]
    t_value = [y[h * patch : (h + 1) * patch] for h in range(heads)]
    t = jnp.concatenate([t_query] + t_key + t_value, axis=1)
    high, low = halves(t)
    embed_rows = own[:, :patch].astype(BF16)
    gq_ref[...] = quick(embed_rows, high) + quick(embed_rows, low)
    ge_ref[...] = quick(qkv_rows[...], high, ((1,), (1,))) + quick(qkv_rows[...], low, ((1,), (1,)))
    v_high, v_low = halves(own[:, patch : 2 * patch])
    z_high, z_low = halves(jnp.concatenate([scr[k, :patch] for k in range(panels)], axis=1))
    go_ref[...] = quick(
        jnp.concatenate([v_high, v_low, v_high], axis=1),
        jnp.concatenate([z_high, z_high, z_low], axis=0),
    )


def slot_kernel(heads, z_high, *refs):
    parts, slots = refs[:-heads], refs[-heads:]
    total = parts[0][...]
    for part in parts[1:]:
        total = total + part[...]
    for q in range(heads):
        slots[q][:z_high] = total[q * z_high : (q + 1) * z_high]
        slots[q][z_high:] = total[heads * z_high :]


def add_kernel(*refs):
    total = refs[0][...]
    for ref in refs[1:-1]:
        total = total + ref[...]
    refs[-1][...] = total


def added(arrays):
    (total,) = call(add_kernel, [(arrays[0].shape, F32)], arrays)
    return total


def shards(
    sources, source_ids, mix_weights, source_lengths, w_embed, w_qkv, w_out, forget, cotangent
):
    mixes = lax.axis_size("mix")
    count = lax.axis_size("ctx")
    patch = w_embed.shape[1]
    local, heads, steps = forget.shape
    width = w_out.shape[0]
    size = width // heads
    lanes = heads * patch
    held = sources.shape[0]
    rows_out = width // count
    per = count // heads
    dma = pltpu.SemaphoreType.DMA
    partial_shape = (local, steps * patch // lanes, lanes)
    partials = call(
        functools.partial(mix_kernel, local, patch, mixes),
        [(partial_shape, F32)] * mixes,
        [source_ids, mix_weights, source_lengths, sources],
        hbm=(0, 1, 2, 3),
        scratch=[
            pltpu.SMEM(source_ids.shape, jnp.int32),
            pltpu.SMEM(mix_weights.shape, F32),
            pltpu.SMEM(source_lengths.shape, jnp.int32),
            pltpu.VMEM(sources.shape, F32),
            pltpu.VMEM((held,) + partial_shape[1:], F32),
            dma((4,)),
        ],
    )
    got = [partials[0]] + [swap(partials[s], "mix", 1, mixes, s) for s in range(1, mixes)]
    gx, grow = call(
        functools.partial(gate_kernel, patch),
        [((local, steps, lanes), F32), ((local * heads, steps), F32)],
        [forget],
        hbm=(0,),
        flops=10**8,
        scratch=[pltpu.VMEM(forget.shape, F32), dma((1,))],
    )
    high = -(-local // 8) * 8
    pack_shape = ((local * patch + high, lanes), F32)
    mt, pack = call(
        functools.partial(gram_kernel, heads, patch, mixes),
        [((local, steps, lanes), BF16), pack_shape],
        got + [gx],
    )
    a, m, c, big_b, bb, keys, v, own, qkv_rows = call(
        functools.partial(weight_kernel, heads, per),
        [
            ((patch, 3 * width), F32),
            ((2 * lanes, 2 * lanes), BF16),
            ((2 * lanes, 2 * lanes), BF16),
            ((lanes, width), BF16),
            ((local, steps, lanes), F32),
            ((3 * lanes, width), BF16),
            ((lanes, size), F32),
            ((rows_out, 2 * patch), F32),
            ((rows_out, 3 * width), BF16),
        ],
        [w_embed.T, w_qkv, w_out, cotangent, pack],
        hbm=(0, 1, 2, 3),
        flops=10**9,
        scratch=[
            pltpu.VMEM((patch, width), BF16),
            pltpu.VMEM(w_qkv.shape, BF16),
            pltpu.VMEM(w_out.shape, BF16),
            pltpu.VMEM(cotangent.shape, BF16),
            pltpu.VMEM((width, 2 * patch), F32),
            dma((4,)),
        ],
    )
    intra, query, decay = call(
        functools.partial(intra_kernel, heads),
        [
            ((local, steps, lanes), F32),
            ((local, steps, 2 * lanes), BF16),
            ((local, heads * steps, steps), F32),
        ],
        [mt, gx, grow, m],
        flops=10**9,
    )
    steps_up = radices(count)
    stride = 1
    near = []
    for i, radix in enumerate(steps_up):
        order = ORDERS.get(radix, tuple(range(1, radix)))
        packs = [pack] + [swap(pack, "ctx", stride, radix, s) for s in order]
        if i == len(steps_up) - 1:
            break
        pack, before = call(
            functools.partial(level_kernel, local, patch, stride, radix, i == 0),
            [pack_shape] * 2,
            packs + near,
        )
        near = [before]
        stride *= radix
    part_rows = heads * (width // 128 // mixes) * patch + lanes // mixes + patch // mixes
    output, *parts = call(
        functools.partial(main_kernel, heads, stride, radix, bool(near), mixes),
        [((local, steps, width), BF16)] + [((part_rows, 128), F32)] * mixes,
        packs + near + [mt, gx, decay, intra, query, bb, c, big_b, v, w_out, cotangent],
        flops=10**9,
        scratch=[pltpu.VMEM((width // 128 + 2, lanes, 128), F32)],
    )
    z_high = (width // 128 // mixes) * patch
    y_high = part_rows - heads * z_high
    slots = call(
        functools.partial(slot_kernel, heads, z_high),
        [((z_high + y_high, 128), F32)] * heads,
        [parts[0]] + [swap(parts[s], "mix", 1, mixes, s) for s in range(1, mixes)],
    )
    order = ORDERS.get(heads, tuple(range(1, heads)))
    both = added([slots[0]] + [swap(slots[s], "ctx", per, heads, s) for s in order])
    stride = 1
    for radix in radices(per):
        order = ORDERS.get(radix, tuple(range(1, radix)))
        both = added([both] + [swap(both, "ctx", stride, radix, s) for s in order])
        stride *= radix
    pieces = [both] + [swap(both, "mix", 1, mixes, s) for s in range(1, mixes)]
    grads = call(
        functools.partial(final_kernel, heads, mixes),
        [((rows_out, 3 * width), F32), ((rows_out, width), F32), ((rows_out, patch), F32)],
        pieces + [a, keys, own, qkv_rows],
        scratch=[pltpu.VMEM((width // 128 + 2, lanes, 128), F32)],
    )
    return output, grads[0], grads[1], grads[2]


def solution(mesh):
    placed = (
        P("mix", "ctx"),
        P(),
        P(),
        P(),
        P(),
        P(),
        P(),
        P("mix", None, "ctx"),
        P("mix", "ctx", None),
    )
    return jax.shard_map(
        shards,
        mesh=mesh,
        in_specs=placed,
        out_specs=(P("mix", "ctx", None), P("ctx", None), P("ctx", None), P("ctx", None)),
        check_vma=False,
    )
```

```python
import functools

import jax
import jax.numpy as jnp
from jax import lax
from jax.experimental import pallas as pl
from jax.experimental.pallas import tpu as pltpu
from jax.sharding import PartitionSpec as P

EPS = 1e-06
F32 = jnp.float32
BF16 = jnp.bfloat16
ORDERS = {4: (1, 2, 3)}
VMEM_LIMIT = 24 * 2**20


def quick(left, right, dims=((1,), (0,))):
    return lax.dot_general(
        left.astype(BF16), right.astype(BF16), (dims, ((), ())), preferred_element_type=F32
    )


def halves(array):
    high = array.astype(BF16)
    return high, (array - high.astype(F32)).astype(BF16)


def rows_cols(shape):
    return lax.broadcasted_iota(jnp.int32, shape, 0), lax.broadcasted_iota(jnp.int32, shape, 1)


def block_mask(heads, high, wide):
    row, col = rows_cols((heads * high, heads * wide))
    return (row // high) == (col // wide)


def stacked(array, heads):
    return jnp.concatenate([array] * heads, axis=0)


def radices(count):
    found = []
    while count > 1:
        radix = 4 if count % 4 == 0 else 2 if count % 2 == 0 else count
        found.append(radix)
        count //= radix
    return found


def other(place, radix, slot):
    if radix & (radix - 1) == 0:
        return place ^ slot
    return (place + slot) % radix


def swap(array, axis, stride, radix, slot):
    pairs = []
    for source in range(lax.axis_size(axis)):
        place = (source // stride) % radix
        for target in range(radix):
            if other(target, radix, slot) == place:
                pairs.append((source, source + (target - place) * stride))
    return lax.ppermute(array, axis, pairs)


def call(kernel, outs, ins, hbm=(), out_hbm=(), flops=0, scratch=()):
    specs = [
        pl.BlockSpec(memory_space=pltpu.HBM if i in hbm else pltpu.VMEM) for i in range(len(ins))
    ]
    ins = [
        pltpu.with_memory_space_constraint(x, pltpu.HBM) if i in hbm else x
        for i, x in enumerate(ins)
    ]
    return pl.pallas_call(
        kernel,
        out_shape=[jax.ShapeDtypeStruct(s, d) for s, d in outs],
        in_specs=specs,
        out_specs=[
            pl.BlockSpec(memory_space=pl.ANY if i in out_hbm else pltpu.VMEM)
            for i in range(len(outs))
        ],
        scratch_shapes=list(scratch),
        compiler_params=pltpu.CompilerParams(vmem_limit_bytes=VMEM_LIMIT),
        cost_estimate=pl.CostEstimate(flops=flops, bytes_accessed=1 << 20, transcendentals=0),
    )(*ins)


def rebuilt(high, low):
    top = jnp.concatenate([high, low], axis=1)
    bottom = jnp.concatenate([high, jnp.zeros_like(low)], axis=1)
    return jnp.concatenate([top, bottom], axis=0)


def pair(array):
    return jnp.concatenate(halves(array), axis=1)


def fine(left, right):
    both = quick(left, right)
    half = both.shape[1] // 2
    return both[:, :half] + both[:, half:]


def summed(array, ones):
    return quick(pair(array), ones)


def fetch(sources, targets, sems):
    copies = [
        pltpu.make_async_copy(source, target, sems.at[i])
        for i, (source, target) in enumerate(zip(sources, targets))
    ]
    for copy in copies:
        copy.start()
    return copies


def mix_kernel(local, patch, mixes, ids_hbm, weights_hbm, lengths_hbm, src_hbm, *rest):
    outs, (ids, weights, lengths, raw, src, sems) = rest[:mixes], rest[mixes:]
    copies = fetch((ids_hbm, weights_hbm, lengths_hbm, src_hbm), (ids, weights, lengths, raw), sems)
    me = lax.axis_index("mix")
    held, high, lanes = src.shape
    first = lax.axis_index("ctx") * (high * lanes // patch)
    row, col = rows_cols((high, lanes))
    position = first + row * (lanes // patch) + col // patch
    for copy in copies:
        copy.wait()
    for r in range(high):
        rows = raw[:, r * lanes : (r + 1) * lanes]
        for s in range(held):
            src[s, r : r + 1] = rows[s : s + 1]
    for slot in range(mixes):
        target = other(me, mixes, slot)
        for b in range(local):
            total = jnp.zeros((high, lanes), F32)
            for term in range(ids.shape[1]):
                mixture = target * local + b
                at = ids[mixture, term] - me * held
                here = jnp.logical_and(at >= 0, at < held)
                factor = jnp.where(here, weights[mixture, term], 0.0)
                rows = src[jnp.where(here, at, 0)]
                total += jnp.where(position < lengths[mixture, term], factor, 0.0) * rows
            outs[slot][b] = total


def gate_kernel(patch, forget_hbm, gx_ref, fade_ref, row_ref, forget, sems):
    copies = fetch((forget_hbm,), (forget,), sems)
    local, heads, steps = forget.shape
    lanes = heads * patch
    s, t = rows_cols((steps, steps))
    upto = (s <= t).astype(BF16)
    for copy in copies:
        copy.wait()
    for b in range(local):
        log_gate = jnp.log1p(forget[b] - 1.0)
        high, low = halves(log_gate)
        lowest = (log_gate - high.astype(F32) - low.astype(F32)).astype(BF16)
        sums = quick(jnp.concatenate([high, low, lowest, jnp.zeros_like(low)], axis=0), upto)
        sums = sums[:heads] + sums[heads : 2 * heads] + sums[2 * heads : 3 * heads]
        row_ref[b * heads : (b + 1) * heads] = sums
        wide = jnp.broadcast_to(sums[:, None, :], (heads, patch, steps)).reshape(lanes, steps)
        gx = wide.T
        gx_ref[b] = gx
        fade_ref[b] = jnp.exp(gx[steps - 1 : steps] - gx)


def gram_kernel(heads, patch, count, *refs):
    parts, (gx, fade) = refs[:count], refs[count : count + 2]
    mt_ref, pack_ref = refs[count + 2 :]
    local, steps, lanes = gx.shape
    per = lanes // patch
    t, r = rows_cols((local * steps, local * steps // per))
    spread = (t // per == r).astype(BF16)
    t, lane = rows_cols((local * steps, lanes))
    chosen = t % per == lane // patch
    a, b_ = rows_cols((lanes, lanes))
    fold = (a % patch == b_ % patch).astype(BF16)
    total = parts[0][...]
    for part in parts[1:]:
        total = total + part[...]
    wide = quick(spread, total.reshape(local * steps // per, lanes))
    mt = quick(jnp.where(chosen, wide, 0.0), fold)
    mt_ref[...] = mt.astype(BF16).reshape(mt_ref.shape)
    pack_ref[local * patch :] = jnp.zeros((pack_ref.shape[0] - local * patch, lanes), F32)
    for b in range(local):
        own = mt[b * steps : (b + 1) * steps]
        pack_ref[b * patch : (b + 1) * patch] = quick(own[:, :patch], own * fade[b], ((0,), (0,)))
        pack_ref[local * patch + b : local * patch + b + 1] = gx[b, steps - 1 : steps]


def weight_kernel(heads, per, *refs):
    embed_hbm, qkv_hbm, out_hbm, cot_hbm, _ = refs[:5]
    a_ref, m_ref, c_ref, b_ref, bb_ref, k_ref, v_ref, own_ref, qkv_ref = refs[5:14]
    embed, qkv, w_out, cot, tall, sems = refs[14:]
    copies = fetch((embed_hbm, qkv_hbm, out_hbm, cot_hbm), (embed, qkv, w_out, cot), sems)
    patch, width = embed.shape
    rows_out = qkv_ref.shape[0]
    ctx = lax.axis_index("ctx")
    mine = pl.ds(pl.multiple_of(ctx * rows_out, rows_out), rows_out)
    copies[0].wait()
    tall[:, :patch] = embed[...].astype(F32).T
    copies[1].wait()
    a = quick(embed[...], qkv[...])
    a_ref[...] = a
    qkv_ref[...] = qkv[mine, :]
    mask = block_mask(heads, patch, width // heads)
    query, key, value = [
        jnp.where(mask, stacked(a[:, j * width : (j + 1) * width], heads), 0.0) for j in range(3)
    ]
    across = ((1,), (1,))
    key_high, key_low = halves(key)
    value_high, value_low = halves(value)
    query_high, query_low = halves(query)
    k_ref[...] = jnp.concatenate([key_high, key_high, key_low], axis=0)
    m = quick(query_high, key_high, across) + quick(query_high, key_low, across)
    m = m + quick(query_low, key_high, across)
    m_ref[...] = rebuilt(*halves(m))
    mixed = quick(value_high, value_low, across)
    c = quick(value_high, value_high, across) + mixed + mixed.T
    c_ref[...] = rebuilt(*halves(c))
    v_ref[...] = stacked_heads(a[:, 2 * width :], heads)
    tall[:, patch : 2 * patch] = a[:, 2 * width :].T
    own_ref[...] = tall[mine, :]
    copies[2].wait()
    product = (quick(value_high, w_out[...]) + quick(value_low, w_out[...])).astype(BF16)
    b_ref[...] = product
    copies[3].wait()
    for b in range(cot.shape[0]):
        bb_ref[b] = quick(cot[b], product, across)


def spread_heads(gram, square, heads):
    return jnp.where(square, stacked(gram, heads), 0.0).astype(BF16)


def intra_kernel(heads, mt, gx, sums, m, z_ref, qe_ref, lead_ref, bd_ref, decay_ref, gl_ref, er_ref):
    local, steps, lanes = mt.shape
    patch = lanes // heads
    subs = bd_ref.shape[1]
    sub = steps // subs
    t, s = rows_cols((sub, heads * sub))
    causal = t >= s % sub
    row, col = rows_cols((heads * sub, lanes))
    diagonal = (row // sub == col // patch).astype(BF16)
    for b in range(local):
        query = fine(jnp.concatenate([mt[b], jnp.zeros_like(mt[b])], axis=1), m[...])
        gates = sums[b * heads : (b + 1) * heads]
        wide = jnp.broadcast_to(gates[:, None, :], (heads, sub, steps))
        wide = wide.reshape(heads * sub, steps).T
        for c in range(subs):
            rows = slice(c * sub, (c + 1) * sub)
            g = gx[b, rows]
            if c == 0:
                start = jnp.zeros((1, lanes), F32)
                gl_ref[b, c] = jnp.zeros((patch, lanes), F32)
            else:
                start = gx[b, c * sub - 1 : c * sub]
                past = mt[b, : c * sub]
                fading = past.astype(F32) * jnp.exp(start - gx[b, : c * sub])
                gl_ref[b, c] = quick(past[:, :patch], fading, ((0,), (0,)))
            er_ref[b, c] = jnp.broadcast_to(jnp.exp(start), (8, lanes))
            lead = jnp.exp(g - start)
            lead_ref[b, rows] = lead
            qe_ref[b, rows] = (query[rows] * lead).astype(BF16)
            bd = stacked(mt[b, rows], heads) * diagonal
            bd_ref[b, c] = bd
            across = jnp.concatenate([gates[h : h + 1, rows] for h in range(heads)], axis=1)
            decay = jnp.where(causal, jnp.exp(wide[rows] - across), 0.0)
            decay_ref[b, c] = decay
            scores = quick(query[rows], bd, ((1,), (1,))) * decay
            z_ref[b, rows] = quick(scores, bd)


def level(packs, place, local, patch, wanted):
    radix = len(packs)
    at = [other(place, radix, slot) for slot in range(radix)]
    totals = [pack[local * patch :] for pack in packs]
    zero = jnp.zeros_like(totals[0])
    grams = None
    total = zero
    for m in range(radix):
        if wanted == "before" and m == 0:
            continue
        power = zero
        for k in range(radix):
            if k == m or (wanted == "before" and k == 0):
                continue
            after = at[k] > at[m]
            if wanted == "before":
                after = jnp.logical_and(after, at[k] < place)
            power = power + jnp.where(after, totals[k], 0.0)
        factor = jnp.exp(power)
        if wanted == "before":
            factor = jnp.where(at[m] < place, factor, 0.0)
            total = total + jnp.where(at[m] < place, totals[m], 0.0)
        else:
            total = total + totals[m]
        terms = [factor[b : b + 1] * packs[m][b * patch : (b + 1) * patch] for b in range(local)]
        grams = terms if grams is None else [g + x for g, x in zip(grams, terms)]
    return jnp.concatenate(grams + [total], axis=0)


def joined(near, far, local, patch):
    totals = near[local * patch :]
    factor = jnp.exp(totals)
    grams = [
        near[b * patch : (b + 1) * patch] + factor[b : b + 1] * far[b * patch : (b + 1) * patch]
        for b in range(local)
    ]
    return jnp.concatenate(grams + [totals + far[local * patch :]], axis=0)


def in_slots(packs):
    order = (0,) + ORDERS.get(len(packs), tuple(range(1, len(packs))))
    return [packs[order.index(slot)] for slot in range(len(packs))]


def level_kernel(local, patch, stride, radix, first, *refs):
    place = (lax.axis_index("ctx") // stride) % radix
    packs = in_slots([ref[...] for ref in refs[:radix]])
    before = level(packs, place, local, patch, "before")
    if not first:
        before = joined(refs[radix][...], before, local, patch)
    refs[-2][...] = level(packs, place, local, patch, "whole")
    refs[-1][...] = before


def main_kernel(heads, stride, radix, near_given, mixes, *refs):
    count = radix + int(near_given)
    packs = in_slots([ref[...] for ref in refs[:radix]])
    mt, lead, bd, decay, intra, qe, gl, er, bb, c, big_b, v, w_out, cot = refs[count : count + 14]
    out_hbm, *part_refs = refs[count + 14 : -3]
    z_scr, out_scr, sems = refs[-3:]
    local, steps, lanes = mt.shape
    patch = lanes // heads
    subs = bd.shape[1]
    sub = steps // subs
    width = w_out.shape[0]
    size = width // heads
    place = (lax.axis_index("ctx") // stride) % radix
    state = level(packs, place, local, patch, "before")
    if near_given:
        state = joined(refs[radix][...], state, local, patch)
    square = block_mask(heads, patch, patch)
    ones = jnp.concatenate([square.astype(BF16)] * 2, axis=0)
    places = [(b, i) for b in range(local) for i in range(subs)]
    grams = []
    z = []
    for b, i in places:
        gram = gl[b, i] + er[b, i, :1] * state[b * patch : (b + 1) * patch]
        grams.append(spread_heads(gram, square, heads))
        rows = slice(i * sub, (i + 1) * sub)
        z.append(intra[b, rows] + quick(qe[b, rows], grams[-1]))
    z = jnp.concatenate(z, axis=0)
    every = (local * steps, lanes)
    around = bb[...].reshape(every)
    zc = fine(pair(z), c[...])
    irms = lax.rsqrt(summed(z * zc, ones) * (1.0 / size) + EPS)
    zn = z * irms
    znb = zn.astype(BF16)
    out_scr[...] = quick(znb, big_b[...]).astype(BF16).reshape(out_scr.shape)
    leaving = fetch((out_scr,), (out_hbm,), sems)
    aligned = summed(zn * around, ones) * (1.0 / size)
    u = irms * (around - aligned * (irms * zc))
    ub = u.astype(BF16)
    ue = (u * lead[...].reshape(every)).astype(BF16)
    y = []
    for (b, i), gram in zip(places, grams):
        rows = slice(b * steps + i * sub, b * steps + (i + 1) * sub)
        scores = (quick(ub[rows], bd[b, i], ((1,), (1,))) * decay[b, i]).astype(BF16)
        left = jnp.concatenate([scores, ue[rows]], axis=1)
        y.append(quick(left, jnp.concatenate([bd[b, i], gram], axis=0)))
    y = jnp.concatenate(y, axis=0)
    given = cot[...].reshape(local * steps, width)
    x_total = quick(mt[...].reshape(every)[:, :patch], y, ((0,), (0,)))
    right = jnp.concatenate([given, (aligned * zn).astype(BF16)], axis=1)
    zw_total = quick(znb, right, ((0,), (0,)))
    big_z = zw_total[:, :width]
    w_total = jnp.where(square, zw_total[:, width:], 0.0)
    y_total = -fine(pair(w_total), rebuilt(*halves(v[...])))
    y_rows = []
    for h in range(heads):
        rows = slice(h * patch, (h + 1) * patch)
        both = jnp.concatenate(halves(big_z[rows]), axis=0)
        found = quick(both, w_out[h * size : (h + 1) * size], ((1,), (1,)))
        y_rows.append(y_total[rows] + found[:patch] + found[patch:])
    y_total = jnp.concatenate(y_rows, axis=0)
    per = lax.axis_size("ctx") // heads
    head = lax.axis_index("ctx") // per
    me = lax.axis_index("mix")
    panels = width // 128
    share = panels // mixes
    for k in range(panels):
        z_scr[k] = big_z[:, k * 128 : (k + 1) * 128]
    y_high = lanes // mixes
    x_high = patch // mixes
    z_scr[panels] = y_total
    z_scr[panels + 1, :patch] = x_total
    for slot in range(mixes):
        part = other(me, mixes, slot)
        out = part_refs[slot]
        at = 0
        for q in range(heads):
            for k in range(share):
                rows = pl.ds(other(head, heads, q) * patch, patch)
                out[at : at + patch] = z_scr[part * share + k, rows, :]
                at += patch
        out[at : at + y_high] = z_scr[panels, pl.ds(part * y_high, y_high), :]
        at += y_high
        out[at : at + x_high] = z_scr[panels + 1, pl.ds(part * x_high, x_high), :]
    for copy in leaving:
        copy.wait()


def stacked_heads(array, heads):
    size = array.shape[1] // heads
    return jnp.concatenate([array[:, h * size : (h + 1) * size] for h in range(heads)], axis=0)


def final_kernel(heads, mixes, *refs):
    parts = refs[:mixes]
    a, keys, own, qkv_rows = refs[mixes : mixes + 4]
    gq_ref, go_ref, ge_ref, scr = refs[mixes + 4 :]
    patch = ge_ref.shape[1]
    width = go_ref.shape[1]
    size = width // heads
    lanes = heads * patch
    panels = width // 128
    share = panels // mixes
    y_high = lanes // mixes
    x_high = patch // mixes
    me = lax.axis_index("mix")
    for slot in range(mixes):
        part = other(me, mixes, slot)
        at = 0
        for k in range(share):
            scr[part * share + k, :patch] = parts[slot][at : at + patch]
            at += patch
        scr[panels, pl.ds(part * y_high, y_high), :] = parts[slot][at : at + y_high]
        at += y_high
        scr[panels + 1, pl.ds(part * x_high, x_high), :] = parts[slot][at : at + x_high]
    y = scr[panels]
    x_high, x_low = halves(scr[panels + 1, :patch])
    t_query = quick(jnp.concatenate([x_high, x_low, x_high], axis=1), keys[...])
    query_high, query_low = halves(a[:, :width])
    crossed = quick(
        jnp.concatenate([x_high, x_low, x_high], axis=0),
        jnp.concatenate([query_high, query_high, query_low], axis=0),
        ((0,), (0,)),
    )
    t_key = [crossed[h * patch : (h + 1) * patch, h * size : (h + 1) * size] for h in range(heads)]
    t_value = [y[h * patch : (h + 1) * patch] for h in range(heads)]
    t = jnp.concatenate([t_query] + t_key + t_value, axis=1)
    high, low = halves(t)
    both = jnp.concatenate([high, low], axis=0)
    embed_rows = own[:, :patch].astype(BF16)
    gq_ref[...] = quick(jnp.concatenate([embed_rows, embed_rows], axis=1), both)
    found = quick(qkv_rows[...], both, ((1,), (1,)))
    ge_ref[...] = found[:, :patch] + found[:, patch:]
    v_high, v_low = halves(own[:, patch : 2 * patch])
    z_high, z_low = halves(jnp.concatenate([scr[k, :patch] for k in range(panels)], axis=1))
    go_ref[...] = quick(
        jnp.concatenate([v_high, v_low, v_high], axis=1),
        jnp.concatenate([z_high, z_high, z_low], axis=0),
    )


def slot_kernel(heads, z_high, *refs):
    parts, slots = refs[:-heads], refs[-heads:]
    total = parts[0][...]
    for part in parts[1:]:
        total = total + part[...]
    for q in range(heads):
        slots[q][:z_high] = total[q * z_high : (q + 1) * z_high]
        slots[q][z_high:] = total[heads * z_high :]


def add_kernel(*refs):
    total = refs[0][...]
    for ref in refs[1:-1]:
        total = total + ref[...]
    refs[-1][...] = total


def added(arrays):
    (total,) = call(add_kernel, [(arrays[0].shape, F32)], arrays)
    return total


def shards(
    sources, source_ids, mix_weights, source_lengths, w_embed, w_qkv, w_out, forget, cotangent
):
    mixes = lax.axis_size("mix")
    count = lax.axis_size("ctx")
    patch = w_embed.shape[1]
    local, heads, steps = forget.shape
    width = w_out.shape[0]
    size = width // heads
    lanes = heads * patch
    held = sources.shape[0]
    rows_out = width // count
    per = count // heads
    dma = pltpu.SemaphoreType.DMA
    partial_shape = (local, steps * patch // lanes, lanes)
    partials = call(
        functools.partial(mix_kernel, local, patch, mixes),
        [(partial_shape, F32)] * mixes,
        [source_ids, mix_weights, source_lengths, sources],
        hbm=(0, 1, 2, 3),
        scratch=[
            pltpu.SMEM(source_ids.shape, jnp.int32),
            pltpu.SMEM(mix_weights.shape, F32),
            pltpu.SMEM(source_lengths.shape, jnp.int32),
            pltpu.VMEM(sources.shape, F32),
            pltpu.VMEM((held,) + partial_shape[1:], F32),
            dma((4,)),
        ],
    )
    got = [partials[0]] + [swap(partials[s], "mix", 1, mixes, s) for s in range(1, mixes)]
    subs = heads
    sub = steps // subs
    gx, fade, sums = call(
        functools.partial(gate_kernel, patch),
        [((local, steps, lanes), F32), ((local, steps, lanes), F32), ((local * heads, steps), F32)],
        [forget],
        hbm=(0,),
        flops=10**8,
        scratch=[pltpu.VMEM(forget.shape, F32), dma((1,))],
    )
    high = -(-local // 8) * 8
    pack_shape = ((local * patch + high, lanes), F32)
    mt, pack = call(
        functools.partial(gram_kernel, heads, patch, mixes),
        [((local, steps, lanes), BF16), pack_shape],
        got + [gx, fade],
    )
    a, m, c, big_b, bb, keys, v, own, qkv_rows = call(
        functools.partial(weight_kernel, heads, per),
        [
            ((patch, 3 * width), F32),
            ((2 * lanes, 2 * lanes), BF16),
            ((2 * lanes, 2 * lanes), BF16),
            ((lanes, width), BF16),
            ((local, steps, lanes), F32),
            ((3 * lanes, width), BF16),
            ((lanes, size), F32),
            ((rows_out, 2 * patch), F32),
            ((rows_out, 3 * width), BF16),
        ],
        [w_embed.T, w_qkv, w_out, cotangent, pack],
        hbm=(0, 1, 2, 3),
        flops=10**9,
        scratch=[
            pltpu.VMEM((patch, width), BF16),
            pltpu.VMEM(w_qkv.shape, BF16),
            pltpu.VMEM(w_out.shape, BF16),
            pltpu.VMEM(cotangent.shape, BF16),
            pltpu.VMEM((width, 2 * patch), F32),
            dma((4,)),
        ],
    )
    intra, qe, lead, bd, decay, gl, er = call(
        functools.partial(intra_kernel, heads),
        [
            ((local, steps, lanes), F32),
            ((local, steps, lanes), BF16),
            ((local, steps, lanes), F32),
            ((local, subs, heads * sub, lanes), BF16),
            ((local, subs, sub, heads * sub), F32),
            ((local, subs, patch, lanes), F32),
            ((local, subs, 8, lanes), F32),
        ],
        [mt, gx, sums, m],
        flops=10**9,
    )
    steps_up = radices(count)
    stride = 1
    near = []
    for i, radix in enumerate(steps_up):
        order = ORDERS.get(radix, tuple(range(1, radix)))
        packs = [pack] + [swap(pack, "ctx", stride, radix, s) for s in order]
        if i == len(steps_up) - 1:
            break
        pack, before = call(
            functools.partial(level_kernel, local, patch, stride, radix, i == 0),
            [pack_shape] * 2,
            packs + near,
        )
        near = [before]
        stride *= radix
    part_rows = heads * (width // 128 // mixes) * patch + lanes // mixes + patch // mixes
    output, *parts = call(
        functools.partial(main_kernel, heads, stride, radix, bool(near), mixes),
        [((local, steps, width), BF16)] + [((part_rows, 128), F32)] * mixes,
        packs + near + [mt, lead, bd, decay, intra, qe, gl, er, bb, c, big_b, v, w_out, cotangent],
        flops=10**9,
        out_hbm=(0,),
        scratch=[
            pltpu.VMEM((width // 128 + 2, lanes, 128), F32),
            pltpu.VMEM((local, steps, width), BF16),
            dma((1,)),
        ],
    )
    z_high = (width // 128 // mixes) * patch
    y_high = part_rows - heads * z_high
    slots = call(
        functools.partial(slot_kernel, heads, z_high),
        [((z_high + y_high, 128), F32)] * heads,
        [parts[0]] + [swap(parts[s], "mix", 1, mixes, s) for s in range(1, mixes)],
    )
    order = ORDERS.get(heads, tuple(range(1, heads)))
    both = added([slots[0]] + [swap(slots[s], "ctx", per, heads, s) for s in order])
    stride = 1
    for radix in radices(per):
        order = ORDERS.get(radix, tuple(range(1, radix)))
        both = added([both] + [swap(both, "ctx", stride, radix, s) for s in order])
        stride *= radix
    pieces = [both] + [swap(both, "mix", 1, mixes, s) for s in range(1, mixes)]
    grads = call(
        functools.partial(final_kernel, heads, mixes),
        [((rows_out, 3 * width), F32), ((rows_out, width), F32), ((rows_out, patch), F32)],
        pieces + [a, keys, own, qkv_rows],
        scratch=[pltpu.VMEM((width // 128 + 2, lanes, 128), F32)],
    )
    return output, grads[0], grads[1], grads[2]


def solution(mesh):
    placed = (
        P("mix", "ctx"),
        P(),
        P(),
        P(),
        P(),
        P(),
        P(),
        P("mix", None, "ctx"),
        P("mix", "ctx", None),
    )
    return jax.shard_map(
        shards,
        mesh=mesh,
        in_specs=placed,
        out_specs=(P("mix", "ctx", None), P("ctx", None), P("ctx", None), P("ctx", None)),
        check_vma=False,
    )
```

```python
import functools

import jax
import jax.numpy as jnp
from jax import lax
from jax.experimental import pallas as pl
from jax.experimental.pallas import tpu as pltpu
from jax.sharding import PartitionSpec as P

EPS = 1e-06
F32 = jnp.float32
BF16 = jnp.bfloat16
LEVEL_ORDERS = ((1, 2, 3), (1, 2, 3))
HEAD_ORDER = (1, 2, 3)
GROUP_ORDER = (1, 2, 3)
VMEM_LIMIT = 24 * 2**20


def quick(left, right, dims=((1,), (0,))):
    return lax.dot_general(
        left.astype(BF16), right.astype(BF16), (dims, ((), ())), preferred_element_type=F32
    )


def halves(array):
    high = array.astype(BF16)
    return high, (array - high.astype(F32)).astype(BF16)


def rows_cols(shape):
    return lax.broadcasted_iota(jnp.int32, shape, 0), lax.broadcasted_iota(jnp.int32, shape, 1)


def block_mask(heads, high, wide):
    row, col = rows_cols((heads * high, heads * wide))
    return (row // high) == (col // wide)


def stacked(array, heads):
    return jnp.concatenate([array] * heads, axis=0)


def radices(count):
    found = []
    while count > 1:
        radix = 4 if count % 4 == 0 else 2 if count % 2 == 0 else count
        found.append(radix)
        count //= radix
    return found


def other(place, radix, slot):
    if radix & (radix - 1) == 0:
        return place ^ slot
    return (place + slot) % radix


def swap(array, axis, stride, radix, slot):
    pairs = []
    for source in range(lax.axis_size(axis)):
        place = (source // stride) % radix
        for target in range(radix):
            if other(target, radix, slot) == place:
                pairs.append((source, source + (target - place) * stride))
    return lax.ppermute(array, axis, pairs)


def call(kernel, outs, ins, hbm=(), out_hbm=(), flops=0, scratch=()):
    specs = [
        pl.BlockSpec(memory_space=pltpu.HBM if i in hbm else pltpu.VMEM) for i in range(len(ins))
    ]
    ins = [
        pltpu.with_memory_space_constraint(x, pltpu.HBM) if i in hbm else x
        for i, x in enumerate(ins)
    ]
    return pl.pallas_call(
        kernel,
        out_shape=[jax.ShapeDtypeStruct(s, d) for s, d in outs],
        in_specs=specs,
        out_specs=[
            pl.BlockSpec(memory_space=pl.ANY if i in out_hbm else pltpu.VMEM)
            for i in range(len(outs))
        ],
        scratch_shapes=list(scratch),
        compiler_params=pltpu.CompilerParams(vmem_limit_bytes=VMEM_LIMIT),
        cost_estimate=pl.CostEstimate(flops=flops, bytes_accessed=1 << 20, transcendentals=0),
    )(*ins)


def rebuilt(high, low):
    top = jnp.concatenate([high, low], axis=1)
    bottom = jnp.concatenate([high, jnp.zeros_like(low)], axis=1)
    return jnp.concatenate([top, bottom], axis=0)


def pair(array):
    return jnp.concatenate(halves(array), axis=1)


def fine(left, right):
    both = quick(left, right)
    half = both.shape[1] // 2
    return both[:, :half] + both[:, half:]


def summed(array, ones):
    return quick(pair(array), ones)


def fetch(sources, targets, sems):
    copies = [
        pltpu.make_async_copy(source, target, sems.at[i])
        for i, (source, target) in enumerate(zip(sources, targets))
    ]
    for copy in copies:
        copy.start()
    return copies


def mix_kernel(held, local, patch, mixes, ids_hbm, weights_hbm, lengths_hbm, src_hbm, *rest):
    outs, (ids, weights, lengths, src, sems) = rest[:mixes], rest[mixes:]
    copies = fetch((src_hbm, ids_hbm, weights_hbm, lengths_hbm), (src, ids, weights, lengths), sems)
    me = lax.axis_index("mix")
    _, high, lanes = outs[0].shape
    first = lax.axis_index("ctx") * (high * lanes // patch)
    row, col = rows_cols((high, lanes))
    position = first + row * (lanes // patch) + col // patch
    for copy in copies:
        copy.wait()
    for slot in range(mixes):
        target = other(me, mixes, slot)
        for b in range(local):
            total = jnp.zeros((high, lanes), F32)
            for term in range(ids.shape[1]):
                mixture = target * local + b
                at = ids[mixture, term] - me * held
                here = jnp.logical_and(at >= 0, at < held)
                factor = jnp.where(here, weights[mixture, term], 0.0)
                rows = src[pl.ds(jnp.where(here, at, 0), high, held), :]
                total += jnp.where(position < lengths[mixture, term], factor, 0.0) * rows
            outs[slot][b] = total


def gate_kernel(patch, forget_hbm, gx_ref, fade_ref, row_ref, forget, sems):
    copies = fetch((forget_hbm,), (forget,), sems)
    local, heads, steps = forget.shape
    lanes = heads * patch
    s, t = rows_cols((steps, steps))
    upto = (s <= t).astype(BF16)
    for copy in copies:
        copy.wait()
    for b in range(local):
        log_gate = jnp.log1p(forget[b] - 1.0)
        high, low = halves(log_gate)
        lowest = (log_gate - high.astype(F32) - low.astype(F32)).astype(BF16)
        sums = quick(jnp.concatenate([high, low, lowest, jnp.zeros_like(low)], axis=0), upto)
        sums = sums[:heads] + sums[heads : 2 * heads] + sums[2 * heads : 3 * heads]
        row_ref[b * heads : (b + 1) * heads] = sums
        wide = jnp.broadcast_to(sums[:, None, :], (heads, patch, steps)).reshape(lanes, steps)
        gx = wide.T
        gx_ref[b] = gx
        fade_ref[b] = jnp.exp(gx[steps - 1 : steps] - gx)


def gram_kernel(heads, patch, count, *refs):
    parts, (gx, fade) = refs[:count], refs[count : count + 2]
    mt_ref, pack_ref = refs[count + 2 :]
    local, steps, lanes = gx.shape
    per = lanes // patch
    t, r = rows_cols((local * steps, local * steps // per))
    spread = (t // per == r).astype(BF16)
    t, lane = rows_cols((local * steps, lanes))
    chosen = t % per == lane // patch
    a, b_ = rows_cols((lanes, lanes))
    fold = (a % patch == b_ % patch).astype(BF16)
    total = parts[0][...]
    for part in parts[1:]:
        total = total + part[...]
    wide = quick(spread, total.reshape(local * steps // per, lanes))
    mt = quick(jnp.where(chosen, wide, 0.0), fold)
    mt_ref[...] = mt.astype(BF16).reshape(mt_ref.shape)
    pack_ref[local * patch :] = jnp.zeros((pack_ref.shape[0] - local * patch, lanes), F32)
    for b in range(local):
        own = mt[b * steps : (b + 1) * steps]
        pack_ref[b * patch : (b + 1) * patch] = quick(own[:, :patch], own * fade[b], ((0,), (0,)))
        pack_ref[local * patch + b : local * patch + b + 1] = gx[b, steps - 1 : steps]


def weight_kernel(heads, *refs):
    embed_hbm, qkv_hbm, _ = refs[:3]
    a_ref, m_ref, c_ref, k_ref, v_ref, vb_ref, own_ref, qkv_ref = refs[3:11]
    embed, qkv, tall, sems = refs[11:]
    copies = fetch((embed_hbm, qkv_hbm), (embed, qkv), sems)
    patch, width = embed.shape
    rows_out = qkv_ref.shape[0]
    ctx = lax.axis_index("ctx")
    mine = pl.ds(pl.multiple_of(ctx * rows_out, rows_out), rows_out)
    copies[0].wait()
    tall[:, :patch] = embed[...].astype(F32).T
    copies[1].wait()
    a = quick(embed[...], qkv[...])
    a_ref[...] = a
    qkv_ref[...] = qkv[mine, :]
    mask = block_mask(heads, patch, width // heads)
    query, key, value = [
        jnp.where(mask, stacked(a[:, j * width : (j + 1) * width], heads), 0.0) for j in range(3)
    ]
    across = ((1,), (1,))
    key_high, key_low = halves(key)
    value_high, value_low = halves(value)
    query_high, query_low = halves(query)
    k_ref[...] = jnp.concatenate([key_high, key_high, key_low], axis=0)
    m = quick(query_high, key_high, across) + quick(query_high, key_low, across)
    m = m + quick(query_low, key_high, across)
    m_ref[...] = rebuilt(*halves(m))
    mixed = quick(value_high, value_low, across)
    c = quick(value_high, value_high, across) + mixed + mixed.T
    c_ref[...] = rebuilt(*halves(c))
    v_ref[...] = rebuilt(*halves(stacked_heads(a[:, 2 * width :], heads)))
    vb_ref[...] = jnp.concatenate([value_high, value_low], axis=1)
    tall[:, patch : 2 * patch] = a[:, 2 * width :].T
    own_ref[...] = tall[mine, :]


def out_kernel(out_hbm, cot_hbm, vb, _, b_ref, bb_ref, out_ref, cot_ref, sems):
    copies = fetch((out_hbm, cot_hbm), (out_ref, cot_ref), sems)
    copies[0].wait()
    product = quick(vb[...], jnp.concatenate([out_ref[...], out_ref[...]], axis=0)).astype(BF16)
    b_ref[...] = product
    copies[1].wait()
    given = cot_ref[...].reshape(bb_ref.shape[0] * bb_ref.shape[1], -1)
    bb_ref[...] = quick(given, product, ((1,), (1,))).reshape(bb_ref.shape)


def spread_heads(gram, square, heads):
    return jnp.where(square, stacked(gram, heads), 0.0).astype(BF16)


def intra_kernel(heads, mt, gx, sums, m, _, z_ref, qe_ref, lead_ref, bd_ref, decay_ref, gl_ref, er_ref):
    local, steps, lanes = mt.shape
    patch = lanes // heads
    subs = bd_ref.shape[1]
    sub = steps // subs
    t, s = rows_cols((sub, heads * sub))
    causal = t >= s % sub
    row, col = rows_cols((heads * sub, lanes))
    diagonal = (row // sub == col // patch).astype(BF16)
    for b in range(local):
        query = fine(jnp.concatenate([mt[b], jnp.zeros_like(mt[b])], axis=1), m[...])
        gates = sums[b * heads : (b + 1) * heads]
        wide = jnp.broadcast_to(gates[:, None, :], (heads, sub, steps))
        wide = wide.reshape(heads * sub, steps).T
        for c in range(subs):
            rows = slice(c * sub, (c + 1) * sub)
            g = gx[b, rows]
            if c == 0:
                start = jnp.zeros((1, lanes), F32)
                gl_ref[b, c] = jnp.zeros((patch, lanes), F32)
            else:
                start = gx[b, c * sub - 1 : c * sub]
                past = mt[b, : c * sub]
                fading = past.astype(F32) * jnp.exp(start - gx[b, : c * sub])
                gl_ref[b, c] = quick(past[:, :patch], fading, ((0,), (0,)))
            er_ref[b, c] = jnp.broadcast_to(jnp.exp(start), (8, lanes))
            lead = jnp.exp(g - start)
            lead_ref[b, rows] = lead
            qe_ref[b, rows] = (query[rows] * lead).astype(BF16)
            bd = stacked(mt[b, rows], heads) * diagonal
            bd_ref[b, c] = bd
            across = jnp.concatenate([gates[h : h + 1, rows] for h in range(heads)], axis=1)
            decay = jnp.where(causal, jnp.exp(wide[rows] - across), 0.0)
            decay_ref[b, c] = decay
            scores = quick(query[rows], bd, ((1,), (1,))) * decay
            z_ref[b, rows] = quick(scores, bd)


def level(packs, place, local, patch, wanted):
    radix = len(packs)
    at = [other(place, radix, slot) for slot in range(radix)]
    totals = [pack[local * patch :] for pack in packs]
    zero = jnp.zeros_like(totals[0])
    grams = None
    total = zero
    for m in range(radix):
        if wanted == "before" and m == 0:
            continue
        power = zero
        for k in range(radix):
            if k == m or (wanted == "before" and k == 0):
                continue
            after = at[k] > at[m]
            if wanted == "before":
                after = jnp.logical_and(after, at[k] < place)
            power = power + jnp.where(after, totals[k], 0.0)
        factor = jnp.exp(power)
        if wanted == "before":
            factor = jnp.where(at[m] < place, factor, 0.0)
            total = total + jnp.where(at[m] < place, totals[m], 0.0)
        else:
            total = total + totals[m]
        terms = [factor[b : b + 1] * packs[m][b * patch : (b + 1) * patch] for b in range(local)]
        grams = terms if grams is None else [g + x for g, x in zip(grams, terms)]
    return jnp.concatenate(grams + [total], axis=0)


def joined(near, far, local, patch):
    totals = near[local * patch :]
    factor = jnp.exp(totals)
    grams = [
        near[b * patch : (b + 1) * patch] + factor[b : b + 1] * far[b * patch : (b + 1) * patch]
        for b in range(local)
    ]
    return jnp.concatenate(grams + [totals + far[local * patch :]], axis=0)


def ordered(radix, order):
    return order if radix == 4 else tuple(range(1, radix))


def level_order(number, radix):
    return ordered(radix, LEVEL_ORDERS[min(number, len(LEVEL_ORDERS) - 1)])


def in_slots(packs, number):
    order = (0,) + level_order(number, len(packs))
    return [packs[order.index(slot)] for slot in range(len(packs))]


def level_kernel(local, patch, stride, radix, number, *refs):
    place = (lax.axis_index("ctx") // stride) % radix
    packs = in_slots([ref[...] for ref in refs[:radix]], number)
    before = level(packs, place, local, patch, "before")
    if number > 0:
        before = joined(refs[radix][...], before, local, patch)
    refs[-2][...] = level(packs, place, local, patch, "whole")
    refs[-1][...] = before


def main_kernel(heads, stride, radix, number, mixes, *refs):
    count = radix + int(number > 0)
    packs = in_slots([ref[...] for ref in refs[:radix]], number)
    mt, lead, bd, decay, intra, qe, gl, er, bb, c, big_b, v, w_out, cot = refs[count : count + 14]
    out_hbm, *part_refs = refs[count + 14 : -3]
    z_scr, out_scr, sems = refs[-3:]
    local, steps, lanes = mt.shape
    patch = lanes // heads
    subs = bd.shape[1]
    sub = steps // subs
    width = w_out.shape[0]
    size = width // heads
    place = (lax.axis_index("ctx") // stride) % radix
    state = level(packs, place, local, patch, "before")
    if number > 0:
        state = joined(refs[radix][...], state, local, patch)
    square = block_mask(heads, patch, patch)
    ones = jnp.concatenate([square.astype(BF16)] * 2, axis=0)
    places = [(b, i) for b in range(local) for i in range(subs)]
    grams = []
    z = []
    for b, i in places:
        gram = gl[b, i] + er[b, i, :1] * state[b * patch : (b + 1) * patch]
        grams.append(spread_heads(gram, square, heads))
        rows = slice(i * sub, (i + 1) * sub)
        z.append(intra[b, rows] + quick(qe[b, rows], grams[-1]))
    z = jnp.concatenate(z, axis=0)
    every = (local * steps, lanes)
    around = bb[...].reshape(every)
    met = summed(z * around, ones)
    zc = fine(pair(z), c[...])
    irms = lax.rsqrt(summed(z * zc, ones) * (1.0 / size) + EPS)
    zn = z * irms
    znb = zn.astype(BF16)
    out_scr[...] = quick(znb, big_b[...]).astype(BF16).reshape(out_scr.shape)
    leaving = fetch((out_scr,), (out_hbm,), sems)
    aligned = met * (irms * (1.0 / size))
    u = irms * (around - aligned * (irms * zc))
    ub = u.astype(BF16)
    ue = (u * lead[...].reshape(every)).astype(BF16)
    y = []
    for (b, i), gram in zip(places, grams):
        rows = slice(b * steps + i * sub, b * steps + (i + 1) * sub)
        scores = (quick(ub[rows], bd[b, i], ((1,), (1,))) * decay[b, i]).astype(BF16)
        left = jnp.concatenate([scores, ue[rows]], axis=1)
        y.append(quick(left, jnp.concatenate([bd[b, i], gram], axis=0)))
    y = jnp.concatenate(y, axis=0)
    given = cot[...].reshape(local * steps, width)
    x_total = quick(mt[...].reshape(every)[:, :patch], y, ((0,), (0,)))
    right = jnp.concatenate([given, (aligned * zn).astype(BF16)], axis=1)
    zw_total = quick(znb, right, ((0,), (0,)))
    big_z = zw_total[:, :width]
    w_total = jnp.where(square, zw_total[:, width:], 0.0)
    y_total = -fine(pair(w_total), v[...])
    y_rows = []
    for h in range(heads):
        rows = slice(h * patch, (h + 1) * patch)
        both = jnp.concatenate(halves(big_z[rows]), axis=0)
        found = quick(both, w_out[h * size : (h + 1) * size], ((1,), (1,)))
        y_rows.append(y_total[rows] + found[:patch] + found[patch:])
    y_total = jnp.concatenate(y_rows, axis=0)
    per = lax.axis_size("ctx") // heads
    head = lax.axis_index("ctx") // per
    me = lax.axis_index("mix")
    panels = width // 128
    share = panels // mixes
    for k in range(panels):
        z_scr[k] = big_z[:, k * 128 : (k + 1) * 128]
    y_high = lanes // mixes
    x_high = patch // mixes
    z_scr[panels] = y_total
    z_scr[panels + 1, :patch] = x_total
    for slot in range(mixes):
        part = other(me, mixes, slot)
        out = part_refs[slot]
        at = 0
        for q in range(heads):
            for k in range(share):
                rows = pl.ds(other(head, heads, q) * patch, patch)
                out[at : at + patch] = z_scr[part * share + k, rows, :]
                at += patch
        out[at : at + y_high] = z_scr[panels, pl.ds(part * y_high, y_high), :]
        at += y_high
        out[at : at + x_high] = z_scr[panels + 1, pl.ds(part * x_high, x_high), :]
    for copy in leaving:
        copy.wait()


def stacked_heads(array, heads):
    size = array.shape[1] // heads
    return jnp.concatenate([array[:, h * size : (h + 1) * size] for h in range(heads)], axis=0)


def final_kernel(heads, mixes, *refs):
    parts = refs[:mixes]
    a, keys, own, qkv_rows = refs[mixes : mixes + 4]
    gq_ref, go_ref, ge_ref, scr = refs[mixes + 4 :]
    patch = ge_ref.shape[1]
    width = go_ref.shape[1]
    size = width // heads
    lanes = heads * patch
    panels = width // 128
    share = panels // mixes
    y_high = lanes // mixes
    x_high = patch // mixes
    me = lax.axis_index("mix")
    for slot in range(mixes):
        part = other(me, mixes, slot)
        at = 0
        for k in range(share):
            scr[part * share + k, :patch] = parts[slot][at : at + patch]
            at += patch
        scr[panels, pl.ds(part * y_high, y_high), :] = parts[slot][at : at + y_high]
        at += y_high
        scr[panels + 1, pl.ds(part * x_high, x_high), :] = parts[slot][at : at + x_high]
    y = scr[panels]
    x_high, x_low = halves(scr[panels + 1, :patch])
    t_query = quick(jnp.concatenate([x_high, x_low, x_high], axis=1), keys[...])
    query_high, query_low = halves(a[:, :width])
    crossed = quick(
        jnp.concatenate([x_high, x_low, x_high], axis=0),
        jnp.concatenate([query_high, query_high, query_low], axis=0),
        ((0,), (0,)),
    )
    t_key = [crossed[h * patch : (h + 1) * patch, h * size : (h + 1) * size] for h in range(heads)]
    t_value = [y[h * patch : (h + 1) * patch] for h in range(heads)]
    t = jnp.concatenate([t_query] + t_key + t_value, axis=1)
    high, low = halves(t)
    both = jnp.concatenate([high, low], axis=0)
    embed_rows = own[:, :patch].astype(BF16)
    gq_ref[...] = quick(jnp.concatenate([embed_rows, embed_rows], axis=1), both)
    found = quick(qkv_rows[...], both, ((1,), (1,)))
    ge_ref[...] = found[:, :patch] + found[:, patch:]
    v_high, v_low = halves(own[:, patch : 2 * patch])
    z_high, z_low = halves(jnp.concatenate([scr[k, :patch] for k in range(panels)], axis=1))
    go_ref[...] = quick(
        jnp.concatenate([v_high, v_low, v_high], axis=1),
        jnp.concatenate([z_high, z_high, z_low], axis=0),
    )


def slot_kernel(heads, z_high, *refs):
    parts, slots = refs[:-heads], refs[-heads:]
    total = parts[0][...]
    for part in parts[1:]:
        total = total + part[...]
    for q in range(heads):
        slots[q][:z_high] = total[q * z_high : (q + 1) * z_high]
        slots[q][z_high:] = total[heads * z_high :]


def add_kernel(*refs):
    total = refs[0][...]
    for ref in refs[1:-1]:
        total = total + ref[...]
    refs[-1][...] = total


def added(arrays):
    (total,) = call(add_kernel, [(arrays[0].shape, F32)], arrays)
    return total


def shards(
    sources, source_ids, mix_weights, source_lengths, w_embed, w_qkv, w_out, forget, cotangent
):
    mixes = lax.axis_size("mix")
    count = lax.axis_size("ctx")
    patch = w_embed.shape[1]
    local, heads, steps = forget.shape
    width = w_out.shape[0]
    size = width // heads
    lanes = heads * patch
    held = sources.shape[0]
    rows_out = width // count
    per = count // heads
    dma = pltpu.SemaphoreType.DMA
    partial_shape = (local, steps * patch // lanes, lanes)
    panels = sources.reshape((held,) + partial_shape[1:]).transpose(1, 0, 2).reshape(-1, lanes)
    partials = call(
        functools.partial(mix_kernel, held, local, patch, mixes),
        [(partial_shape, F32)] * mixes,
        [source_ids, mix_weights, source_lengths, panels],
        hbm=(0, 1, 2, 3),
        scratch=[
            pltpu.SMEM(source_ids.shape, jnp.int32),
            pltpu.SMEM(mix_weights.shape, F32),
            pltpu.SMEM(source_lengths.shape, jnp.int32),
            pltpu.VMEM(panels.shape, F32),
            dma((4,)),
        ],
    )
    got = [partials[0]] + [swap(partials[s], "mix", 1, mixes, s) for s in range(1, mixes)]
    subs = heads
    sub = steps // subs
    gx, fade, sums = call(
        functools.partial(gate_kernel, patch),
        [((local, steps, lanes), F32), ((local, steps, lanes), F32), ((local * heads, steps), F32)],
        [forget],
        hbm=(0,),
        flops=10**8,
        scratch=[pltpu.VMEM(forget.shape, F32), dma((1,))],
    )
    high = -(-local // 8) * 8
    pack_shape = ((local * patch + high, lanes), F32)
    mt, pack = call(
        functools.partial(gram_kernel, heads, patch, mixes),
        [((local, steps, lanes), BF16), pack_shape],
        got + [gx, fade],
    )
    a, m, c, keys, v, value_blocks, own, qkv_rows = call(
        functools.partial(weight_kernel, heads),
        [
            ((patch, 3 * width), F32),
            ((2 * lanes, 2 * lanes), BF16),
            ((2 * lanes, 2 * lanes), BF16),
            ((3 * lanes, width), BF16),
            ((2 * lanes, 2 * size), BF16),
            ((lanes, 2 * width), BF16),
            ((rows_out, 2 * patch), F32),
            ((rows_out, 3 * width), BF16),
        ],
        [w_embed.T, w_qkv, pack],
        hbm=(0, 1),
        flops=10**9,
        scratch=[
            pltpu.VMEM((patch, width), BF16),
            pltpu.VMEM(w_qkv.shape, BF16),
            pltpu.VMEM((width, 2 * patch), F32),
            dma((2,)),
        ],
    )
    steps_up = radices(count)
    stride = 1
    near = []
    for i, radix in enumerate(steps_up):
        order = level_order(i, radix)
        packs = [pack] + [swap(pack, "ctx", stride, radix, s) for s in order]
        if i == len(steps_up) - 1:
            break
        pack, before = call(
            functools.partial(level_kernel, local, patch, stride, radix, i),
            [pack_shape] * 2,
            packs + near,
        )
        near = [before]
        stride *= radix
    intra, qe, lead, bd, decay, gl, er = call(
        functools.partial(intra_kernel, heads),
        [
            ((local, steps, lanes), F32),
            ((local, steps, lanes), BF16),
            ((local, steps, lanes), F32),
            ((local, subs, heads * sub, lanes), BF16),
            ((local, subs, sub, heads * sub), F32),
            ((local, subs, patch, lanes), F32),
            ((local, subs, 8, lanes), F32),
        ],
        [mt, gx, sums, m, pack],
        flops=10**9,
    )
    big_b, bb, w_out_near, cot_near = call(
        out_kernel,
        [
            ((lanes, width), BF16),
            ((local, steps, lanes), F32),
            (w_out.shape, BF16),
            (cotangent.shape, BF16),
        ],
        [w_out, cotangent, value_blocks, pack],
        hbm=(0, 1),
        flops=10**9,
        scratch=[dma((2,))],
    )
    part_rows = heads * (width // 128 // mixes) * patch + lanes // mixes + patch // mixes
    output, *parts = call(
        functools.partial(main_kernel, heads, stride, radix, i, mixes),
        [((local, steps, width), BF16)] + [((part_rows, 128), F32)] * mixes,
        packs + near + [mt, lead, bd, decay, intra, qe, gl, er, bb, c, big_b, v, w_out_near, cot_near],
        flops=10**9,
        out_hbm=(0,),
        scratch=[
            pltpu.VMEM((width // 128 + 2, lanes, 128), F32),
            pltpu.VMEM((local, steps, width), BF16),
            dma((1,)),
        ],
    )
    z_high = (width // 128 // mixes) * patch
    y_high = part_rows - heads * z_high
    slots = call(
        functools.partial(slot_kernel, heads, z_high),
        [((z_high + y_high, 128), F32)] * heads,
        [parts[0]] + [swap(parts[s], "mix", 1, mixes, s) for s in range(1, mixes)],
    )
    order = ordered(heads, HEAD_ORDER)
    both = added([slots[0]] + [swap(slots[s], "ctx", per, heads, s) for s in order])
    stride = 1
    for radix in radices(per):
        order = ordered(radix, GROUP_ORDER)
        both = added([both] + [swap(both, "ctx", stride, radix, s) for s in order])
        stride *= radix
    pieces = [both] + [swap(both, "mix", 1, mixes, s) for s in range(1, mixes)]
    grads = call(
        functools.partial(final_kernel, heads, mixes),
        [((rows_out, 3 * width), F32), ((rows_out, width), F32), ((rows_out, patch), F32)],
        pieces + [a, keys, own, qkv_rows],
        scratch=[pltpu.VMEM((width // 128 + 2, lanes, 128), F32)],
    )
    return output, grads[0], grads[1], grads[2]


def solution(mesh):
    placed = (
        P("mix", "ctx"),
        P(),
        P(),
        P(),
        P(),
        P(),
        P(),
        P("mix", None, "ctx"),
        P("mix", "ctx", None),
    )
    return jax.shard_map(
        shards,
        mesh=mesh,
        in_specs=placed,
        out_specs=(P("mix", "ctx", None), P("ctx", None), P("ctx", None), P("ctx", None)),
        check_vma=False,
    )
```

```python
import functools

import jax
import jax.numpy as jnp
from jax import lax
from jax.experimental import pallas as pl
from jax.experimental.pallas import tpu as pltpu
from jax.sharding import PartitionSpec as P

EPS = 1e-06
F32 = jnp.float32
BF16 = jnp.bfloat16
LEVEL_ORDERS = ((1, 2, 3), (1, 2, 3))
HEAD_ORDER = (1, 2, 3)
GROUP_ORDER = (1, 2, 3)
VMEM_LIMIT = 24 * 2**20


def quick(left, right, dims=((1,), (0,))):
    return lax.dot_general(
        left.astype(BF16), right.astype(BF16), (dims, ((), ())), preferred_element_type=F32
    )


def halves(array):
    high = array.astype(BF16)
    return high, (array - high.astype(F32)).astype(BF16)


def rows_cols(shape):
    return lax.broadcasted_iota(jnp.int32, shape, 0), lax.broadcasted_iota(jnp.int32, shape, 1)


def block_mask(heads, high, wide):
    row, col = rows_cols((heads * high, heads * wide))
    return (row // high) == (col // wide)


def stacked(array, heads):
    return jnp.concatenate([array] * heads, axis=0)


def radices(count):
    found = []
    while count > 1:
        radix = 4 if count % 4 == 0 else 2 if count % 2 == 0 else count
        found.append(radix)
        count //= radix
    return found


def other(place, radix, slot):
    if radix & (radix - 1) == 0:
        return place ^ slot
    return (place + slot) % radix


def swap(array, axis, stride, radix, slot):
    pairs = []
    for source in range(lax.axis_size(axis)):
        place = (source // stride) % radix
        for target in range(radix):
            if other(target, radix, slot) == place:
                pairs.append((source, source + (target - place) * stride))
    return lax.ppermute(array, axis, pairs)


def call(kernel, outs, ins, hbm=(), out_hbm=(), flops=0, scratch=()):
    specs = [
        pl.BlockSpec(memory_space=pltpu.HBM if i in hbm else pltpu.VMEM) for i in range(len(ins))
    ]
    ins = [
        pltpu.with_memory_space_constraint(x, pltpu.HBM) if i in hbm else x
        for i, x in enumerate(ins)
    ]
    return pl.pallas_call(
        kernel,
        out_shape=[jax.ShapeDtypeStruct(s, d) for s, d in outs],
        in_specs=specs,
        out_specs=[
            pl.BlockSpec(memory_space=pl.ANY if i in out_hbm else pltpu.VMEM)
            for i in range(len(outs))
        ],
        scratch_shapes=list(scratch),
        compiler_params=pltpu.CompilerParams(vmem_limit_bytes=VMEM_LIMIT),
        cost_estimate=pl.CostEstimate(flops=flops, bytes_accessed=1 << 20, transcendentals=0),
    )(*ins)


def rebuilt(high, low):
    top = jnp.concatenate([high, low], axis=1)
    bottom = jnp.concatenate([high, jnp.zeros_like(low)], axis=1)
    return jnp.concatenate([top, bottom], axis=0)


def pair(array):
    return jnp.concatenate(halves(array), axis=1)


def fine(left, right):
    both = quick(left, right)
    half = both.shape[1] // 2
    return both[:, :half] + both[:, half:]


def summed(array, ones):
    return quick(pair(array), ones)


def fetch(sources, targets, sems):
    copies = [
        pltpu.make_async_copy(source, target, sems.at[i])
        for i, (source, target) in enumerate(zip(sources, targets))
    ]
    for copy in copies:
        copy.start()
    return copies


def local_kernel(held, patch, mixes, *refs):
    inputs, outs, scratch = refs[:5], refs[5:10], refs[10:]
    part_ref, factor_ref, gx_ref, fade_ref, row_ref = outs
    src, forget, ids, weights, lengths, sems = scratch
    copies = fetch(inputs, (src, forget, ids, weights, lengths), sems)
    me = lax.axis_index("mix")
    local, high, lanes = part_ref.shape
    _, heads, steps = forget.shape
    s, t = rows_cols((steps, steps))
    upto = (s <= t).astype(BF16)
    first = lax.axis_index("ctx") * (high * lanes // patch)
    row, col = rows_cols((high, lanes))
    position = first + row * (lanes // patch) + col // patch
    for copy in copies:
        copy.wait()
    for b in range(local):
        mixture = me * local + b
        total = jnp.zeros((high, lanes), F32)
        terms = []
        for term in range(ids.shape[1]):
            shown = jnp.where(position < lengths[mixture, term], weights[mixture, term], 0.0)
            at = ids[mixture, term] - me * held
            here = jnp.logical_and(at >= 0, at < held)
            rows = src[pl.ds(jnp.where(here, at, 0), high, held), :]
            total += jnp.where(here, shown, 0.0) * rows
            terms.append((ids[mixture, term], shown))
        part_ref[b] = total
        for slot in range(1, mixes):
            for source in range(held):
                wanted = other(me, mixes, slot) * held + source
                factor = jnp.zeros((high, lanes), F32)
                for identity, shown in terms:
                    factor += jnp.where(identity == wanted, shown, 0.0)
                factor_ref[slot - 1, b, source] = factor
    for b in range(local):
        log_gate = jnp.log1p(forget[b] - 1.0)
        high_half, low = halves(log_gate)
        lowest = (log_gate - high_half.astype(F32) - low.astype(F32)).astype(BF16)
        sums = quick(jnp.concatenate([high_half, low, lowest, jnp.zeros_like(low)], axis=0), upto)
        sums = sums[:heads] + sums[heads : 2 * heads] + sums[2 * heads : 3 * heads]
        row_ref[b * heads : (b + 1) * heads] = sums
        wide = jnp.broadcast_to(sums[:, None, :], (heads, patch, steps)).reshape(-1, steps)
        gx = wide.T
        gx_ref[b] = gx
        fade_ref[b] = jnp.exp(gx[steps - 1 : steps] - gx)


def gram_kernel(held, patch, others, *refs):
    sources, (part, factor, gx, fade, mt_ref, pack_ref) = refs[:others], refs[others:]
    local, steps, lanes = gx.shape
    per = lanes // patch
    t, r = rows_cols((local * steps, local * steps // per))
    spread = (t // per == r).astype(BF16)
    t, lane = rows_cols((local * steps, lanes))
    chosen = t % per == lane // patch
    a, b_ = rows_cols((lanes, lanes))
    fold = (a % patch == b_ % patch).astype(BF16)
    totals = []
    for b in range(local):
        total = part[b]
        for slot, source in enumerate(sources):
            for s in range(held):
                total += factor[slot, b, s] * source[pl.ds(s, steps // per, held), :]
        totals.append(total)
    wide = quick(spread, jnp.concatenate(totals, axis=0))
    mt = quick(jnp.where(chosen, wide, 0.0), fold)
    mt_ref[...] = mt.astype(BF16).reshape(mt_ref.shape)
    pack_ref[local * patch :] = jnp.zeros((pack_ref.shape[0] - local * patch, lanes), F32)
    for b in range(local):
        own = mt[b * steps : (b + 1) * steps]
        pack_ref[b * patch : (b + 1) * patch] = quick(own[:, :patch], own * fade[b], ((0,), (0,)))
        pack_ref[local * patch + b : local * patch + b + 1] = gx[b, steps - 1 : steps]


def weight_kernel(heads, *refs):
    embed_hbm, qkv_hbm, _ = refs[:3]
    a_ref, m_ref, c_ref, k_ref, v_ref, vb_ref, own_ref, qkv_ref = refs[3:11]
    embed, qkv, tall, sems = refs[11:]
    copies = fetch((embed_hbm, qkv_hbm), (embed, qkv), sems)
    patch, width = embed.shape
    rows_out = qkv_ref.shape[0]
    ctx = lax.axis_index("ctx")
    mine = pl.ds(pl.multiple_of(ctx * rows_out, rows_out), rows_out)
    copies[0].wait()
    tall[:, :patch] = embed[...].astype(F32).T
    copies[1].wait()
    a = quick(embed[...], qkv[...])
    a_ref[...] = a
    qkv_ref[...] = qkv[mine, :]
    mask = block_mask(heads, patch, width // heads)
    query, key, value = [
        jnp.where(mask, stacked(a[:, j * width : (j + 1) * width], heads), 0.0) for j in range(3)
    ]
    across = ((1,), (1,))
    key_high, key_low = halves(key)
    value_high, value_low = halves(value)
    query_high, query_low = halves(query)
    k_ref[...] = jnp.concatenate([key_high, key_high, key_low], axis=0)
    m = quick(query_high, key_high, across) + quick(query_high, key_low, across)
    m = m + quick(query_low, key_high, across)
    m_ref[...] = rebuilt(*halves(m))
    mixed = quick(value_high, value_low, across)
    c = quick(value_high, value_high, across) + mixed + mixed.T
    c_ref[...] = rebuilt(*halves(c))
    v_ref[...] = rebuilt(*halves(stacked_heads(a[:, 2 * width :], heads)))
    vb_ref[...] = jnp.concatenate([value_high, value_low], axis=1)
    tall[:, patch : 2 * patch] = a[:, 2 * width :].T
    own_ref[...] = tall[mine, :]


def out_kernel(out_hbm, cot_hbm, vb, _, b_ref, bb_ref, out_ref, cot_ref, sems):
    copies = fetch((out_hbm, cot_hbm), (out_ref, cot_ref), sems)
    copies[0].wait()
    product = quick(vb[...], jnp.concatenate([out_ref[...], out_ref[...]], axis=0)).astype(BF16)
    b_ref[...] = product
    copies[1].wait()
    given = cot_ref[...].reshape(bb_ref.shape[0] * bb_ref.shape[1], -1)
    bb_ref[...] = quick(given, product, ((1,), (1,))).reshape(bb_ref.shape)


def spread_heads(gram, square, heads):
    return jnp.where(square, stacked(gram, heads), 0.0).astype(BF16)


def intra_kernel(heads, mt, gx, sums, m, _, z_ref, qe_ref, lead_ref, bd_ref, decay_ref, gl_ref, er_ref):
    local, steps, lanes = mt.shape
    patch = lanes // heads
    subs = bd_ref.shape[1]
    sub = steps // subs
    t, s = rows_cols((sub, heads * sub))
    causal = t >= s % sub
    row, col = rows_cols((heads * sub, lanes))
    diagonal = (row // sub == col // patch).astype(BF16)
    for b in range(local):
        query = fine(jnp.concatenate([mt[b], jnp.zeros_like(mt[b])], axis=1), m[...])
        gates = sums[b * heads : (b + 1) * heads]
        wide = jnp.broadcast_to(gates[:, None, :], (heads, sub, steps))
        wide = wide.reshape(heads * sub, steps).T
        for c in range(subs):
            rows = slice(c * sub, (c + 1) * sub)
            g = gx[b, rows]
            if c == 0:
                start = jnp.zeros((1, lanes), F32)
                gl_ref[b, c] = jnp.zeros((patch, lanes), F32)
            else:
                start = gx[b, c * sub - 1 : c * sub]
                past = mt[b, : c * sub]
                fading = past.astype(F32) * jnp.exp(start - gx[b, : c * sub])
                gl_ref[b, c] = quick(past[:, :patch], fading, ((0,), (0,)))
            er_ref[b, c] = jnp.broadcast_to(jnp.exp(start), (8, lanes))
            lead = jnp.exp(g - start)
            lead_ref[b, rows] = lead
            qe_ref[b, rows] = (query[rows] * lead).astype(BF16)
            bd = stacked(mt[b, rows], heads) * diagonal
            bd_ref[b, c] = bd
            across = jnp.concatenate([gates[h : h + 1, rows] for h in range(heads)], axis=1)
            decay = jnp.where(causal, jnp.exp(wide[rows] - across), 0.0)
            decay_ref[b, c] = decay
            scores = quick(query[rows], bd, ((1,), (1,))) * decay
            z_ref[b, rows] = quick(scores, bd)


def level(packs, place, local, patch, wanted):
    radix = len(packs)
    at = [other(place, radix, slot) for slot in range(radix)]
    totals = [pack[local * patch :] for pack in packs]
    zero = jnp.zeros_like(totals[0])
    grams = None
    total = zero
    for m in range(radix):
        if wanted == "before" and m == 0:
            continue
        power = zero
        for k in range(radix):
            if k == m or (wanted == "before" and k == 0):
                continue
            after = at[k] > at[m]
            if wanted == "before":
                after = jnp.logical_and(after, at[k] < place)
            power = power + jnp.where(after, totals[k], 0.0)
        factor = jnp.exp(power)
        if wanted == "before":
            factor = jnp.where(at[m] < place, factor, 0.0)
            total = total + jnp.where(at[m] < place, totals[m], 0.0)
        else:
            total = total + totals[m]
        terms = [factor[b : b + 1] * packs[m][b * patch : (b + 1) * patch] for b in range(local)]
        grams = terms if grams is None else [g + x for g, x in zip(grams, terms)]
    return jnp.concatenate(grams + [total], axis=0)


def joined(near, far, local, patch):
    totals = near[local * patch :]
    factor = jnp.exp(totals)
    grams = [
        near[b * patch : (b + 1) * patch] + factor[b : b + 1] * far[b * patch : (b + 1) * patch]
        for b in range(local)
    ]
    return jnp.concatenate(grams + [totals + far[local * patch :]], axis=0)


def ordered(radix, order):
    return order if radix == 4 else tuple(range(1, radix))


def level_order(number, radix):
    return ordered(radix, LEVEL_ORDERS[min(number, len(LEVEL_ORDERS) - 1)])


def in_slots(packs, number):
    order = (0,) + level_order(number, len(packs))
    return [packs[order.index(slot)] for slot in range(len(packs))]


def level_kernel(local, patch, stride, radix, number, *refs):
    place = (lax.axis_index("ctx") // stride) % radix
    packs = in_slots([ref[...] for ref in refs[:radix]], number)
    before = level(packs, place, local, patch, "before")
    if number > 0:
        before = joined(refs[radix][...], before, local, patch)
    refs[-2][...] = level(packs, place, local, patch, "whole")
    refs[-1][...] = before


def main_kernel(heads, stride, radix, number, mixes, *refs):
    count = radix + int(number > 0)
    packs = in_slots([ref[...] for ref in refs[:radix]], number)
    mt, lead, bd, decay, intra, qe, gl, er, bb, c, big_b, v, w_out, cot = refs[count : count + 14]
    out_hbm, *part_refs = refs[count + 14 : -3]
    z_scr, out_scr, sems = refs[-3:]
    local, steps, lanes = mt.shape
    patch = lanes // heads
    subs = bd.shape[1]
    sub = steps // subs
    width = w_out.shape[0]
    size = width // heads
    place = (lax.axis_index("ctx") // stride) % radix
    state = level(packs, place, local, patch, "before")
    if number > 0:
        state = joined(refs[radix][...], state, local, patch)
    square = block_mask(heads, patch, patch)
    ones = jnp.concatenate([square.astype(BF16)] * 2, axis=0)
    places = [(b, i) for b in range(local) for i in range(subs)]
    grams = []
    z = []
    for b, i in places:
        gram = gl[b, i] + er[b, i, :1] * state[b * patch : (b + 1) * patch]
        grams.append(spread_heads(gram, square, heads))
        rows = slice(i * sub, (i + 1) * sub)
        z.append(intra[b, rows] + quick(qe[b, rows], grams[-1]))
    z = jnp.concatenate(z, axis=0)
    every = (local * steps, lanes)
    around = bb[...].reshape(every)
    met = summed(z * around, ones)
    zc = fine(pair(z), c[...])
    irms = lax.rsqrt(summed(z * zc, ones) * (1.0 / size) + EPS)
    zn = z * irms
    znb = zn.astype(BF16)
    out_scr[...] = quick(znb, big_b[...]).astype(BF16).reshape(out_scr.shape)
    leaving = fetch((out_scr,), (out_hbm,), sems)
    aligned = met * (irms * (1.0 / size))
    u = irms * (around - aligned * (irms * zc))
    ub = u.astype(BF16)
    ue = (u * lead[...].reshape(every)).astype(BF16)
    y = []
    for (b, i), gram in zip(places, grams):
        rows = slice(b * steps + i * sub, b * steps + (i + 1) * sub)
        scores = (quick(ub[rows], bd[b, i], ((1,), (1,))) * decay[b, i]).astype(BF16)
        left = jnp.concatenate([scores, ue[rows]], axis=1)
        y.append(quick(left, jnp.concatenate([bd[b, i], gram], axis=0)))
    y = jnp.concatenate(y, axis=0)
    given = cot[...].reshape(local * steps, width)
    x_total = quick(mt[...].reshape(every)[:, :patch], y, ((0,), (0,)))
    right = jnp.concatenate([given, (aligned * zn).astype(BF16)], axis=1)
    zw_total = quick(znb, right, ((0,), (0,)))
    big_z = zw_total[:, :width]
    w_total = jnp.where(square, zw_total[:, width:], 0.0)
    y_total = -fine(pair(w_total), v[...])
    y_rows = []
    for h in range(heads):
        rows = slice(h * patch, (h + 1) * patch)
        both = jnp.concatenate(halves(big_z[rows]), axis=0)
        found = quick(both, w_out[h * size : (h + 1) * size], ((1,), (1,)))
        y_rows.append(y_total[rows] + found[:patch] + found[patch:])
    y_total = jnp.concatenate(y_rows, axis=0)
    per = lax.axis_size("ctx") // heads
    head = lax.axis_index("ctx") // per
    me = lax.axis_index("mix")
    panels = width // 128
    share = panels // mixes
    for k in range(panels):
        z_scr[k] = big_z[:, k * 128 : (k + 1) * 128]
    y_high = lanes // mixes
    x_high = patch // mixes
    z_scr[panels] = y_total
    z_scr[panels + 1, :patch] = x_total
    for slot in range(mixes):
        part = other(me, mixes, slot)
        out = part_refs[slot]
        at = 0
        for q in range(heads):
            for k in range(share):
                rows = pl.ds(other(head, heads, q) * patch, patch)
                out[at : at + patch] = z_scr[part * share + k, rows, :]
                at += patch
        out[at : at + y_high] = z_scr[panels, pl.ds(part * y_high, y_high), :]
        at += y_high
        out[at : at + x_high] = z_scr[panels + 1, pl.ds(part * x_high, x_high), :]
    for copy in leaving:
        copy.wait()


def stacked_heads(array, heads):
    size = array.shape[1] // heads
    return jnp.concatenate([array[:, h * size : (h + 1) * size] for h in range(heads)], axis=0)


def final_kernel(heads, mixes, *refs):
    parts = refs[:mixes]
    a, keys, own, qkv_rows = refs[mixes : mixes + 4]
    gq_ref, go_ref, ge_ref, scr = refs[mixes + 4 :]
    patch = ge_ref.shape[1]
    width = go_ref.shape[1]
    size = width // heads
    lanes = heads * patch
    panels = width // 128
    share = panels // mixes
    y_high = lanes // mixes
    x_high = patch // mixes
    me = lax.axis_index("mix")
    for slot in range(mixes):
        part = other(me, mixes, slot)
        at = 0
        for k in range(share):
            scr[part * share + k, :patch] = parts[slot][at : at + patch]
            at += patch
        scr[panels, pl.ds(part * y_high, y_high), :] = parts[slot][at : at + y_high]
        at += y_high
        scr[panels + 1, pl.ds(part * x_high, x_high), :] = parts[slot][at : at + x_high]
    y = scr[panels]
    x_high, x_low = halves(scr[panels + 1, :patch])
    t_query = quick(jnp.concatenate([x_high, x_low, x_high], axis=1), keys[...])
    query_high, query_low = halves(a[:, :width])
    crossed = quick(
        jnp.concatenate([x_high, x_low, x_high], axis=0),
        jnp.concatenate([query_high, query_high, query_low], axis=0),
        ((0,), (0,)),
    )
    t_key = [crossed[h * patch : (h + 1) * patch, h * size : (h + 1) * size] for h in range(heads)]
    t_value = [y[h * patch : (h + 1) * patch] for h in range(heads)]
    t = jnp.concatenate([t_query] + t_key + t_value, axis=1)
    high, low = halves(t)
    both = jnp.concatenate([high, low], axis=0)
    embed_rows = own[:, :patch].astype(BF16)
    gq_ref[...] = quick(jnp.concatenate([embed_rows, embed_rows], axis=1), both)
    found = quick(qkv_rows[...], both, ((1,), (1,)))
    ge_ref[...] = found[:, :patch] + found[:, patch:]
    v_high, v_low = halves(own[:, patch : 2 * patch])
    z_high, z_low = halves(jnp.concatenate([scr[k, :patch] for k in range(panels)], axis=1))
    go_ref[...] = quick(
        jnp.concatenate([v_high, v_low, v_high], axis=1),
        jnp.concatenate([z_high, z_high, z_low], axis=0),
    )


def slot_kernel(heads, z_high, *refs):
    parts, slots = refs[:-heads], refs[-heads:]
    total = parts[0][...]
    for part in parts[1:]:
        total = total + part[...]
    for q in range(heads):
        slots[q][:z_high] = total[q * z_high : (q + 1) * z_high]
        slots[q][z_high:] = total[heads * z_high :]


def add_kernel(*refs):
    total = refs[0][...]
    for ref in refs[1:-1]:
        total = total + ref[...]
    refs[-1][...] = total


def added(arrays):
    (total,) = call(add_kernel, [(arrays[0].shape, F32)], arrays)
    return total


def shards(
    sources, source_ids, mix_weights, source_lengths, w_embed, w_qkv, w_out, forget, cotangent
):
    mixes = lax.axis_size("mix")
    count = lax.axis_size("ctx")
    patch = w_embed.shape[1]
    local, heads, steps = forget.shape
    width = w_out.shape[0]
    size = width // heads
    lanes = heads * patch
    held = sources.shape[0]
    rows_out = width // count
    per = count // heads
    dma = pltpu.SemaphoreType.DMA
    subs = heads
    sub = steps // subs
    part_shape = (local, steps * patch // lanes, lanes)
    panels = sources.reshape((held,) + part_shape[1:]).transpose(1, 0, 2).reshape(-1, lanes)
    got = [swap(panels, "mix", 1, mixes, s) for s in range(1, mixes)]
    part, factor, gx, fade, sums = call(
        functools.partial(local_kernel, held, patch, mixes),
        [
            (part_shape, F32),
            ((max(mixes - 1, 1), local, held) + part_shape[1:], F32),
            ((local, steps, lanes), F32),
            ((local, steps, lanes), F32),
            ((local * heads, steps), F32),
        ],
        [panels, forget, source_ids, mix_weights, source_lengths],
        hbm=(0, 1, 2, 3, 4),
        flops=10**9,
        scratch=[
            pltpu.VMEM(panels.shape, F32),
            pltpu.VMEM(forget.shape, F32),
            pltpu.SMEM(source_ids.shape, jnp.int32),
            pltpu.SMEM(mix_weights.shape, F32),
            pltpu.SMEM(source_lengths.shape, jnp.int32),
            dma((5,)),
        ],
    )
    high = -(-local // 8) * 8
    pack_shape = ((local * patch + high, lanes), F32)
    mt, pack = call(
        functools.partial(gram_kernel, held, patch, len(got)),
        [((local, steps, lanes), BF16), pack_shape],
        got + [part, factor, gx, fade],
    )
    a, m, c, keys, v, value_blocks, own, qkv_rows = call(
        functools.partial(weight_kernel, heads),
        [
            ((patch, 3 * width), F32),
            ((2 * lanes, 2 * lanes), BF16),
            ((2 * lanes, 2 * lanes), BF16),
            ((3 * lanes, width), BF16),
            ((2 * lanes, 2 * size), BF16),
            ((lanes, 2 * width), BF16),
            ((rows_out, 2 * patch), F32),
            ((rows_out, 3 * width), BF16),
        ],
        [w_embed.T, w_qkv, pack],
        hbm=(0, 1),
        flops=10**9,
        scratch=[
            pltpu.VMEM((patch, width), BF16),
            pltpu.VMEM(w_qkv.shape, BF16),
            pltpu.VMEM((width, 2 * patch), F32),
            dma((2,)),
        ],
    )
    steps_up = radices(count)
    stride = 1
    near = []
    for i, radix in enumerate(steps_up):
        order = level_order(i, radix)
        packs = [pack] + [swap(pack, "ctx", stride, radix, s) for s in order]
        if i == len(steps_up) - 1:
            break
        pack, before = call(
            functools.partial(level_kernel, local, patch, stride, radix, i),
            [pack_shape] * 2,
            packs + near,
        )
        near = [before]
        stride *= radix
    intra, qe, lead, bd, decay, gl, er = call(
        functools.partial(intra_kernel, heads),
        [
            ((local, steps, lanes), F32),
            ((local, steps, lanes), BF16),
            ((local, steps, lanes), F32),
            ((local, subs, heads * sub, lanes), BF16),
            ((local, subs, sub, heads * sub), F32),
            ((local, subs, patch, lanes), F32),
            ((local, subs, 8, lanes), F32),
        ],
        [mt, gx, sums, m, pack],
        flops=10**9,
    )
    big_b, bb, w_out_near, cot_near = call(
        out_kernel,
        [
            ((lanes, width), BF16),
            ((local, steps, lanes), F32),
            (w_out.shape, BF16),
            (cotangent.shape, BF16),
        ],
        [w_out, cotangent, value_blocks, pack],
        hbm=(0, 1),
        flops=10**9,
        scratch=[dma((2,))],
    )
    part_rows = heads * (width // 128 // mixes) * patch + lanes // mixes + patch // mixes
    output, *parts = call(
        functools.partial(main_kernel, heads, stride, radix, i, mixes),
        [((local, steps, width), BF16)] + [((part_rows, 128), F32)] * mixes,
        packs + near + [mt, lead, bd, decay, intra, qe, gl, er, bb, c, big_b, v, w_out_near, cot_near],
        flops=10**9,
        out_hbm=(0,),
        scratch=[
            pltpu.VMEM((width // 128 + 2, lanes, 128), F32),
            pltpu.VMEM((local, steps, width), BF16),
            dma((1,)),
        ],
    )
    z_high = (width // 128 // mixes) * patch
    y_high = part_rows - heads * z_high
    slots = call(
        functools.partial(slot_kernel, heads, z_high),
        [((z_high + y_high, 128), F32)] * heads,
        [parts[0]] + [swap(parts[s], "mix", 1, mixes, s) for s in range(1, mixes)],
    )
    order = ordered(heads, HEAD_ORDER)
    both = added([slots[0]] + [swap(slots[s], "ctx", per, heads, s) for s in order])
    stride = 1
    for radix in radices(per):
        order = ordered(radix, GROUP_ORDER)
        both = added([both] + [swap(both, "ctx", stride, radix, s) for s in order])
        stride *= radix
    pieces = [both] + [swap(both, "mix", 1, mixes, s) for s in range(1, mixes)]
    grads = call(
        functools.partial(final_kernel, heads, mixes),
        [((rows_out, 3 * width), F32), ((rows_out, width), F32), ((rows_out, patch), F32)],
        pieces + [a, keys, own, qkv_rows],
        scratch=[pltpu.VMEM((width // 128 + 2, lanes, 128), F32)],
    )
    return output, grads[0], grads[1], grads[2]


def solution(mesh):
    placed = (
        P("mix", "ctx"),
        P(),
        P(),
        P(),
        P(),
        P(),
        P(),
        P("mix", None, "ctx"),
        P("mix", "ctx", None),
    )
    return jax.shard_map(
        shards,
        mesh=mesh,
        in_specs=placed,
        out_specs=(P("mix", "ctx", None), P("ctx", None), P("ctx", None), P("ctx", None)),
        check_vma=False,
    )
```

```python
import functools

import jax
import jax.numpy as jnp
from jax import lax
from jax.experimental import pallas as pl
from jax.experimental.pallas import tpu as pltpu
from jax.sharding import PartitionSpec as P

EPS = 1e-06
F32 = jnp.float32
BF16 = jnp.bfloat16
LEVEL_ORDERS = ((1, 2, 3), (1, 2, 3))
HEAD_ORDER = (1, 2, 3)
GROUP_ORDER = (1, 2, 3)
VMEM_LIMIT = 24 * 2**20


def quick(left, right, dims=((1,), (0,))):
    return lax.dot_general(
        left.astype(BF16), right.astype(BF16), (dims, ((), ())), preferred_element_type=F32
    )


def halves(array):
    high = array.astype(BF16)
    return high, (array - high.astype(F32)).astype(BF16)


def rows_cols(shape):
    return lax.broadcasted_iota(jnp.int32, shape, 0), lax.broadcasted_iota(jnp.int32, shape, 1)


def block_mask(heads, high, wide):
    row, col = rows_cols((heads * high, heads * wide))
    return (row // high) == (col // wide)


def stacked(array, heads):
    return jnp.concatenate([array] * heads, axis=0)


def radices(count):
    found = []
    while count > 1:
        radix = 4 if count % 4 == 0 else 2 if count % 2 == 0 else count
        found.append(radix)
        count //= radix
    return found


def other(place, radix, slot):
    if radix & (radix - 1) == 0:
        return place ^ slot
    return (place + slot) % radix


def swap(array, axis, stride, radix, slot):
    pairs = []
    for source in range(lax.axis_size(axis)):
        place = (source // stride) % radix
        for target in range(radix):
            if other(target, radix, slot) == place:
                pairs.append((source, source + (target - place) * stride))
    return lax.ppermute(array, axis, pairs)


def call(kernel, outs, ins, hbm=(), out_hbm=(), flops=0, scratch=()):
    specs = [
        pl.BlockSpec(memory_space=pltpu.HBM if i in hbm else pltpu.VMEM) for i in range(len(ins))
    ]
    ins = [
        pltpu.with_memory_space_constraint(x, pltpu.HBM) if i in hbm else x
        for i, x in enumerate(ins)
    ]
    return pl.pallas_call(
        kernel,
        out_shape=[jax.ShapeDtypeStruct(s, d) for s, d in outs],
        in_specs=specs,
        out_specs=[
            pl.BlockSpec(memory_space=pl.ANY if i in out_hbm else pltpu.VMEM)
            for i in range(len(outs))
        ],
        scratch_shapes=list(scratch),
        compiler_params=pltpu.CompilerParams(vmem_limit_bytes=VMEM_LIMIT),
        cost_estimate=pl.CostEstimate(flops=flops, bytes_accessed=1 << 20, transcendentals=0),
    )(*ins)


def rebuilt(high, low):
    top = jnp.concatenate([high, low], axis=1)
    bottom = jnp.concatenate([high, jnp.zeros_like(low)], axis=1)
    return jnp.concatenate([top, bottom], axis=0)


def pair(array):
    return jnp.concatenate(halves(array), axis=1)


def fine(left, right):
    both = quick(left, right)
    half = both.shape[1] // 2
    return both[:, :half] + both[:, half:]


def summed(array, ones):
    return quick(pair(array), ones)


def fetch(sources, targets, sems):
    copies = [
        pltpu.make_async_copy(source, target, sems.at[i])
        for i, (source, target) in enumerate(zip(sources, targets))
    ]
    for copy in copies:
        copy.start()
    return copies


def local_kernel(held, patch, mixes, *refs):
    inputs, outs, scratch = refs[:5], refs[5:10], refs[10:]
    part_ref, factor_ref, gx_ref, fade_ref, row_ref = outs
    src, forget, ids, weights, lengths, sems = scratch
    copies = fetch(inputs, (src, forget, ids, weights, lengths), sems)
    me = lax.axis_index("mix")
    local, high, lanes = part_ref.shape
    _, heads, steps = forget.shape
    s, t = rows_cols((steps, steps))
    upto = (s <= t).astype(BF16)
    first = lax.axis_index("ctx") * (high * lanes // patch)
    row, col = rows_cols((high, lanes))
    position = first + row * (lanes // patch) + col // patch
    for copy in copies:
        copy.wait()
    for b in range(local):
        mixture = me * local + b
        total = jnp.zeros((high, lanes), F32)
        terms = []
        for term in range(ids.shape[1]):
            shown = jnp.where(position < lengths[mixture, term], weights[mixture, term], 0.0)
            at = ids[mixture, term] - me * held
            here = jnp.logical_and(at >= 0, at < held)
            rows = src[pl.ds(jnp.where(here, at, 0), high, held), :]
            total += jnp.where(here, shown, 0.0) * rows
            terms.append((ids[mixture, term], shown))
        part_ref[b] = total
        for slot in range(1, mixes):
            for source in range(held):
                wanted = other(me, mixes, slot) * held + source
                factor = jnp.zeros((high, lanes), F32)
                for identity, shown in terms:
                    factor += jnp.where(identity == wanted, shown, 0.0)
                factor_ref[slot - 1, b, source] = factor
    for b in range(local):
        log_gate = jnp.log1p(forget[b] - 1.0)
        high_half, low = halves(log_gate)
        lowest = (log_gate - high_half.astype(F32) - low.astype(F32)).astype(BF16)
        sums = quick(jnp.concatenate([high_half, low, lowest, jnp.zeros_like(low)], axis=0), upto)
        sums = sums[:heads] + sums[heads : 2 * heads] + sums[2 * heads : 3 * heads]
        row_ref[b * heads : (b + 1) * heads] = sums
        wide = jnp.broadcast_to(sums[:, None, :], (heads, patch, steps)).reshape(-1, steps)
        gx = wide.T
        gx_ref[b] = gx
        fade_ref[b] = jnp.exp(gx[steps - 1 : steps] - gx)


def gram_kernel(held, patch, others, *refs):
    sources, (part, factor, gx, fade, mt_ref, pack_ref) = refs[:others], refs[others:]
    local, steps, lanes = gx.shape
    per = lanes // patch
    t, r = rows_cols((local * steps, local * steps // per))
    spread = (t // per == r).astype(BF16)
    t, lane = rows_cols((local * steps, lanes))
    chosen = t % per == lane // patch
    a, b_ = rows_cols((lanes, lanes))
    fold = (a % patch == b_ % patch).astype(BF16)
    totals = []
    for b in range(local):
        total = part[b]
        for slot, source in enumerate(sources):
            for s in range(held):
                total += factor[slot, b, s] * source[pl.ds(s, steps // per, held), :]
        totals.append(total)
    wide = quick(spread, jnp.concatenate(totals, axis=0))
    mt = quick(jnp.where(chosen, wide, 0.0), fold)
    mt_ref[...] = mt.astype(BF16).reshape(mt_ref.shape)
    pack_ref[local * patch :] = jnp.zeros((pack_ref.shape[0] - local * patch, lanes), F32)
    for b in range(local):
        own = mt[b * steps : (b + 1) * steps]
        pack_ref[b * patch : (b + 1) * patch] = quick(own[:, :patch], own * fade[b], ((0,), (0,)))
        pack_ref[local * patch + b : local * patch + b + 1] = gx[b, steps - 1 : steps]


def weight_kernel(heads, *refs):
    embed_hbm, qkv_hbm, _ = refs[:3]
    a_ref, m_ref, c_ref, k_ref, v_ref, vb_ref, own_ref, qkv_ref = refs[3:11]
    embed, qkv, tall, sems = refs[11:]
    copies = fetch((embed_hbm, qkv_hbm), (embed, qkv), sems)
    patch, width = embed.shape
    rows_out = qkv_ref.shape[0]
    ctx = lax.axis_index("ctx")
    mine = pl.ds(pl.multiple_of(ctx * rows_out, rows_out), rows_out)
    copies[0].wait()
    tall[:, :patch] = embed[...].astype(F32).T
    copies[1].wait()
    a = quick(embed[...], qkv[...])
    a_ref[...] = a
    qkv_ref[...] = qkv[mine, :]
    mask = block_mask(heads, patch, width // heads)
    query, key, value = [
        jnp.where(mask, stacked(a[:, j * width : (j + 1) * width], heads), 0.0) for j in range(3)
    ]
    across = ((1,), (1,))
    key_high, key_low = halves(key)
    value_high, value_low = halves(value)
    query_high, query_low = halves(query)
    k_ref[...] = jnp.concatenate([key_high, key_high, key_low], axis=0)
    m = quick(query_high, key_high, across) + quick(query_high, key_low, across)
    m = m + quick(query_low, key_high, across)
    m_ref[...] = rebuilt(*halves(m))
    mixed = quick(value_high, value_low, across)
    c = quick(value_high, value_high, across) + mixed + mixed.T
    c_ref[...] = rebuilt(*halves(c))
    v_ref[...] = rebuilt(*halves(stacked_heads(a[:, 2 * width :], heads)))
    vb_ref[...] = jnp.concatenate([value_high, value_low], axis=1)
    tall[:, patch : 2 * patch] = a[:, 2 * width :].T
    own_ref[...] = tall[mine, :]


def out_kernel(out_hbm, cot_hbm, vb, _, b_ref, bb_ref, out_ref, cot_ref, sems):
    copies = fetch((out_hbm, cot_hbm), (out_ref, cot_ref), sems)
    copies[0].wait()
    product = quick(vb[...], jnp.concatenate([out_ref[...], out_ref[...]], axis=0)).astype(BF16)
    b_ref[...] = product
    copies[1].wait()
    given = cot_ref[...].reshape(bb_ref.shape[0] * bb_ref.shape[1], -1)
    bb_ref[...] = quick(given, product, ((1,), (1,))).reshape(bb_ref.shape)


def spread_heads(gram, square, heads):
    return jnp.where(square, stacked(gram, heads), 0.0).astype(BF16)


def intra_kernel(heads, mt, gx, sums, m, _, z_ref, qe_ref, lead_ref, bd_ref, decay_ref, gl_ref, er_ref, turned_ref):
    local, steps, lanes = mt.shape
    patch = lanes // heads
    subs = bd_ref.shape[1]
    sub = steps // subs
    t, s = rows_cols((sub, heads * sub))
    causal = t >= s % sub
    row, col = rows_cols((heads * sub, lanes))
    diagonal = (row // sub == col // patch).astype(BF16)
    for b in range(local):
        query = fine(jnp.concatenate([mt[b], jnp.zeros_like(mt[b])], axis=1), m[...])
        turned_ref[:, b * steps : (b + 1) * steps] = mt[b].astype(F32).T[:patch].astype(BF16)
        gates = sums[b * heads : (b + 1) * heads]
        wide = jnp.broadcast_to(gates[:, None, :], (heads, sub, steps))
        wide = wide.reshape(heads * sub, steps).T
        for c in range(subs):
            rows = slice(c * sub, (c + 1) * sub)
            g = gx[b, rows]
            if c == 0:
                start = jnp.zeros((1, lanes), F32)
                gl_ref[b, c] = jnp.zeros((patch, lanes), F32)
            else:
                start = gx[b, c * sub - 1 : c * sub]
                past = mt[b, : c * sub]
                fading = past.astype(F32) * jnp.exp(start - gx[b, : c * sub])
                gl_ref[b, c] = quick(past[:, :patch], fading, ((0,), (0,)))
            er_ref[b, c] = jnp.broadcast_to(jnp.exp(start), (8, lanes))
            lead = jnp.exp(g - start)
            lead_ref[b, rows] = lead
            qe_ref[b, rows] = (query[rows] * lead).astype(BF16)
            bd = stacked(mt[b, rows], heads) * diagonal
            bd_ref[b, c] = bd
            across = jnp.concatenate([gates[h : h + 1, rows] for h in range(heads)], axis=1)
            decay = jnp.where(causal, jnp.exp(wide[rows] - across), 0.0)
            decay_ref[b, c] = decay
            scores = quick(query[rows], bd, ((1,), (1,))) * decay
            z_ref[b, rows] = quick(scores, bd)


def level(packs, place, local, patch, wanted):
    radix = len(packs)
    at = [other(place, radix, slot) for slot in range(radix)]
    totals = [pack[local * patch :] for pack in packs]
    zero = jnp.zeros_like(totals[0])
    grams = None
    total = zero
    for m in range(radix):
        if wanted == "before" and m == 0:
            continue
        power = zero
        for k in range(radix):
            if k == m or (wanted == "before" and k == 0):
                continue
            after = at[k] > at[m]
            if wanted == "before":
                after = jnp.logical_and(after, at[k] < place)
            power = power + jnp.where(after, totals[k], 0.0)
        factor = jnp.exp(power)
        if wanted == "before":
            factor = jnp.where(at[m] < place, factor, 0.0)
            total = total + jnp.where(at[m] < place, totals[m], 0.0)
        else:
            total = total + totals[m]
        terms = [factor[b : b + 1] * packs[m][b * patch : (b + 1) * patch] for b in range(local)]
        grams = terms if grams is None else [g + x for g, x in zip(grams, terms)]
    return jnp.concatenate(grams + [total], axis=0)


def joined(near, far, local, patch):
    totals = near[local * patch :]
    factor = jnp.exp(totals)
    grams = [
        near[b * patch : (b + 1) * patch] + factor[b : b + 1] * far[b * patch : (b + 1) * patch]
        for b in range(local)
    ]
    return jnp.concatenate(grams + [totals + far[local * patch :]], axis=0)


def ordered(radix, order):
    return order if radix == 4 else tuple(range(1, radix))


def level_order(number, radix):
    return ordered(radix, LEVEL_ORDERS[min(number, len(LEVEL_ORDERS) - 1)])


def in_slots(packs, number):
    order = (0,) + level_order(number, len(packs))
    return [packs[order.index(slot)] for slot in range(len(packs))]


def level_kernel(local, patch, stride, radix, number, *refs):
    place = (lax.axis_index("ctx") // stride) % radix
    packs = in_slots([ref[...] for ref in refs[:radix]], number)
    before = level(packs, place, local, patch, "before")
    if number > 0:
        before = joined(refs[radix][...], before, local, patch)
    refs[-2][...] = level(packs, place, local, patch, "whole")
    refs[-1][...] = before


def main_kernel(heads, stride, radix, number, mixes, *refs):
    count = radix + int(number > 0)
    packs = in_slots([ref[...] for ref in refs[:radix]], number)
    turned, lead, bd, decay, intra, qe, gl, er, bb, c, v, w_out, cot = refs[count : count + 13]
    zn_ref, *part_refs = refs[count + 13 :]
    local, steps, lanes = lead.shape
    patch = lanes // heads
    subs = bd.shape[1]
    sub = steps // subs
    width = w_out.shape[0]
    size = width // heads
    place = (lax.axis_index("ctx") // stride) % radix
    state = level(packs, place, local, patch, "before")
    if number > 0:
        state = joined(refs[radix][...], state, local, patch)
    square = block_mask(heads, patch, patch)
    ones = jnp.concatenate([square.astype(BF16)] * 2, axis=0)
    places = [(b, i) for b in range(local) for i in range(subs)]
    grams = []
    z = []
    for b, i in places:
        gram = gl[b, i] + er[b, i, :1] * state[b * patch : (b + 1) * patch]
        grams.append(spread_heads(gram, square, heads))
        rows = slice(i * sub, (i + 1) * sub)
        z.append(intra[b, rows] + quick(qe[b, rows], grams[-1]))
    z = jnp.concatenate(z, axis=0)
    every = (local * steps, lanes)
    around = bb[...].reshape(every)
    met = summed(z * around, ones)
    zc = fine(pair(z), c[...])
    irms = lax.rsqrt(summed(z * zc, ones) * (1.0 / size) + EPS)
    zn = z * irms
    znb = zn.astype(BF16)
    zn_ref[...] = znb.reshape(zn_ref.shape)
    aligned = met * (irms * (1.0 / size))
    u = irms * (around - aligned * (irms * zc))
    ub = u.astype(BF16)
    ue = (u * lead[...].reshape(every)).astype(BF16)
    y = []
    for (b, i), gram in zip(places, grams):
        rows = slice(b * steps + i * sub, b * steps + (i + 1) * sub)
        scores = (quick(ub[rows], bd[b, i], ((1,), (1,))) * decay[b, i]).astype(BF16)
        left = jnp.concatenate([scores, ue[rows]], axis=1)
        y.append(quick(left, jnp.concatenate([bd[b, i], gram], axis=0)))
    y = jnp.concatenate(y, axis=0)
    given = cot[...].reshape(local * steps, width)
    x_total = quick(turned[...], y)
    right = jnp.concatenate([given, (aligned * zn).astype(BF16)], axis=1)
    zw_total = quick(znb, right, ((0,), (0,)))
    big_z = zw_total[:, :width]
    w_total = jnp.where(square, zw_total[:, width:], 0.0)
    y_total = -fine(pair(w_total), v[...])
    y_rows = []
    for h in range(heads):
        rows = slice(h * patch, (h + 1) * patch)
        both = jnp.concatenate(halves(big_z[rows]), axis=0)
        found = quick(both, w_out[h * size : (h + 1) * size], ((1,), (1,)))
        y_rows.append(y_total[rows] + found[:patch] + found[patch:])
    y_total = jnp.concatenate(y_rows, axis=0)
    per = lax.axis_size("ctx") // heads
    head = lax.axis_index("ctx") // per
    me = lax.axis_index("mix")
    panels = width // 128
    share = panels // mixes
    y_high = lanes // mixes
    x_high = patch // mixes

    def chosen(slot, of_part):
        part = other(me, mixes, slot)
        found = of_part(0)
        for i in range(1, mixes):
            found = jnp.where(part == i, of_part(i), found)
        return found

    for slot, out in enumerate(part_refs):
        for h in range(heads):
            at = other(head, heads, h) * (share * patch)
            z_rows = big_z[h * patch : (h + 1) * patch]
            for k in range(share):
                out[pl.ds(pl.multiple_of(at + k * patch, patch), patch), :] = chosen(
                    slot, lambda i: z_rows[:, (i * share + k) * 128 : (i * share + k + 1) * 128]
                )
        at = heads * share * patch
        out[at : at + y_high] = chosen(slot, lambda i: y_total[i * y_high : (i + 1) * y_high])
        at += y_high
        out[at : at + x_high] = chosen(slot, lambda i: x_total[i * x_high : (i + 1) * x_high])


def result_kernel(zn, big_b, _, out_ref):
    rows = zn[...].reshape(-1, zn.shape[-1])
    out_ref[...] = quick(rows, big_b[...]).astype(BF16).reshape(out_ref.shape)


def stacked_heads(array, heads):
    size = array.shape[1] // heads
    return jnp.concatenate([array[:, h * size : (h + 1) * size] for h in range(heads)], axis=0)


def final_kernel(heads, mixes, *refs):
    parts = refs[:mixes]
    a, keys, own, qkv_rows = refs[mixes : mixes + 4]
    gq_ref, go_ref, ge_ref, scr = refs[mixes + 4 :]
    patch = ge_ref.shape[1]
    width = go_ref.shape[1]
    size = width // heads
    lanes = heads * patch
    panels = width // 128
    share = panels // mixes
    y_high = lanes // mixes
    x_high = patch // mixes
    me = lax.axis_index("mix")
    for slot in range(mixes):
        part = other(me, mixes, slot)
        at = 0
        for k in range(share):
            scr[part * share + k, :patch] = parts[slot][at : at + patch]
            at += patch
        scr[panels, pl.ds(part * y_high, y_high), :] = parts[slot][at : at + y_high]
        at += y_high
        scr[panels + 1, pl.ds(part * x_high, x_high), :] = parts[slot][at : at + x_high]
    y = scr[panels]
    x_high, x_low = halves(scr[panels + 1, :patch])
    t_query = quick(jnp.concatenate([x_high, x_low, x_high], axis=1), keys[...])
    query_high, query_low = halves(a[:, :width])
    crossed = quick(
        jnp.concatenate([x_high, x_low, x_high], axis=0),
        jnp.concatenate([query_high, query_high, query_low], axis=0),
        ((0,), (0,)),
    )
    t_key = [crossed[h * patch : (h + 1) * patch, h * size : (h + 1) * size] for h in range(heads)]
    t_value = [y[h * patch : (h + 1) * patch] for h in range(heads)]
    t = jnp.concatenate([t_query] + t_key + t_value, axis=1)
    high, low = halves(t)
    both = jnp.concatenate([high, low], axis=0)
    embed_rows = own[:, :patch].astype(BF16)
    gq_ref[...] = quick(jnp.concatenate([embed_rows, embed_rows], axis=1), both)
    found = quick(qkv_rows[...], both, ((1,), (1,)))
    ge_ref[...] = found[:, :patch] + found[:, patch:]
    v_high, v_low = halves(own[:, patch : 2 * patch])
    z_high, z_low = halves(jnp.concatenate([scr[k, :patch] for k in range(panels)], axis=1))
    go_ref[...] = quick(
        jnp.concatenate([v_high, v_low, v_high], axis=1),
        jnp.concatenate([z_high, z_high, z_low], axis=0),
    )


def slot_kernel(heads, z_high, *refs):
    parts, slots = refs[:-heads], refs[-heads:]
    total = parts[0][...]
    for part in parts[1:]:
        total = total + part[...]
    for q in range(heads):
        slots[q][:z_high] = total[q * z_high : (q + 1) * z_high]
        slots[q][z_high:] = total[heads * z_high :]


def add_kernel(*refs):
    total = refs[0][...]
    for ref in refs[1:-1]:
        total = total + ref[...]
    refs[-1][...] = total


def added(arrays):
    (total,) = call(add_kernel, [(arrays[0].shape, F32)], arrays)
    return total


def shards(
    sources, source_ids, mix_weights, source_lengths, w_embed, w_qkv, w_out, forget, cotangent
):
    mixes = lax.axis_size("mix")
    count = lax.axis_size("ctx")
    patch = w_embed.shape[1]
    local, heads, steps = forget.shape
    width = w_out.shape[0]
    size = width // heads
    lanes = heads * patch
    held = sources.shape[0]
    rows_out = width // count
    per = count // heads
    dma = pltpu.SemaphoreType.DMA
    subs = heads
    sub = steps // subs
    part_shape = (local, steps * patch // lanes, lanes)
    panels = sources.reshape((held,) + part_shape[1:]).transpose(1, 0, 2).reshape(-1, lanes)
    got = [swap(panels, "mix", 1, mixes, s) for s in range(1, mixes)]
    part, factor, gx, fade, sums = call(
        functools.partial(local_kernel, held, patch, mixes),
        [
            (part_shape, F32),
            ((max(mixes - 1, 1), local, held) + part_shape[1:], F32),
            ((local, steps, lanes), F32),
            ((local, steps, lanes), F32),
            ((local * heads, steps), F32),
        ],
        [panels, forget, source_ids, mix_weights, source_lengths],
        hbm=(0, 1, 2, 3, 4),
        flops=10**9,
        scratch=[
            pltpu.VMEM(panels.shape, F32),
            pltpu.VMEM(forget.shape, F32),
            pltpu.SMEM(source_ids.shape, jnp.int32),
            pltpu.SMEM(mix_weights.shape, F32),
            pltpu.SMEM(source_lengths.shape, jnp.int32),
            dma((5,)),
        ],
    )
    high = -(-local // 8) * 8
    pack_shape = ((local * patch + high, lanes), F32)
    mt, pack = call(
        functools.partial(gram_kernel, held, patch, len(got)),
        [((local, steps, lanes), BF16), pack_shape],
        got + [part, factor, gx, fade],
    )
    a, m, c, keys, v, value_blocks, own, qkv_rows = call(
        functools.partial(weight_kernel, heads),
        [
            ((patch, 3 * width), F32),
            ((2 * lanes, 2 * lanes), BF16),
            ((2 * lanes, 2 * lanes), BF16),
            ((3 * lanes, width), BF16),
            ((2 * lanes, 2 * size), BF16),
            ((lanes, 2 * width), BF16),
            ((rows_out, 2 * patch), F32),
            ((rows_out, 3 * width), BF16),
        ],
        [w_embed.T, w_qkv, pack],
        hbm=(0, 1),
        flops=10**9,
        scratch=[
            pltpu.VMEM((patch, width), BF16),
            pltpu.VMEM(w_qkv.shape, BF16),
            pltpu.VMEM((width, 2 * patch), F32),
            dma((2,)),
        ],
    )
    steps_up = radices(count)
    stride = 1
    near = []
    for i, radix in enumerate(steps_up):
        order = level_order(i, radix)
        packs = [pack] + [swap(pack, "ctx", stride, radix, s) for s in order]
        if i == len(steps_up) - 1:
            break
        pack, before = call(
            functools.partial(level_kernel, local, patch, stride, radix, i),
            [pack_shape] * 2,
            packs + near,
        )
        near = [before]
        stride *= radix
    intra, qe, lead, bd, decay, gl, er, turned = call(
        functools.partial(intra_kernel, heads),
        [
            ((local, steps, lanes), F32),
            ((local, steps, lanes), BF16),
            ((local, steps, lanes), F32),
            ((local, subs, heads * sub, lanes), BF16),
            ((local, subs, sub, heads * sub), F32),
            ((local, subs, patch, lanes), F32),
            ((local, subs, 8, lanes), F32),
            ((patch, local * steps), BF16),
        ],
        [mt, gx, sums, m, pack],
        flops=10**9,
    )
    big_b, bb, w_out_near, cot_near = call(
        out_kernel,
        [
            ((lanes, width), BF16),
            ((local, steps, lanes), F32),
            (w_out.shape, BF16),
            (cotangent.shape, BF16),
        ],
        [w_out, cotangent, value_blocks, pack],
        hbm=(0, 1),
        flops=10**9,
        scratch=[dma((2,))],
    )
    part_rows = heads * (width // 128 // mixes) * patch + lanes // mixes + patch // mixes
    zn, *parts = call(
        functools.partial(main_kernel, heads, stride, radix, i, mixes),
        [((local, steps, lanes), BF16)] + [((part_rows, 128), F32)] * mixes,
        packs + near + [turned, lead, bd, decay, intra, qe, gl, er, bb, c, v, w_out_near, cot_near],
        flops=10**9,
    )
    z_high = (width // 128 // mixes) * patch
    y_high = part_rows - heads * z_high
    slots = call(
        functools.partial(slot_kernel, heads, z_high),
        [((z_high + y_high, 128), F32)] * heads,
        [parts[0]] + [swap(parts[s], "mix", 1, mixes, s) for s in range(1, mixes)],
    )
    (output,) = call(
        result_kernel, [((local, steps, width), BF16)], [zn, big_b, slots[0]], flops=10**9
    )
    order = ordered(heads, HEAD_ORDER)
    both = added([slots[0]] + [swap(slots[s], "ctx", per, heads, s) for s in order])
    stride = 1
    for radix in radices(per):
        order = ordered(radix, GROUP_ORDER)
        both = added([both] + [swap(both, "ctx", stride, radix, s) for s in order])
        stride *= radix
    pieces = [both] + [swap(both, "mix", 1, mixes, s) for s in range(1, mixes)]
    grads = call(
        functools.partial(final_kernel, heads, mixes),
        [((rows_out, 3 * width), F32), ((rows_out, width), F32), ((rows_out, patch), F32)],
        pieces + [a, keys, own, qkv_rows],
        scratch=[pltpu.VMEM((width // 128 + 2, lanes, 128), F32)],
    )
    return output, grads[0], grads[1], grads[2]


def solution(mesh):
    placed = (
        P("mix", "ctx"),
        P(),
        P(),
        P(),
        P(),
        P(),
        P(),
        P("mix", None, "ctx"),
        P("mix", "ctx", None),
    )
    return jax.shard_map(
        shards,
        mesh=mesh,
        in_specs=placed,
        out_specs=(P("mix", "ctx", None), P("ctx", None), P("ctx", None), P("ctx", None)),
        check_vma=False,
    )
```

```python
import functools

import jax
import jax.numpy as jnp
from jax import lax
from jax.experimental import pallas as pl
from jax.experimental.pallas import tpu as pltpu
from jax.sharding import PartitionSpec as P

EPS = 1e-06
F32 = jnp.float32
BF16 = jnp.bfloat16
LEVEL_ORDERS = ((3, 2, 1), (3, 2, 1))
HEAD_ORDER = (2, 3, 1)
GROUP_ORDER = (3, 2, 1)
VMEM_LIMIT = 24 * 2**20


def quick(left, right, dims=((1,), (0,))):
    return lax.dot_general(
        left.astype(BF16), right.astype(BF16), (dims, ((), ())), preferred_element_type=F32
    )


def halves(array):
    high = array.astype(BF16)
    return high, (array - high.astype(F32)).astype(BF16)


def rows_cols(shape):
    return lax.broadcasted_iota(jnp.int32, shape, 0), lax.broadcasted_iota(jnp.int32, shape, 1)


def block_mask(heads, high, wide):
    row, col = rows_cols((heads * high, heads * wide))
    return (row // high) == (col // wide)


def stacked(array, heads):
    return jnp.concatenate([array] * heads, axis=0)


def radices(count):
    found = []
    while count > 1:
        radix = 4 if count % 4 == 0 else 2 if count % 2 == 0 else count
        found.append(radix)
        count //= radix
    return found


def other(place, radix, slot):
    if radix & (radix - 1) == 0:
        return place ^ slot
    return (place + slot) % radix


def swap(array, axis, stride, radix, slot):
    pairs = []
    for source in range(lax.axis_size(axis)):
        place = (source // stride) % radix
        for target in range(radix):
            if other(target, radix, slot) == place:
                pairs.append((source, source + (target - place) * stride))
    return lax.ppermute(array, axis, pairs)


def call(kernel, outs, ins, hbm=(), out_hbm=(), flops=0, scratch=()):
    specs = [
        pl.BlockSpec(memory_space=pltpu.HBM if i in hbm else pltpu.VMEM) for i in range(len(ins))
    ]
    ins = [
        pltpu.with_memory_space_constraint(x, pltpu.HBM) if i in hbm else x
        for i, x in enumerate(ins)
    ]
    return pl.pallas_call(
        kernel,
        out_shape=[jax.ShapeDtypeStruct(s, d) for s, d in outs],
        in_specs=specs,
        out_specs=[
            pl.BlockSpec(memory_space=pl.ANY if i in out_hbm else pltpu.VMEM)
            for i in range(len(outs))
        ],
        scratch_shapes=list(scratch),
        compiler_params=pltpu.CompilerParams(vmem_limit_bytes=VMEM_LIMIT),
        cost_estimate=pl.CostEstimate(flops=flops, bytes_accessed=1 << 20, transcendentals=0),
    )(*ins)


def rebuilt(high, low):
    top = jnp.concatenate([high, low], axis=1)
    bottom = jnp.concatenate([high, jnp.zeros_like(low)], axis=1)
    return jnp.concatenate([top, bottom], axis=0)


def pair(array):
    return jnp.concatenate(halves(array), axis=1)


def fine(left, right):
    both = quick(left, right)
    half = both.shape[1] // 2
    return both[:, :half] + both[:, half:]


def summed(array, ones):
    return quick(pair(array), ones)


def fetch(sources, targets, sems):
    copies = [
        pltpu.make_async_copy(source, target, sems.at[i])
        for i, (source, target) in enumerate(zip(sources, targets))
    ]
    for copy in copies:
        copy.start()
    return copies


def local_kernel(held, patch, mixes, *refs):
    inputs, outs, scratch = refs[:5], refs[5:10], refs[10:]
    part_ref, factor_ref, gx_ref, fade_ref, row_ref = outs
    src, forget, ids, weights, lengths, sems = scratch
    own_rows = src.at[pl.ds(0, inputs[0].shape[0])]
    copies = fetch(inputs, (own_rows, forget, ids, weights, lengths), sems)
    me = lax.axis_index("mix")
    local, high, lanes = part_ref.shape
    _, heads, steps = forget.shape
    s, t = rows_cols((steps, steps))
    upto = (s <= t).astype(BF16)
    first = lax.axis_index("ctx") * (high * lanes // patch)
    row, col = rows_cols((high, lanes))
    position = first + row * (lanes // patch) + col // patch
    for copy in copies:
        copy.wait()
    for b in range(local):
        mixture = me * local + b
        total = jnp.zeros((high, lanes), F32)
        terms = []
        for term in range(ids.shape[1]):
            shown = jnp.where(position < lengths[mixture, term], weights[mixture, term], 0.0)
            at = ids[mixture, term] - me * held
            here = jnp.logical_and(at >= 0, at < held)
            rows = src[pl.ds(jnp.where(here, at, 0), high, held), :]
            total += jnp.where(here, shown, 0.0) * rows
            terms.append((ids[mixture, term], shown))
        part_ref[b] = total
        for slot in range(1, mixes):
            for source in range(held):
                wanted = other(me, mixes, slot) * held + source
                factor = jnp.zeros((high, lanes), F32)
                for identity, shown in terms:
                    factor += jnp.where(identity == wanted, shown, 0.0)
                factor_ref[slot - 1, b, source] = factor
    for b in range(local):
        log_gate = jnp.log1p(forget[b] - 1.0)
        high_half, low = halves(log_gate)
        lowest = (log_gate - high_half.astype(F32) - low.astype(F32)).astype(BF16)
        sums = quick(jnp.concatenate([high_half, low, lowest, jnp.zeros_like(low)], axis=0), upto)
        sums = sums[:heads] + sums[heads : 2 * heads] + sums[2 * heads : 3 * heads]
        row_ref[b * heads : (b + 1) * heads] = sums
        wide = jnp.broadcast_to(sums[:, None, :], (heads, patch, steps)).reshape(-1, steps)
        gx = wide.T
        gx_ref[b] = gx
        fade_ref[b] = jnp.exp(gx[steps - 1 : steps] - gx)


def gram_kernel(held, patch, others, *refs):
    sources, (part, factor, gx, fade, mt_ref, pack_ref) = refs[:others], refs[others:]
    local, steps, lanes = gx.shape
    per = lanes // patch
    t, r = rows_cols((local * steps, local * steps // per))
    spread = (t // per == r).astype(BF16)
    t, lane = rows_cols((local * steps, lanes))
    chosen = t % per == lane // patch
    a, b_ = rows_cols((lanes, lanes))
    fold = (a % patch == b_ % patch).astype(BF16)
    totals = []
    for b in range(local):
        total = part[b]
        for slot, source in enumerate(sources):
            for s in range(held):
                total += factor[slot, b, s] * source[pl.ds(s, steps // per, held), :]
        totals.append(total)
    wide = quick(spread, jnp.concatenate(totals, axis=0))
    mt = quick(jnp.where(chosen, wide, 0.0), fold)
    mt_ref[...] = mt.astype(BF16).reshape(mt_ref.shape)
    pack_ref[local * patch :] = jnp.zeros((pack_ref.shape[0] - local * patch, lanes), F32)
    for b in range(local):
        own = mt[b * steps : (b + 1) * steps]
        pack_ref[b * patch : (b + 1) * patch] = quick(own[:, :patch], own * fade[b], ((0,), (0,)))
        pack_ref[local * patch + b : local * patch + b + 1] = gx[b, steps - 1 : steps]


def weight_kernel(heads, *refs):
    a_ref, m_ref, c_ref, k_ref, v_ref, vb_ref, own_ref, qkv_ref, out_ref, cot_ref = refs[5:15]
    embed, qkv, tall, sems = refs[15:]
    copies = fetch(refs[:4], (embed, qkv, out_ref, cot_ref), sems)
    patch, width = embed.shape
    rows_out = qkv_ref.shape[0]
    ctx = lax.axis_index("ctx")
    mine = pl.ds(pl.multiple_of(ctx * rows_out, rows_out), rows_out)
    copies[0].wait()
    tall[:, :patch] = embed[...].astype(F32).T
    copies[1].wait()
    a = quick(embed[...], qkv[...])
    a_ref[...] = a
    qkv_ref[...] = qkv[mine, :]
    mask = block_mask(heads, patch, width // heads)
    query, key, value = [
        jnp.where(mask, stacked(a[:, j * width : (j + 1) * width], heads), 0.0) for j in range(3)
    ]
    across = ((1,), (1,))
    key_high, key_low = halves(key)
    value_high, value_low = halves(value)
    query_high, query_low = halves(query)
    k_ref[...] = jnp.concatenate([key_high, key_high, key_low], axis=0)
    m = quick(query_high, key_high, across) + quick(query_high, key_low, across)
    m = m + quick(query_low, key_high, across)
    m_ref[...] = rebuilt(*halves(m))
    mixed = quick(value_high, value_low, across)
    c = quick(value_high, value_high, across) + mixed + mixed.T
    c_ref[...] = rebuilt(*halves(c))
    v_ref[...] = rebuilt(*halves(stacked_heads(a[:, 2 * width :], heads)))
    vb_ref[...] = jnp.concatenate([value_high, value_low], axis=1)
    tall[:, patch : 2 * patch] = a[:, 2 * width :].T
    own_ref[...] = tall[mine, :]
    for copy in copies[2:]:
        copy.wait()


def out_kernel(w_out, cot, vb, _, b_ref, bb_ref):
    product = quick(vb[...], jnp.concatenate([w_out[...], w_out[...]], axis=0)).astype(BF16)
    b_ref[...] = product
    given = cot[...].reshape(bb_ref.shape[0] * bb_ref.shape[1], -1)
    bb_ref[...] = quick(given, product, ((1,), (1,))).reshape(bb_ref.shape)


def spread_heads(gram, square, heads):
    return jnp.where(square, stacked(gram, heads), 0.0).astype(BF16)


def intra_kernel(heads, mt, gx, sums, m, embed, qkv, _, z_ref, qe_ref, lead_ref, bd_ref, decay_ref, gl_ref, er_ref, turned_ref):
    local, steps, lanes = mt.shape
    patch = lanes // heads
    subs = bd_ref.shape[1]
    sub = steps // subs
    width = embed.shape[1]
    size = width // heads
    t, s = rows_cols((sub, heads * sub))
    causal = t >= s % sub
    row, col = rows_cols((heads * sub, lanes))
    diagonal = (row // sub == col // patch).astype(BF16)
    for b in range(local):
        query = fine(jnp.concatenate([mt[b], jnp.zeros_like(mt[b])], axis=1), m[...])
        turned_ref[:, b * steps : (b + 1) * steps] = mt[b].astype(F32).T[:patch].astype(BF16)
        embedded = quick(mt[b, :, :patch], embed[...]).astype(BF16)
        projected = quick(embedded, qkv[:, : 2 * width]).astype(BF16)
        gates = sums[b * heads : (b + 1) * heads]
        wide = jnp.broadcast_to(gates[:, None, :], (heads, sub, steps))
        wide = wide.reshape(heads * sub, steps).T
        for c in range(subs):
            rows = slice(c * sub, (c + 1) * sub)
            g = gx[b, rows]
            if c == 0:
                start = jnp.zeros((1, lanes), F32)
                gl_ref[b, c] = jnp.zeros((patch, lanes), F32)
            else:
                start = gx[b, c * sub - 1 : c * sub]
                past = mt[b, : c * sub]
                fading = past.astype(F32) * jnp.exp(start - gx[b, : c * sub])
                gl_ref[b, c] = quick(past[:, :patch], fading, ((0,), (0,)))
            er_ref[b, c] = jnp.broadcast_to(jnp.exp(start), (8, lanes))
            lead = jnp.exp(g - start)
            lead_ref[b, rows] = lead
            qe_ref[b, rows] = (query[rows] * lead).astype(BF16)
            bd = stacked(mt[b, rows], heads) * diagonal
            bd_ref[b, c] = bd
            across = jnp.concatenate([gates[h : h + 1, rows] for h in range(heads)], axis=1)
            decay = jnp.where(causal, jnp.exp(wide[rows] - across), 0.0)
            decay_ref[b, c] = decay
            scores = [
                quick(
                    projected[rows, h * size : (h + 1) * size],
                    projected[rows, width + h * size : width + (h + 1) * size],
                    ((1,), (1,)),
                )
                for h in range(heads)
            ]
            scores = jnp.concatenate(scores, axis=1) * decay
            z_ref[b, rows] = quick(scores, bd)


def level(packs, place, local, patch, wanted):
    radix = len(packs)
    at = [other(place, radix, slot) for slot in range(radix)]
    totals = [pack[local * patch :] for pack in packs]
    zero = jnp.zeros_like(totals[0])
    grams = None
    total = zero
    for m in range(radix):
        if wanted == "before" and m == 0:
            continue
        power = zero
        for k in range(radix):
            if k == m or (wanted == "before" and k == 0):
                continue
            after = at[k] > at[m]
            if wanted == "before":
                after = jnp.logical_and(after, at[k] < place)
            power = power + jnp.where(after, totals[k], 0.0)
        factor = jnp.exp(power)
        if wanted == "before":
            factor = jnp.where(at[m] < place, factor, 0.0)
            total = total + jnp.where(at[m] < place, totals[m], 0.0)
        else:
            total = total + totals[m]
        terms = [factor[b : b + 1] * packs[m][b * patch : (b + 1) * patch] for b in range(local)]
        grams = terms if grams is None else [g + x for g, x in zip(grams, terms)]
    return jnp.concatenate(grams + [total], axis=0)


def joined(near, far, local, patch):
    totals = near[local * patch :]
    factor = jnp.exp(totals)
    grams = [
        near[b * patch : (b + 1) * patch] + factor[b : b + 1] * far[b * patch : (b + 1) * patch]
        for b in range(local)
    ]
    return jnp.concatenate(grams + [totals + far[local * patch :]], axis=0)


def ordered(radix, order):
    return order if radix == 4 else tuple(range(1, radix))


def level_order(number, radix):
    return ordered(radix, LEVEL_ORDERS[min(number, len(LEVEL_ORDERS) - 1)])


def in_slots(packs, number):
    order = (0,) + level_order(number, len(packs))
    return [packs[order.index(slot)] for slot in range(len(packs))]


def level_kernel(local, patch, stride, radix, number, *refs):
    place = (lax.axis_index("ctx") // stride) % radix
    packs = in_slots([ref[...] for ref in refs[:radix]], number)
    before = level(packs, place, local, patch, "before")
    if number > 0:
        before = joined(refs[radix][...], before, local, patch)
    refs[-2][...] = level(packs, place, local, patch, "whole")
    refs[-1][...] = before


def main_kernel(heads, stride, radix, number, mixes, *refs):
    count = radix + int(number > 0)
    packs = in_slots([ref[...] for ref in refs[:radix]], number)
    turned, lead, bd, decay, intra, qe, gl, er, bb, c, v, w_out, cot = refs[count : count + 13]
    zn_ref, *part_refs = refs[count + 13 :]
    local, steps, lanes = lead.shape
    patch = lanes // heads
    subs = bd.shape[1]
    sub = steps // subs
    width = w_out.shape[0]
    size = width // heads
    place = (lax.axis_index("ctx") // stride) % radix
    state = level(packs, place, local, patch, "before")
    if number > 0:
        state = joined(refs[radix][...], state, local, patch)
    square = block_mask(heads, patch, patch)
    ones = jnp.concatenate([square.astype(BF16)] * 2, axis=0)
    places = [(b, i) for b in range(local) for i in range(subs)]
    grams = []
    z = []
    for b, i in places:
        gram = gl[b, i] + er[b, i, :1] * state[b * patch : (b + 1) * patch]
        grams.append(spread_heads(gram, square, heads))
        rows = slice(i * sub, (i + 1) * sub)
        z.append(intra[b, rows] + quick(qe[b, rows], grams[-1]))
    z = jnp.concatenate(z, axis=0)
    every = (local * steps, lanes)
    around = bb[...].reshape(every)
    met = summed(z * around, ones)
    zc = fine(pair(z), c[...])
    irms = lax.rsqrt(summed(z * zc, ones) * (1.0 / size) + EPS)
    zn = z * irms
    znb = zn.astype(BF16)
    zn_ref[...] = znb.reshape(zn_ref.shape)
    aligned = met * (irms * (1.0 / size))
    u = irms * (around - aligned * (irms * zc))
    ub = u.astype(BF16)
    ue = (u * lead[...].reshape(every)).astype(BF16)
    y = []
    for (b, i), gram in zip(places, grams):
        rows = slice(b * steps + i * sub, b * steps + (i + 1) * sub)
        scores = (quick(ub[rows], bd[b, i], ((1,), (1,))) * decay[b, i]).astype(BF16)
        left = jnp.concatenate([scores, ue[rows]], axis=1)
        y.append(quick(left, jnp.concatenate([bd[b, i], gram], axis=0)))
    y = jnp.concatenate(y, axis=0)
    given = cot[...].reshape(local * steps, width)
    x_total = quick(turned[...], y)
    right = jnp.concatenate([given, (aligned * zn).astype(BF16)], axis=1)
    zw_total = quick(znb, right, ((0,), (0,)))
    big_z = zw_total[:, :width]
    w_total = jnp.where(square, zw_total[:, width:], 0.0)
    y_total = -fine(pair(w_total), v[...])
    y_rows = []
    for h in range(heads):
        rows = slice(h * patch, (h + 1) * patch)
        both = jnp.concatenate(halves(big_z[rows]), axis=0)
        found = quick(both, w_out[h * size : (h + 1) * size], ((1,), (1,)))
        y_rows.append(y_total[rows] + found[:patch] + found[patch:])
    y_total = jnp.concatenate(y_rows, axis=0)
    per = lax.axis_size("ctx") // heads
    head = lax.axis_index("ctx") // per
    me = lax.axis_index("mix")
    panels = width // 128
    share = panels // mixes
    y_high = lanes // mixes
    x_high = patch // mixes

    def chosen(slot, of_part):
        part = other(me, mixes, slot)
        found = of_part(0)
        for i in range(1, mixes):
            found = jnp.where(part == i, of_part(i), found)
        return found

    for slot, out in enumerate(part_refs):
        for h in range(heads):
            at = other(head, heads, h) * (share * patch)
            z_rows = big_z[h * patch : (h + 1) * patch]
            for k in range(share):
                out[pl.ds(pl.multiple_of(at + k * patch, patch), patch), :] = chosen(
                    slot, lambda i: z_rows[:, (i * share + k) * 128 : (i * share + k + 1) * 128]
                )
        at = heads * share * patch
        out[at : at + y_high] = chosen(slot, lambda i: y_total[i * y_high : (i + 1) * y_high])
        at += y_high
        out[at : at + x_high] = chosen(slot, lambda i: x_total[i * x_high : (i + 1) * x_high])


def result_kernel(zn, big_b, _, out_ref):
    rows = zn[...].reshape(-1, zn.shape[-1])
    out_ref[...] = quick(rows, big_b[...]).astype(BF16).reshape(out_ref.shape)


def stacked_heads(array, heads):
    size = array.shape[1] // heads
    return jnp.concatenate([array[:, h * size : (h + 1) * size] for h in range(heads)], axis=0)


def final_kernel(heads, mixes, *refs):
    parts = refs[:mixes]
    a, keys, own, qkv_rows = refs[mixes : mixes + 4]
    gq_ref, go_ref, ge_ref, scr = refs[mixes + 4 :]
    patch = ge_ref.shape[1]
    width = go_ref.shape[1]
    size = width // heads
    lanes = heads * patch
    panels = width // 128
    share = panels // mixes
    y_high = lanes // mixes
    x_high = patch // mixes
    me = lax.axis_index("mix")
    for slot in range(mixes):
        part = other(me, mixes, slot)
        at = 0
        for k in range(share):
            scr[part * share + k, :patch] = parts[slot][at : at + patch]
            at += patch
        scr[panels, pl.ds(part * y_high, y_high), :] = parts[slot][at : at + y_high]
        at += y_high
        scr[panels + 1, pl.ds(part * x_high, x_high), :] = parts[slot][at : at + x_high]
    y = scr[panels]
    x_high, x_low = halves(scr[panels + 1, :patch])
    t_query = quick(jnp.concatenate([x_high, x_low, x_high], axis=1), keys[...])
    query_high, query_low = halves(a[:, :width])
    crossed = quick(
        jnp.concatenate([x_high, x_low, x_high], axis=0),
        jnp.concatenate([query_high, query_high, query_low], axis=0),
        ((0,), (0,)),
    )
    t_key = [crossed[h * patch : (h + 1) * patch, h * size : (h + 1) * size] for h in range(heads)]
    t_value = [y[h * patch : (h + 1) * patch] for h in range(heads)]
    t = jnp.concatenate([t_query] + t_key + t_value, axis=1)
    high, low = halves(t)
    both = jnp.concatenate([high, low], axis=0)
    embed_rows = own[:, :patch].astype(BF16)
    gq_ref[...] = quick(jnp.concatenate([embed_rows, embed_rows], axis=1), both)
    found = quick(qkv_rows[...], both, ((1,), (1,)))
    ge_ref[...] = found[:, :patch] + found[:, patch:]
    v_high, v_low = halves(own[:, patch : 2 * patch])
    z_high, z_low = halves(jnp.concatenate([scr[k, :patch] for k in range(panels)], axis=1))
    go_ref[...] = quick(
        jnp.concatenate([v_high, v_low, v_high], axis=1),
        jnp.concatenate([z_high, z_high, z_low], axis=0),
    )


def slot_kernel(heads, z_high, *refs):
    parts, slots = refs[:-heads], refs[-heads:]
    total = parts[0][...]
    for part in parts[1:]:
        total = total + part[...]
    for q in range(heads):
        slots[q][:z_high] = total[q * z_high : (q + 1) * z_high]
        slots[q][z_high:] = total[heads * z_high :]


def add_kernel(*refs):
    total = refs[0][...]
    for ref in refs[1:-1]:
        total = total + ref[...]
    refs[-1][...] = total


def added(arrays):
    (total,) = call(add_kernel, [(arrays[0].shape, F32)], arrays)
    return total


def shards(
    sources, source_ids, mix_weights, source_lengths, w_embed, w_qkv, w_out, forget, cotangent
):
    mixes = lax.axis_size("mix")
    count = lax.axis_size("ctx")
    patch = w_embed.shape[1]
    local, heads, steps = forget.shape
    width = w_out.shape[0]
    size = width // heads
    lanes = heads * patch
    held = sources.shape[0]
    rows_out = width // count
    per = count // heads
    dma = pltpu.SemaphoreType.DMA
    subs = heads
    sub = steps // subs
    part_shape = (local, steps * patch // lanes, lanes)
    panels = sources.reshape((held,) + part_shape[1:]).transpose(1, 0, 2).reshape(-1, lanes)
    got = [swap(panels, "mix", 1, mixes, s) for s in range(1, mixes)]
    part, factor, gx, fade, sums = call(
        functools.partial(local_kernel, held, patch, mixes),
        [
            (part_shape, F32),
            ((max(mixes - 1, 1), local, held) + part_shape[1:], F32),
            ((local, steps, lanes), F32),
            ((local, steps, lanes), F32),
            ((local * heads, steps), F32),
        ],
        [panels, forget, source_ids, mix_weights, source_lengths],
        hbm=(0, 1, 2, 3, 4),
        flops=10**9,
        scratch=[
            pltpu.VMEM((panels.shape[0] + 8, lanes), F32),
            pltpu.VMEM(forget.shape, F32),
            pltpu.SMEM(source_ids.shape, jnp.int32),
            pltpu.SMEM(mix_weights.shape, F32),
            pltpu.SMEM(source_lengths.shape, jnp.int32),
            dma((5,)),
        ],
    )
    high = -(-local // 8) * 8
    pack_shape = ((local * patch + high, lanes), F32)
    mt, pack = call(
        functools.partial(gram_kernel, held, patch, len(got)),
        [((local, steps, lanes), BF16), pack_shape],
        got + [part, factor, gx, fade],
    )
    a, m, c, keys, v, value_blocks, own, qkv_rows, w_out_near, cot_near, embed, qkv = call(
        functools.partial(weight_kernel, heads),
        [
            ((patch, 3 * width), F32),
            ((2 * lanes, 2 * lanes), BF16),
            ((2 * lanes, 2 * lanes), BF16),
            ((3 * lanes, width), BF16),
            ((2 * lanes, 2 * size), BF16),
            ((lanes, 2 * width), BF16),
            ((rows_out, 2 * patch), F32),
            ((rows_out, 3 * width), BF16),
            (w_out.shape, BF16),
            (cotangent.shape, BF16),
            ((patch, width), BF16),
            (w_qkv.shape, BF16),
        ],
        [w_embed.T, w_qkv, w_out, cotangent, pack],
        hbm=(0, 1, 2, 3),
        flops=10**9,
        scratch=[
            pltpu.VMEM((width, 2 * patch), F32),
            dma((4,)),
        ],
    )
    steps_up = radices(count)
    stride = 1
    near = []
    for i, radix in enumerate(steps_up):
        order = level_order(i, radix)
        packs = [pack] + [swap(pack, "ctx", stride, radix, s) for s in order]
        if i == len(steps_up) - 1:
            break
        pack, before = call(
            functools.partial(level_kernel, local, patch, stride, radix, i),
            [pack_shape] * 2,
            packs + near,
        )
        near = [before]
        stride *= radix
    intra, qe, lead, bd, decay, gl, er, turned = call(
        functools.partial(intra_kernel, heads),
        [
            ((local, steps, lanes), F32),
            ((local, steps, lanes), BF16),
            ((local, steps, lanes), F32),
            ((local, subs, heads * sub, lanes), BF16),
            ((local, subs, sub, heads * sub), F32),
            ((local, subs, patch, lanes), F32),
            ((local, subs, 8, lanes), F32),
            ((patch, local * steps), BF16),
        ],
        [mt, gx, sums, m, embed, qkv, pack],
        flops=10**9,
    )
    big_b, bb = call(
        out_kernel,
        [((lanes, width), BF16), ((local, steps, lanes), F32)],
        [w_out_near, cot_near, value_blocks, pack],
        flops=10**9,
    )
    part_rows = heads * (width // 128 // mixes) * patch + lanes // mixes + patch // mixes
    zn, *parts = call(
        functools.partial(main_kernel, heads, stride, radix, i, mixes),
        [((local, steps, lanes), BF16)] + [((part_rows, 128), F32)] * mixes,
        packs + near + [turned, lead, bd, decay, intra, qe, gl, er, bb, c, v, w_out_near, cot_near],
        flops=10**9,
    )
    z_high = (width // 128 // mixes) * patch
    y_high = part_rows - heads * z_high
    slots = call(
        functools.partial(slot_kernel, heads, z_high),
        [((z_high + y_high, 128), F32)] * heads,
        [parts[0]] + [swap(parts[s], "mix", 1, mixes, s) for s in range(1, mixes)],
    )
    (output,) = call(
        result_kernel, [((local, steps, width), BF16)], [zn, big_b, slots[0]], flops=10**9
    )
    order = ordered(heads, HEAD_ORDER)
    both = added([slots[0]] + [swap(slots[s], "ctx", per, heads, s) for s in order])
    stride = 1
    for radix in radices(per):
        order = ordered(radix, GROUP_ORDER)
        both = added([both] + [swap(both, "ctx", stride, radix, s) for s in order])
        stride *= radix
    pieces = [both] + [swap(both, "mix", 1, mixes, s) for s in range(1, mixes)]
    grads = call(
        functools.partial(final_kernel, heads, mixes),
        [((rows_out, 3 * width), F32), ((rows_out, width), F32), ((rows_out, patch), F32)],
        pieces + [a, keys, own, qkv_rows],
        scratch=[pltpu.VMEM((width // 128 + 2, lanes, 128), F32)],
    )
    return output, grads[0], grads[1], grads[2]


def solution(mesh):
    placed = (
        P("mix", "ctx"),
        P(),
        P(),
        P(),
        P(),
        P(),
        P(),
        P("mix", None, "ctx"),
        P("mix", "ctx", None),
    )
    return jax.shard_map(
        shards,
        mesh=mesh,
        in_specs=placed,
        out_specs=(P("mix", "ctx", None), P("ctx", None), P("ctx", None), P("ctx", None)),
        check_vma=False,
    )
```

```python
import functools

import jax
import jax.numpy as jnp
from jax import lax
from jax.experimental import pallas as pl
from jax.experimental.pallas import tpu as pltpu
from jax.sharding import PartitionSpec as P

EPS = 1e-06
F32 = jnp.float32
BF16 = jnp.bfloat16
LEVEL_ORDERS = ((1, 2, 3), (1, 2, 3))
HEAD_ORDER = (2, 3, 1)
GROUP_ORDER = (1, 2, 3)
VMEM_LIMIT = 24 * 2**20


def quick(left, right, dims=((1,), (0,))):
    return lax.dot_general(
        left.astype(BF16), right.astype(BF16), (dims, ((), ())), preferred_element_type=F32
    )


def halves(array):
    high = array.astype(BF16)
    return high, (array - high.astype(F32)).astype(BF16)


def rows_cols(shape):
    return lax.broadcasted_iota(jnp.int32, shape, 0), lax.broadcasted_iota(jnp.int32, shape, 1)


def block_mask(heads, high, wide):
    row, col = rows_cols((heads * high, heads * wide))
    return (row // high) == (col // wide)


def stacked(array, heads):
    return jnp.concatenate([array] * heads, axis=0)


def radices(count):
    found = []
    while count > 1:
        radix = 4 if count % 4 == 0 else 2 if count % 2 == 0 else count
        found.append(radix)
        count //= radix
    return found


def other(place, radix, slot):
    if radix & (radix - 1) == 0:
        return place ^ slot
    return (place + slot) % radix


def swap(array, axis, stride, radix, slot):
    pairs = []
    for source in range(lax.axis_size(axis)):
        place = (source // stride) % radix
        for target in range(radix):
            if other(target, radix, slot) == place:
                pairs.append((source, source + (target - place) * stride))
    return lax.ppermute(array, axis, pairs)


def call(kernel, outs, ins, hbm=(), out_hbm=(), flops=0, scratch=(), aliases=None):
    specs = [
        pl.BlockSpec(memory_space=pltpu.HBM if i in hbm else pltpu.VMEM) for i in range(len(ins))
    ]
    ins = [
        pltpu.with_memory_space_constraint(x, pltpu.HBM) if i in hbm else x
        for i, x in enumerate(ins)
    ]
    return pl.pallas_call(
        kernel,
        out_shape=[jax.ShapeDtypeStruct(s, d) for s, d in outs],
        in_specs=specs,
        out_specs=[
            pl.BlockSpec(memory_space=pl.ANY if i in out_hbm else pltpu.VMEM)
            for i in range(len(outs))
        ],
        scratch_shapes=list(scratch),
        input_output_aliases=aliases or {},
        compiler_params=pltpu.CompilerParams(vmem_limit_bytes=VMEM_LIMIT),
        cost_estimate=pl.CostEstimate(flops=flops, bytes_accessed=1 << 20, transcendentals=0),
    )(*ins)


def rebuilt(high, low):
    top = jnp.concatenate([high, low], axis=1)
    bottom = jnp.concatenate([high, jnp.zeros_like(low)], axis=1)
    return jnp.concatenate([top, bottom], axis=0)


def pair(array):
    return jnp.concatenate(halves(array), axis=1)


def fine(left, right):
    both = quick(left, right)
    half = both.shape[1] // 2
    return both[:, :half] + both[:, half:]


def summed(array, ones):
    return quick(pair(array), ones)


def fetch(sources, targets, sems):
    copies = [
        pltpu.make_async_copy(source, target, sems.at[i])
        for i, (source, target) in enumerate(zip(sources, targets))
    ]
    for copy in copies:
        copy.start()
    return copies


def local_kernel(held, patch, mixes, *refs):
    inputs, outs, scratch = refs[:5], refs[5:10], refs[10:]
    part_ref, factor_ref, gx_ref, fade_ref, row_ref = outs
    src, forget, ids, weights, lengths, sems = scratch
    own_rows = src.at[pl.ds(0, inputs[0].shape[0])]
    copies = fetch(inputs, (own_rows, forget, ids, weights, lengths), sems)
    me = lax.axis_index("mix")
    local, high, lanes = part_ref.shape
    _, heads, steps = forget.shape
    s, t = rows_cols((steps, steps))
    upto = (s <= t).astype(BF16)
    first = lax.axis_index("ctx") * (high * lanes // patch)
    row, col = rows_cols((high, lanes))
    position = first + row * (lanes // patch) + col // patch
    for copy in copies:
        copy.wait()
    for b in range(local):
        mixture = me * local + b
        total = jnp.zeros((high, lanes), F32)
        terms = []
        for term in range(ids.shape[1]):
            shown = jnp.where(position < lengths[mixture, term], weights[mixture, term], 0.0)
            at = ids[mixture, term] - me * held
            here = jnp.logical_and(at >= 0, at < held)
            rows = src[pl.ds(jnp.where(here, at, 0), high, held), :]
            total += jnp.where(here, shown, 0.0) * rows
            terms.append((ids[mixture, term], shown))
        part_ref[b] = total
        for slot in range(1, mixes):
            for source in range(held):
                wanted = other(me, mixes, slot) * held + source
                factor = jnp.zeros((high, lanes), F32)
                for identity, shown in terms:
                    factor += jnp.where(identity == wanted, shown, 0.0)
                factor_ref[slot - 1, b, source] = factor
    for b in range(local):
        log_gate = jnp.log1p(forget[b] - 1.0)
        high_half, low = halves(log_gate)
        lowest = (log_gate - high_half.astype(F32) - low.astype(F32)).astype(BF16)
        sums = quick(jnp.concatenate([high_half, low, lowest, jnp.zeros_like(low)], axis=0), upto)
        sums = sums[:heads] + sums[heads : 2 * heads] + sums[2 * heads : 3 * heads]
        row_ref[b * heads : (b + 1) * heads] = sums
        wide = jnp.broadcast_to(sums[:, None, :], (heads, patch, steps)).reshape(-1, steps)
        gx = wide.T
        gx_ref[b] = gx
        fade_ref[b] = jnp.exp(gx[steps - 1 : steps] - gx)


def gram_kernel(held, patch, others, *refs):
    sources, (part, factor, gx, fade, mt_ref, pack_ref) = refs[:others], refs[others:]
    local, steps, lanes = gx.shape
    per = lanes // patch
    t, r = rows_cols((local * steps, local * steps // per))
    spread = (t // per == r).astype(BF16)
    t, lane = rows_cols((local * steps, lanes))
    chosen = t % per == lane // patch
    a, b_ = rows_cols((lanes, lanes))
    fold = (a % patch == b_ % patch).astype(BF16)
    totals = []
    for b in range(local):
        total = part[b]
        for slot, source in enumerate(sources):
            for s in range(held):
                total += factor[slot, b, s] * source[pl.ds(s, steps // per, held), :]
        totals.append(total)
    wide = quick(spread, jnp.concatenate(totals, axis=0))
    mt = quick(jnp.where(chosen, wide, 0.0), fold)
    mt_ref[...] = mt.astype(BF16).reshape(mt_ref.shape)
    pack_ref[local * patch :] = jnp.zeros((pack_ref.shape[0] - local * patch, lanes), F32)
    for b in range(local):
        own = mt[b * steps : (b + 1) * steps]
        pack_ref[b * patch : (b + 1) * patch] = quick(own[:, :patch], own * fade[b], ((0,), (0,)))
        pack_ref[local * patch + b : local * patch + b + 1] = gx[b, steps - 1 : steps]


def weight_kernel(heads, *refs):
    a_ref, m_ref, c_ref, k_ref, v_ref, vb_ref, own_ref, qkv_ref, out_ref, cot_ref = refs[5:15]
    embed, qkv, tall, sems = refs[15:]
    copies = fetch(refs[:4], (embed, qkv, out_ref, cot_ref), sems)
    patch, width = embed.shape
    rows_out = qkv_ref.shape[0]
    ctx = lax.axis_index("ctx")
    mine = pl.ds(pl.multiple_of(ctx * rows_out, rows_out), rows_out)
    copies[0].wait()
    tall[:, :patch] = embed[...].astype(F32).T
    copies[1].wait()
    a = quick(embed[...], qkv[...])
    a_ref[...] = a
    qkv_ref[...] = qkv[mine, :]
    mask = block_mask(heads, patch, width // heads)
    query, key, value = [
        jnp.where(mask, stacked(a[:, j * width : (j + 1) * width], heads), 0.0) for j in range(3)
    ]
    across = ((1,), (1,))
    key_high, key_low = halves(key)
    value_high, value_low = halves(value)
    query_high, query_low = halves(query)
    k_ref[...] = jnp.concatenate([key_high, key_high, key_low], axis=0)
    m = quick(query_high, key_high, across) + quick(query_high, key_low, across)
    m = m + quick(query_low, key_high, across)
    m_ref[...] = rebuilt(*halves(m))
    mixed = quick(value_high, value_low, across)
    c = quick(value_high, value_high, across) + mixed + mixed.T
    c_ref[...] = rebuilt(*halves(c))
    v_ref[...] = rebuilt(*halves(stacked_heads(a[:, 2 * width :], heads)))
    vb_ref[...] = jnp.concatenate([value_high, value_low], axis=1)
    tall[:, patch : 2 * patch] = a[:, 2 * width :].T
    own_ref[...] = tall[mine, :]
    for copy in copies[2:]:
        copy.wait()


def out_kernel(w_out, cot, vb, _, b_ref, bb_ref):
    product = quick(vb[...], jnp.concatenate([w_out[...], w_out[...]], axis=0)).astype(BF16)
    b_ref[...] = product
    given = cot[...].reshape(bb_ref.shape[0] * bb_ref.shape[1], -1)
    bb_ref[...] = quick(given, product, ((1,), (1,))).reshape(bb_ref.shape)


def spread_heads(gram, square, heads):
    return jnp.where(square, stacked(gram, heads), 0.0).astype(BF16)


def intra_kernel(heads, mt, gx, sums, m, embed, qkv, _, z_ref, qe_ref, lead_ref, bd_ref, decay_ref, gl_ref, er_ref, turned_ref):
    local, steps, lanes = mt.shape
    patch = lanes // heads
    subs = bd_ref.shape[1]
    sub = steps // subs
    width = embed.shape[1]
    size = width // heads
    t, s = rows_cols((sub, heads * sub))
    causal = t >= s % sub
    row, col = rows_cols((heads * sub, lanes))
    diagonal = (row // sub == col // patch).astype(BF16)
    for b in range(local):
        query = fine(jnp.concatenate([mt[b], jnp.zeros_like(mt[b])], axis=1), m[...])
        turned_ref[:, b * steps : (b + 1) * steps] = mt[b].astype(F32).T[:patch].astype(BF16)
        embedded = quick(mt[b, :, :patch], embed[...]).astype(BF16)
        projected = quick(embedded, qkv[:, : 2 * width]).astype(BF16)
        gates = sums[b * heads : (b + 1) * heads]
        wide = jnp.broadcast_to(gates[:, None, :], (heads, sub, steps))
        wide = wide.reshape(heads * sub, steps).T
        for c in range(subs):
            rows = slice(c * sub, (c + 1) * sub)
            g = gx[b, rows]
            if c == 0:
                start = jnp.zeros((1, lanes), F32)
                gl_ref[b, c] = jnp.zeros((patch, lanes), F32)
            else:
                start = gx[b, c * sub - 1 : c * sub]
                past = mt[b, : c * sub]
                fading = past.astype(F32) * jnp.exp(start - gx[b, : c * sub])
                gl_ref[b, c] = quick(past[:, :patch], fading, ((0,), (0,)))
            er_ref[b, c] = jnp.broadcast_to(jnp.exp(start), (8, lanes))
            lead = jnp.exp(g - start)
            lead_ref[b, rows] = lead
            qe_ref[b, rows] = (query[rows] * lead).astype(BF16)
            bd = stacked(mt[b, rows], heads) * diagonal
            bd_ref[b, c] = bd
            across = jnp.concatenate([gates[h : h + 1, rows] for h in range(heads)], axis=1)
            decay = jnp.where(causal, jnp.exp(wide[rows] - across), 0.0)
            decay_ref[b, c] = decay
            scores = [
                quick(
                    projected[rows, h * size : (h + 1) * size],
                    projected[rows, width + h * size : width + (h + 1) * size],
                    ((1,), (1,)),
                )
                for h in range(heads)
            ]
            scores = jnp.concatenate(scores, axis=1) * decay
            z_ref[b, rows] = quick(scores, bd)


def level(packs, place, local, patch, wanted):
    radix = len(packs)
    at = [other(place, radix, slot) for slot in range(radix)]
    totals = [pack[local * patch :] for pack in packs]
    zero = jnp.zeros_like(totals[0])
    grams = None
    total = zero
    for m in range(radix):
        if wanted == "before" and m == 0:
            continue
        power = zero
        for k in range(radix):
            if k == m or (wanted == "before" and k == 0):
                continue
            after = at[k] > at[m]
            if wanted == "before":
                after = jnp.logical_and(after, at[k] < place)
            power = power + jnp.where(after, totals[k], 0.0)
        factor = jnp.exp(power)
        if wanted == "before":
            factor = jnp.where(at[m] < place, factor, 0.0)
            total = total + jnp.where(at[m] < place, totals[m], 0.0)
        else:
            total = total + totals[m]
        terms = [factor[b : b + 1] * packs[m][b * patch : (b + 1) * patch] for b in range(local)]
        grams = terms if grams is None else [g + x for g, x in zip(grams, terms)]
    return jnp.concatenate(grams + [total], axis=0)


def joined(near, far, local, patch):
    totals = near[local * patch :]
    factor = jnp.exp(totals)
    grams = [
        near[b * patch : (b + 1) * patch] + factor[b : b + 1] * far[b * patch : (b + 1) * patch]
        for b in range(local)
    ]
    return jnp.concatenate(grams + [totals + far[local * patch :]], axis=0)


def ordered(radix, order):
    return order if radix == 4 else tuple(range(1, radix))


def level_order(number, radix):
    return ordered(radix, LEVEL_ORDERS[min(number, len(LEVEL_ORDERS) - 1)])


def in_slots(packs, number):
    order = (0,) + level_order(number, len(packs))
    return [packs[order.index(slot)] for slot in range(len(packs))]


def level_kernel(local, patch, stride, radix, number, *refs):
    place = (lax.axis_index("ctx") // stride) % radix
    packs = in_slots([ref[...] for ref in refs[:radix]], number)
    before = level(packs, place, local, patch, "before")
    if number > 0:
        before = joined(refs[radix][...], before, local, patch)
    refs[-2][...] = level(packs, place, local, patch, "whole")
    refs[-1][...] = before


def main_kernel(heads, stride, radix, number, mixes, given, places, handed, *refs):
    near_given = int(number > 0)
    count = 1 + len(given) + near_given
    own = refs[0][...]
    packs = [own] * radix
    for i, slot in enumerate(given):
        packs[slot] = refs[1 + i][...]
    near = refs[1 + len(given)] if near_given else None
    place = (lax.axis_index("ctx") // stride) % radix
    here = place == places[0]
    for p in places[1:]:
        here = jnp.logical_or(here, place == p)
    inputs, outs = refs[count : count + 13], refs[count + 13 + handed :]

    @pl.when(here)
    def _():
        main_work(heads, number, mixes, packs, near, place, inputs, outs)


def main_work(heads, number, mixes, packs, near, place, inputs, outs):
    turned, lead, bd, decay, intra, qe, gl, er, bb, c, v, w_out, cot = inputs
    zn_ref, *part_refs = outs
    local, steps, lanes = lead.shape
    patch = lanes // heads
    subs = bd.shape[1]
    sub = steps // subs
    width = w_out.shape[0]
    size = width // heads
    state = level(packs, place, local, patch, "before")
    if number > 0:
        state = joined(near[...], state, local, patch)
    square = block_mask(heads, patch, patch)
    ones = jnp.concatenate([square.astype(BF16)] * 2, axis=0)
    places = [(b, i) for b in range(local) for i in range(subs)]
    grams = []
    z = []
    for b, i in places:
        gram = gl[b, i] + er[b, i, :1] * state[b * patch : (b + 1) * patch]
        grams.append(spread_heads(gram, square, heads))
        rows = slice(i * sub, (i + 1) * sub)
        z.append(intra[b, rows] + quick(qe[b, rows], grams[-1]))
    z = jnp.concatenate(z, axis=0)
    every = (local * steps, lanes)
    around = bb[...].reshape(every)
    met = summed(z * around, ones)
    zc = fine(pair(z), c[...])
    irms = lax.rsqrt(summed(z * zc, ones) * (1.0 / size) + EPS)
    zn = z * irms
    znb = zn.astype(BF16)
    zn_ref[...] = znb.reshape(zn_ref.shape)
    aligned = met * (irms * (1.0 / size))
    u = irms * (around - aligned * (irms * zc))
    ub = u.astype(BF16)
    ue = (u * lead[...].reshape(every)).astype(BF16)
    y = []
    for (b, i), gram in zip(places, grams):
        rows = slice(b * steps + i * sub, b * steps + (i + 1) * sub)
        scores = (quick(ub[rows], bd[b, i], ((1,), (1,))) * decay[b, i]).astype(BF16)
        left = jnp.concatenate([scores, ue[rows]], axis=1)
        y.append(quick(left, jnp.concatenate([bd[b, i], gram], axis=0)))
    y = jnp.concatenate(y, axis=0)
    given = cot[...].reshape(local * steps, width)
    x_total = quick(turned[...], y)
    right = jnp.concatenate([given, (aligned * zn).astype(BF16)], axis=1)
    zw_total = quick(znb, right, ((0,), (0,)))
    big_z = zw_total[:, :width]
    w_total = jnp.where(square, zw_total[:, width:], 0.0)
    y_total = -fine(pair(w_total), v[...])
    y_rows = []
    for h in range(heads):
        rows = slice(h * patch, (h + 1) * patch)
        both = jnp.concatenate(halves(big_z[rows]), axis=0)
        found = quick(both, w_out[h * size : (h + 1) * size], ((1,), (1,)))
        y_rows.append(y_total[rows] + found[:patch] + found[patch:])
    y_total = jnp.concatenate(y_rows, axis=0)
    per = lax.axis_size("ctx") // heads
    head = lax.axis_index("ctx") // per
    me = lax.axis_index("mix")
    panels = width // 128
    share = panels // mixes
    y_high = lanes // mixes
    x_high = patch // mixes

    def chosen(slot, of_part):
        part = other(me, mixes, slot)
        found = of_part(0)
        for i in range(1, mixes):
            found = jnp.where(part == i, of_part(i), found)
        return found

    for slot, out in enumerate(part_refs):
        for h in range(heads):
            at = other(head, heads, h) * (share * patch)
            z_rows = big_z[h * patch : (h + 1) * patch]
            for k in range(share):
                out[pl.ds(pl.multiple_of(at + k * patch, patch), patch), :] = chosen(
                    slot, lambda i: z_rows[:, (i * share + k) * 128 : (i * share + k + 1) * 128]
                )
        at = heads * share * patch
        out[at : at + y_high] = chosen(slot, lambda i: y_total[i * y_high : (i + 1) * y_high])
        at += y_high
        out[at : at + x_high] = chosen(slot, lambda i: x_total[i * x_high : (i + 1) * x_high])


def result_kernel(zn, big_b, _, out_ref):
    rows = zn[...].reshape(-1, zn.shape[-1])
    out_ref[...] = quick(rows, big_b[...]).astype(BF16).reshape(out_ref.shape)


def stacked_heads(array, heads):
    size = array.shape[1] // heads
    return jnp.concatenate([array[:, h * size : (h + 1) * size] for h in range(heads)], axis=0)


def final_kernel(heads, mixes, *refs):
    parts = refs[:mixes]
    a, keys, own, qkv_rows = refs[mixes : mixes + 4]
    gq_ref, go_ref, ge_ref, scr = refs[mixes + 4 :]
    patch = ge_ref.shape[1]
    width = go_ref.shape[1]
    size = width // heads
    lanes = heads * patch
    panels = width // 128
    share = panels // mixes
    y_high = lanes // mixes
    x_high = patch // mixes
    me = lax.axis_index("mix")
    for slot in range(mixes):
        part = other(me, mixes, slot)
        at = 0
        for k in range(share):
            scr[part * share + k, :patch] = parts[slot][at : at + patch]
            at += patch
        scr[panels, pl.ds(part * y_high, y_high), :] = parts[slot][at : at + y_high]
        at += y_high
        scr[panels + 1, pl.ds(part * x_high, x_high), :] = parts[slot][at : at + x_high]
    y = scr[panels]
    x_high, x_low = halves(scr[panels + 1, :patch])
    t_query = quick(jnp.concatenate([x_high, x_low, x_high], axis=1), keys[...])
    query_high, query_low = halves(a[:, :width])
    crossed = quick(
        jnp.concatenate([x_high, x_low, x_high], axis=0),
        jnp.concatenate([query_high, query_high, query_low], axis=0),
        ((0,), (0,)),
    )
    t_key = [crossed[h * patch : (h + 1) * patch, h * size : (h + 1) * size] for h in range(heads)]
    t_value = [y[h * patch : (h + 1) * patch] for h in range(heads)]
    t = jnp.concatenate([t_query] + t_key + t_value, axis=1)
    high, low = halves(t)
    both = jnp.concatenate([high, low], axis=0)
    embed_rows = own[:, :patch].astype(BF16)
    gq_ref[...] = quick(jnp.concatenate([embed_rows, embed_rows], axis=1), both)
    found = quick(qkv_rows[...], both, ((1,), (1,)))
    ge_ref[...] = found[:, :patch] + found[:, patch:]
    v_high, v_low = halves(own[:, patch : 2 * patch])
    z_high, z_low = halves(jnp.concatenate([scr[k, :patch] for k in range(panels)], axis=1))
    go_ref[...] = quick(
        jnp.concatenate([v_high, v_low, v_high], axis=1),
        jnp.concatenate([z_high, z_high, z_low], axis=0),
    )


def slot_kernel(heads, z_high, *refs):
    parts, slots = refs[:-heads], refs[-heads:]
    total = parts[0][...]
    for part in parts[1:]:
        total = total + part[...]
    for q in range(heads):
        slots[q][:z_high] = total[q * z_high : (q + 1) * z_high]
        slots[q][z_high:] = total[heads * z_high :]


def add_kernel(*refs):
    total = refs[0][...]
    for ref in refs[1:-1]:
        total = total + ref[...]
    refs[-1][...] = total


def added(arrays):
    (total,) = call(add_kernel, [(arrays[0].shape, F32)], arrays)
    return total


def shards(
    sources, source_ids, mix_weights, source_lengths, w_embed, w_qkv, w_out, forget, cotangent
):
    mixes = lax.axis_size("mix")
    count = lax.axis_size("ctx")
    patch = w_embed.shape[1]
    local, heads, steps = forget.shape
    width = w_out.shape[0]
    size = width // heads
    lanes = heads * patch
    held = sources.shape[0]
    rows_out = width // count
    per = count // heads
    dma = pltpu.SemaphoreType.DMA
    subs = heads
    sub = steps // subs
    part_shape = (local, steps * patch // lanes, lanes)
    panels = sources.reshape((held,) + part_shape[1:]).transpose(1, 0, 2).reshape(-1, lanes)
    got = [swap(panels, "mix", 1, mixes, s) for s in range(1, mixes)]
    part, factor, gx, fade, sums = call(
        functools.partial(local_kernel, held, patch, mixes),
        [
            (part_shape, F32),
            ((max(mixes - 1, 1), local, held) + part_shape[1:], F32),
            ((local, steps, lanes), F32),
            ((local, steps, lanes), F32),
            ((local * heads, steps), F32),
        ],
        [panels, forget, source_ids, mix_weights, source_lengths],
        hbm=(0, 1, 2, 3, 4),
        flops=10**9,
        scratch=[
            pltpu.VMEM((panels.shape[0] + 8, lanes), F32),
            pltpu.VMEM(forget.shape, F32),
            pltpu.SMEM(source_ids.shape, jnp.int32),
            pltpu.SMEM(mix_weights.shape, F32),
            pltpu.SMEM(source_lengths.shape, jnp.int32),
            dma((5,)),
        ],
    )
    high = -(-local // 8) * 8
    pack_shape = ((local * patch + high, lanes), F32)
    mt, pack = call(
        functools.partial(gram_kernel, held, patch, len(got)),
        [((local, steps, lanes), BF16), pack_shape],
        got + [part, factor, gx, fade],
    )
    a, m, c, keys, v, value_blocks, own, qkv_rows, w_out_near, cot_near, embed, qkv = call(
        functools.partial(weight_kernel, heads),
        [
            ((patch, 3 * width), F32),
            ((2 * lanes, 2 * lanes), BF16),
            ((2 * lanes, 2 * lanes), BF16),
            ((3 * lanes, width), BF16),
            ((2 * lanes, 2 * size), BF16),
            ((lanes, 2 * width), BF16),
            ((rows_out, 2 * patch), F32),
            ((rows_out, 3 * width), BF16),
            (w_out.shape, BF16),
            (cotangent.shape, BF16),
            ((patch, width), BF16),
            (w_qkv.shape, BF16),
        ],
        [w_embed.T, w_qkv, w_out, cotangent, pack],
        hbm=(0, 1, 2, 3),
        flops=10**9,
        scratch=[
            pltpu.VMEM((width, 2 * patch), F32),
            dma((4,)),
        ],
    )
    steps_up = radices(count)
    stride = 1
    near = []
    for i, radix in enumerate(steps_up):
        order = level_order(i, radix)
        packs = [pack] + [swap(pack, "ctx", stride, radix, s) for s in order]
        if i == len(steps_up) - 1:
            break
        pack, before = call(
            functools.partial(level_kernel, local, patch, stride, radix, i),
            [pack_shape] * 2,
            packs + near,
        )
        near = [before]
        stride *= radix
    intra, qe, lead, bd, decay, gl, er, turned = call(
        functools.partial(intra_kernel, heads),
        [
            ((local, steps, lanes), F32),
            ((local, steps, lanes), BF16),
            ((local, steps, lanes), F32),
            ((local, subs, heads * sub, lanes), BF16),
            ((local, subs, sub, heads * sub), F32),
            ((local, subs, patch, lanes), F32),
            ((local, subs, 8, lanes), F32),
            ((patch, local * steps), BF16),
        ],
        [mt, gx, sums, m, embed, qkv, pack],
        flops=10**9,
    )
    big_b, bb = call(
        out_kernel,
        [((lanes, width), BF16), ((local, steps, lanes), F32)],
        [w_out_near, cot_near, value_blocks, pack],
        flops=10**9,
    )
    part_rows = heads * (width // 128 // mixes) * patch + lanes // mixes + patch // mixes
    order = level_order(i, radix)
    ending = order[::-1]
    served = {}
    for place in range(radix):
        lower = [k for k, slot in enumerate(ending) if other(place, radix, slot) < place]
        served.setdefault(max(lower) + 1 if lower else 0, []).append(place)
    main_outs = [((local, steps, lanes), BF16)] + [((part_rows, 128), F32)] * mixes
    results = []
    for ends in sorted(served):
        given = [slot for slot in order if slot in ending[:ends]]
        ins = [packs[0]] + [packs[1 + order.index(slot)] for slot in given] + near
        ins = ins + [turned, lead, bd, decay, intra, qe, gl, er, bb, c, v, w_out_near, cot_near]
        results = call(
            functools.partial(
                main_kernel, heads, stride, radix, i, mixes, given, served[ends], len(results)
            ),
            main_outs,
            ins + list(results),
            flops=10**9,
            aliases={len(ins) + k: k for k in range(len(results))},
        )
    zn, *parts = results
    z_high = (width // 128 // mixes) * patch
    y_high = part_rows - heads * z_high
    slots = call(
        functools.partial(slot_kernel, heads, z_high),
        [((z_high + y_high, 128), F32)] * heads,
        [parts[0]] + [swap(parts[s], "mix", 1, mixes, s) for s in range(1, mixes)],
    )
    (output,) = call(
        result_kernel, [((local, steps, width), BF16)], [zn, big_b, slots[0]], flops=10**9
    )
    order = ordered(heads, HEAD_ORDER)
    both = added([slots[0]] + [swap(slots[s], "ctx", per, heads, s) for s in order])
    stride = 1
    for radix in radices(per):
        order = ordered(radix, GROUP_ORDER)
        both = added([both] + [swap(both, "ctx", stride, radix, s) for s in order])
        stride *= radix
    pieces = [both] + [swap(both, "mix", 1, mixes, s) for s in range(1, mixes)]
    grads = call(
        functools.partial(final_kernel, heads, mixes),
        [((rows_out, 3 * width), F32), ((rows_out, width), F32), ((rows_out, patch), F32)],
        pieces + [a, keys, own, qkv_rows],
        scratch=[pltpu.VMEM((width // 128 + 2, lanes, 128), F32)],
    )
    return output, grads[0], grads[1], grads[2]


def solution(mesh):
    placed = (
        P("mix", "ctx"),
        P(),
        P(),
        P(),
        P(),
        P(),
        P(),
        P("mix", None, "ctx"),
        P("mix", "ctx", None),
    )
    return jax.shard_map(
        shards,
        mesh=mesh,
        in_specs=placed,
        out_specs=(P("mix", "ctx", None), P("ctx", None), P("ctx", None), P("ctx", None)),
        check_vma=False,
    )
```
